32 devices in a mesh: mode: 8 (over y, x, core), elem: 4 (over z).
Axes of the slice: x: 2, y: 2, z: 4, core: 2. Of those that a mesh axis runs over, the one named last changes fastest.
Arguments:
- rhs_phys: float32 [128, 12288], P(None, ('elem', 'mode')), may hold values from -6 to 6
- radial_basis: float32 [12, 128, 128], P('elem'), may hold values from -0.5 to 0.5
- axial_basis: float32 [12, 7, 7], P('elem'), may hold values from -2 to 2
- radial_eig: float32 [12, 128], P('elem'), may hold values from 0.25 to 8
- axial_eig: float32 [12, 7], P('elem'), may hold values from 0.25 to 8
- face_stiff: float32 [12, 128, 128], P('elem'), may hold values from -0.5 to 0.5
- face_mass: float32 [12, 128, 128], P('elem'), may hold values from -0.5 to 0.5
- axial_coupling: float32 [12, 2, 7], P('elem'), may hold values from -3 to 3
- face_numbering: int32 [12, 2, 128], P('elem'), may hold values from 0 to 127, each once within a row
- band_panels: float32 [2, 12, 128, 128], P(None, 'elem'), may hold values from -1 to 1
- inverse_panels: float32 [64, 12, 128, 128], P('mode', 'elem'), may hold values from -2 to 2
Outputs:
- pressure: float32 [128, 12288], P('mode', 'elem')
The draws below stay inside these ranges and needn't reach their ends.
Inputs may be any that keep to these rules, and one draw needn't show every extreme that they name: Each row of face_numbering is a permutation of 0 to 127.
All inputs are finite; a program needn't handle non-finite values.
Results may differ from the reference program's by a relative error of at most 0.0003.
Values sent between devices are 32-bit elements; how exact they have to be, the bound alone decides.
No kernel may reach another device: no remote copies, remote signals or barrier semaphores. Data moves between devices by JAX's collectives and lax.ppermute only.
A program may use at most 64 MiB of HBM per device.

```python
import math
import jax
import jax.numpy as jnp
from jax import lax

RADIAL = 128
INNER = 7
FOURIER_COUNT = 64
PLANES = 128
SLAB_COUNT = 12
NODES = 12288


def panel_noise(key, shape, scales):
    noise = jax.random.truncated_normal(key, -4.0, 4.0, shape, jnp.float32)
    off_diag = 1.0 - jnp.eye(RADIAL, dtype=jnp.float32)
    return noise * off_diag * (0.22 / jnp.sqrt(jnp.float32(RADIAL))) * scales[..., :, None]


def band_parts(key):
    first = jax.random.uniform(jax.random.fold_in(key, 11), (SLAB_COUNT, RADIAL), jnp.float32, 0.5, 1.0)
    second = jax.random.uniform(jax.random.fold_in(key, 12), (SLAB_COUNT, RADIAL), jnp.float32, 0.1, 0.3)
    return (first, second)


def draw_band_panels(key, part):
    first, second = band_parts(key)
    identity_mat = jnp.eye(RADIAL, dtype=jnp.float32)
    lead = identity_mat * first[..., None] + panel_noise(jax.random.fold_in(key, 13), (SLAB_COUNT, RADIAL, RADIAL), first)
    extra = identity_mat * second[..., None] + panel_noise(jax.random.fold_in(key, 14), (SLAB_COUNT, RADIAL, RADIAL), second)
    return jnp.stack([lead, extra])


def draw_inverse_panels(key, part):
    first, second = band_parts(key)
    wavenumber = jnp.arange(FOURIER_COUNT, dtype=jnp.float32) / FOURIER_COUNT
    wavenumber_squared = 4.0 * wavenumber * wavenumber
    diag_band = first[None] + wavenumber_squared[:, None, None] * second[None]
    slow_share = 0.5
    picks = jax.random.uniform(jax.random.fold_in(key, 21), (FOURIER_COUNT, 1, RADIAL), jnp.float32)
    depth = jax.random.uniform(jax.random.fold_in(key, 22), (FOURIER_COUNT, SLAB_COUNT, RADIAL), jnp.float32, 0.5, 1.0)
    slow_rate = jnp.exp(jnp.log(0.2) / SLAB_COUNT * depth)
    fast_rate = jax.random.uniform(jax.random.fold_in(key, 23), (FOURIER_COUNT, SLAB_COUNT, RADIAL), jnp.float32, 0.3, 0.6)
    decay_rates = jnp.where(picks < slow_share, slow_rate, fast_rate)
    interface_batch = jax.random.uniform(jax.random.fold_in(key, 24), (FOURIER_COUNT, SLAB_COUNT, 1), jnp.float32) < 2.0 / SLAB_COUNT
    truncation_factor = jax.random.uniform(jax.random.fold_in(key, 25), (FOURIER_COUNT, SLAB_COUNT, 1), jnp.float32, 0.5, 0.8)
    decay_rates = jnp.where(interface_batch, decay_rates * truncation_factor, decay_rates)
    diag_inverse = decay_rates / diag_band
    identity_mat = jnp.eye(RADIAL, dtype=jnp.float32)
    return identity_mat * diag_inverse[..., None] + panel_noise(jax.random.fold_in(key, 26), (FOURIER_COUNT, SLAB_COUNT, RADIAL, RADIAL), diag_inverse)


def block_levels(own_key, dims, pieces, least, top_value):
    def one(axis_at, blocks):
        heights = jax.random.uniform(jax.random.fold_in(jax.random.fold_in(own_key, 6), axis_at), (blocks,), jnp.float32, least / len(pieces), top_value / len(pieces))
        return jnp.repeat(jnp.exp(heights), dims[axis_at] // blocks).reshape((-1,) + (1,) * (len(dims) - axis_at - 1))

    gain = one(*pieces[0])
    for cut in pieces[1:]:
        gain = gain * one(*cut)
    return gain


def bell_draw(own_key, shape, deviation, most, shards=(), kind=jnp.bfloat16):
    array = jax.random.normal(own_key, shape, jnp.float32) * deviation
    if len(shards) > 0:
        array = block_levels(own_key, shape, shards, -0.22, 0.18) * array
    return jnp.clip(array, min=-most, max=most).astype(kind)


def setup_inputs(seed: int = 0) -> dict:
    key_list = jax.random.split(jax.random.key(seed), 12)
    return {
        "rhs_phys": bell_draw(key_list[0], (PLANES, NODES), 1.0, 6.0, ((1, 32),), jnp.float32),
        "radial_basis": bell_draw(key_list[1], (SLAB_COUNT, RADIAL, RADIAL), RADIAL ** -0.5, 0.5, ((0, 4),), jnp.float32),
        "axial_basis": bell_draw(key_list[2], (SLAB_COUNT, INNER, INNER), INNER ** -0.5, 2.0, ((0, 4),), jnp.float32),
        "radial_eig": jnp.clip(jnp.exp(math.log(8.0) - 3.465736 * jax.random.uniform(key_list[3], (SLAB_COUNT, RADIAL), jnp.float32) ** block_levels(key_list[3], (SLAB_COUNT, RADIAL), ((0, 4),), -0.2, 0.2)), 0.25, 8.0),
        "axial_eig": jnp.clip(jnp.exp(math.log(8.0) - 3.465736 * jax.random.uniform(key_list[4], (SLAB_COUNT, INNER), jnp.float32) ** block_levels(key_list[4], (SLAB_COUNT, INNER), ((0, 4),), -0.2, 0.2)), 0.25, 8.0),
        "face_stiff": bell_draw(key_list[5], (SLAB_COUNT, RADIAL, RADIAL), RADIAL ** -0.5, 0.5, ((0, 4),), jnp.float32),
        "face_mass": bell_draw(key_list[6], (SLAB_COUNT, RADIAL, RADIAL), RADIAL ** -0.5, 0.5, ((0, 4),), jnp.float32),
        "axial_coupling": bell_draw(key_list[7], (SLAB_COUNT, 2, INNER), 0.5, 3.0, ((0, 4),), jnp.float32),
        "face_numbering": jax.vmap(lambda own: jax.random.permutation(own, RADIAL))(jax.random.split(key_list[8], SLAB_COUNT * 2)).reshape((SLAB_COUNT, 2, RADIAL)).astype(jnp.int32),
        "band_panels": draw_band_panels(jax.random.fold_in(key_list[11], 71), 0),
        "inverse_panels": draw_inverse_panels(jax.random.fold_in(key_list[11], 71), 0),
    }


HIGHEST = lax.Precision.HIGHEST

def inverse_interior(values, radial_basis, axial_basis, denominator):
    section_one = jnp.einsum('cjar,jrs->cjas', values, radial_basis, precision=HIGHEST)
    section_one = jnp.einsum('cjas,jab->cjbs', section_one, axial_basis, precision=HIGHEST)
    section_one = section_one / denominator[None]
    section_one = jnp.einsum('cjbs,jrs->cjbr', section_one, radial_basis, precision=HIGHEST)
    return jnp.einsum('cjbr,jab->cjar', section_one, axial_basis, precision=HIGHEST)

def reference(rhs_phys, radial_basis, axial_basis, radial_eig, axial_eig, face_stiff, face_mass, axial_coupling, face_numbering, band_panels, inverse_panels):
    transform = jnp.fft.rfft(rhs_phys, axis=0)[:FOURIER_COUNT] / jnp.sqrt(jnp.float32(PLANES))
    spectrum = jnp.stack([jnp.real(transform), jnp.imag(transform)], axis=1)
    onehot = (face_numbering[..., None] == jnp.arange(RADIAL, dtype=jnp.int32)).astype(jnp.float32)

    def solve_mode(inputs):
        mode_index, modal, panels = inputs
        wavenumber = mode_index.astype(jnp.float32) / FOURIER_COUNT
        wavenumber_squared = 4.0 * wavenumber * wavenumber
        fields = modal.reshape(2, SLAB_COUNT, INNER + 1, RADIAL)
        source_in = fields[:, :, :INNER]
        source_bd = fields[:, :, INNER]
        denominator = axial_eig[:, :, None] + radial_eig[:, None, :] + wavenumber_squared
        solved_values = inverse_interior(source_in, radial_basis, axial_basis, denominator)
        face_sums = jnp.einsum('cjar,jsa->cjsr', solved_values, axial_coupling, precision=HIGHEST)
        pushed = jnp.einsum('cjsr,jrq->cjsq', face_sums, face_stiff, precision=HIGHEST) + wavenumber_squared * jnp.einsum('cjsr,jrq->cjsq', face_sums, face_mass, precision=HIGHEST)
        placed = jnp.einsum('cjsq,jsqp->cjsp', pushed, onehot, precision=HIGHEST)
        from_right = jnp.concatenate([placed[:, 1:, 0], jnp.zeros((2, 1, RADIAL), jnp.float32)], axis=1)
        reduced = source_bd - placed[:, :, 1] - from_right
        coupling = band_panels[0] + wavenumber_squared * band_panels[1]

        def forward_step(carried, parts):
            panel, band, source = parts
            inner_term = source - jnp.einsum('rs,cs->cr', band, carried, precision=HIGHEST)
            value = jnp.einsum('rs,cs->cr', panel, inner_term, precision=HIGHEST)
            return (value, value)
        zero_vec = jnp.zeros((2, RADIAL), jnp.float32)
        unused_one, forward_vals = lax.scan(forward_step, zero_vec, (panels, coupling, jnp.moveaxis(reduced, 1, 0)))
        next_band = jnp.concatenate([coupling[1:], jnp.zeros((1, RADIAL, RADIAL), jnp.float32)], axis=0)

        def backward_step(carried, parts):
            panel, band, value = parts
            solution = value - jnp.einsum('rs,cs->cr', panel, carried, precision=HIGHEST)
            return (jnp.einsum('rs,cr->cs', band, solution, precision=HIGHEST), solution)
        shifted_band = coupling
        unused_two, back_vals = lax.scan(backward_step, zero_vec, (panels, shifted_band, forward_vals), reverse=True)
        interface = jnp.moveaxis(back_vals, 0, 1)
        previous = jnp.concatenate([jnp.zeros((2, 1, RADIAL), jnp.float32), interface[:, :-1]], axis=1)
        face_vals = jnp.stack([previous, interface], axis=2)
        local_face = jnp.einsum('cjsp,jsqp->cjsq', face_vals, onehot, precision=HIGHEST)
        lifted = jnp.einsum('jrq,cjsq->cjsr', face_stiff, local_face, precision=HIGHEST) + wavenumber_squared * jnp.einsum('jrq,cjsq->cjsr', face_mass, local_face, precision=HIGHEST)
        spread = jnp.einsum('cjsr,jsa->cjar', lifted, axial_coupling, precision=HIGHEST)
        interior_values = solved_values - inverse_interior(spread, radial_basis, axial_basis, denominator)
        assembled = jnp.concatenate([interior_values, interface[:, :, None]], axis=2)
        return assembled.reshape(2, NODES)
    solutions = lax.map(solve_mode, (jnp.arange(FOURIER_COUNT, dtype=jnp.int32), spectrum, inverse_panels))
    return solutions.reshape(PLANES, NODES)
```

```python
import functools
import math

import jax
import jax.numpy as jnp
import numpy as np
from jax import lax
from jax.experimental import pallas as pl
from jax.experimental.pallas import tpu as pltpu
from jax.sharding import PartitionSpec as P

F32 = jnp.float32
BF16 = jnp.bfloat16
VMEM = pl.BlockSpec(memory_space=pltpu.VMEM)
SMEM = pl.BlockSpec(memory_space=pltpu.SMEM)
NN = (((1,), (0,)), ((), ()))
NT = (((1,), (1,)), ((), ()))


def call(kernel, outs, args, smem=0, aliases=None):
    return pl.pallas_call(
        kernel,
        out_shape=outs,
        in_specs=[VMEM] * (len(args) - smem) + [SMEM] * smem,
        out_specs=[VMEM] * len(outs),
        input_output_aliases=aliases or {},
        compiler_params=pltpu.CompilerParams(vmem_limit_bytes=56 * 2**20),
    )(*args)


def split(x):
    high = x.astype(BF16)
    return high, (x - high.astype(F32)).astype(BF16)


def dot(a, b, dims=NN):
    return lax.dot_general(a, b, dims, preferred_element_type=F32)


def wide(x):
    return jnp.concatenate(split(x), axis=1)


def tall(x):
    return jnp.concatenate(split(x), axis=0)


def product(left, right):
    size = right.shape[1] // 2
    high, low = split(left)
    upper, lower = right[:, :size], right[:, size:]
    return dot(
        jnp.concatenate([high, low, high], axis=1), jnp.concatenate([upper, upper, lower], axis=0)
    )


def by_mode(x, modes):
    mode_of = lax.broadcasted_iota(jnp.int32, x.shape, 0) // 2
    spread = jnp.concatenate([jnp.where(mode_of == k, x, 0.0) for k in range(modes)], axis=1)
    return tall(spread)


def folded(out, rows):
    size = out.shape[1] // 2
    return out[:rows, :size] + out[:rows, size:] + out[rows:, :size]


def apply(x, weight, modes):
    return folded(dot(by_mode(x, modes), weight), x.shape[0])


def wave(mode_total, shape, modes, axis=0):
    first = lax.axis_index("mode") * modes
    index = first + lax.broadcasted_iota(jnp.int32, shape, axis) // 2
    number = index.astype(F32) / mode_total
    return 4.0 * number * number


def wave_of(k, mode_total, modes):
    number = (jnp.full((1, 1), lax.axis_index("mode") * modes + k, jnp.int32)).astype(F32) / mode_total
    return 4.0 * number * number


def dft_kernel(table_ref, rhs_ref, out_ref):
    high, low = split(rhs_ref[...])
    out_ref[...] = dot(table_ref[...], jnp.concatenate([high, high, low], axis=0))


def maps_kernel(
    modes,
    mode_total,
    panels_ref,
    band_ref,
    radial_ref,
    stiff_ref,
    mass_ref,
    number_ref,
    wp_ref,
    wg_ref,
    wh_ref,
    we_ref,
    rad_ref,
    radt_ref,
    face_ref,
    ship_ref,
):
    slabs = panels_ref.shape[1]
    size = panels_ref.shape[2]
    elem, last = lax.axis_index("elem"), lax.axis_size("elem") - 1
    band_t = [(band_ref[0, j].T, band_ref[1, j].T) for j in range(slabs)]
    for j in range(slabs):
        for k in range(modes):
            rows = pl.ds(k * size, size)
            weight = wide(panels_ref[k, j].T)
            wp_ref[j, rows] = weight
            lam = wave_of(k, mode_total, modes)
            wg_ref[j, rows] = wide(product(band_t[j][0] + lam * band_t[j][1], weight))
            if j + 1 < slabs:
                wh_ref[j, rows] = wide(
                    product(band_ref[0, j + 1] + lam * band_ref[1, j + 1], weight)
                )
    stiff_high, stiff_low = split(band_ref[0, 0])
    mass_high, mass_low = split(band_ref[1, 0])
    we_ref[...] = jnp.concatenate([stiff_high, mass_high, stiff_low, mass_low], axis=1)
    for j in range(slabs):
        radial = wide(radial_ref[j])
        rad_ref[j] = radial
        radt_ref[j] = wide(radial_ref[j].T)
        parts = [wide(product(ref[j].T, radial)) for ref in (stiff_ref, mass_ref)]
        both = jnp.concatenate(
            [parts[0][:, :size], parts[1][:, :size], parts[0][:, size:], parts[1][:, size:]], axis=1
        )
        for side in range(2):
            place = lax.broadcasted_iota(jnp.int32, (size, size), 0)
            onehot = jnp.where(number_ref[j, side : side + 1] == place, 1.0, 0.0).astype(BF16)
            face_ref[j, side] = dot(onehot, both).astype(BF16)

    @pl.when(elem == last)
    def _():
        for k in range(modes):
            rows = pl.ds(k * size, size)
            lam = wave_of(k, mode_total, modes)
            forward = []
            current = None
            for j in range(slabs):
                if current is None:
                    weight = wg_ref[j, rows].astype(F32)
                    current = -(weight[:, :size] + weight[:, size:])
                else:
                    current = -product(current, wg_ref[j, rows])
                forward.append(current)
            for j in range(slabs - 2, -1, -1):
                current = forward[j] - product(current, wh_ref[j, rows])
            ship_ref[k] = product(current, wide(band_ref[0, 0] + lam * band_ref[1, 0]))

    @pl.when(elem != last)
    def _():
        for k in range(modes):
            ship_ref[k] = panels_ref[k, slabs - 1]


def face_push(values, weight, lam):
    rows, size = values.shape
    high, low = split(values)
    blocks = [weight[:, i * size : (i + 1) * size] for i in range(4)]
    out = dot(
        jnp.concatenate([high, low], axis=0), jnp.concatenate(blocks, axis=0), NT
    )
    out = out[:rows, : 2 * size] + out[:rows, 2 * size :] + out[rows:, : 2 * size]
    return out[:, :size] + lam * out[:, size:]


def face_lift(values, weight, lam):
    rows, size = values.shape
    out = folded(dot(tall(values), weight), rows)
    return out[:, :size] + lam * out[:, size:]


def block_of(spec_ref, index, size):
    per = spec_ref.shape[2] // size
    at = index % per * size
    return spec_ref[index // per, :, at : at + size]


def inner_kernel(
    modes,
    mode_total,
    spec_ref,
    rad_ref,
    face_ref,
    wp_ref,
    wg_ref,
    wh_ref,
    we_ref,
    reig_ref,
    axial_ref,
    aeig_ref,
    coup_ref,
    zsrc_ref,
    solved_ref,
    y_ref,
    msg_ref,
):
    slabs, inner = aeig_ref.shape
    size = rad_ref.shape[1]
    rows = 2 * modes
    lam = wave(mode_total, (rows, size), modes)
    elem, last = lax.axis_index("elem"), lax.axis_size("elem") - 1
    pushed = []
    for j in range(slabs):
        source = jnp.concatenate(
            [block_of(spec_ref, j * (inner + 1) + a, size) for a in range(inner)], axis=0
        )
        first = folded(dot(tall(source), rad_ref[j]), inner * rows)
        first = [first[a * rows : (a + 1) * rows] for a in range(inner)]
        sums = [None, None]
        for b in range(inner):
            value = first[0] * axial_ref[j, 0, b]
            for a in range(1, inner):
                value = value + first[a] * axial_ref[j, a, b]
            value = value / (aeig_ref[j, b] + reig_ref[j : j + 1] + lam)
            zsrc_ref[j, b] = value
            for side in range(2):
                weight = coup_ref[j, side, 0] * axial_ref[j, 0, b]
                for a in range(1, inner):
                    weight = weight + coup_ref[j, side, a] * axial_ref[j, a, b]
                term = value * weight
                sums[side] = term if sums[side] is None else sums[side] + term
        pushed.append([face_push(sums[side], face_ref[j, side], lam) for side in range(2)])
    solved = []
    for j in range(slabs):
        reduced = block_of(spec_ref, j * (inner + 1) + inner, size) - pushed[j][1]
        if j + 1 < slabs:
            reduced = reduced - pushed[j + 1][0]
        solved.append(apply(reduced, wp_ref[j], modes))
        solved_ref[j] = solved[j]
    values = [solved[0]]
    for j in range(1, slabs):
        values.append(solved[j] - apply(values[-1], wg_ref[j], modes))
    for j in range(slabs):
        y_ref[j] = values[j]
    load = pushed[0][0]
    msg_ref[1] = load

    @pl.when(elem != last)
    def _():
        msg_ref[0] = values[slabs - 1]

    @pl.when(elem == last)
    def _():
        current = values[slabs - 1]
        for j in range(slabs - 2, -1, -1):
            current = values[j] - apply(current, wh_ref[j], modes)
        msg_ref[0] = load + face_lift(current, we_ref[...], lam)


def previous_weight(panel_ref, modes):
    parts = [split(panel_ref[k]) for k in range(modes)]
    return jnp.concatenate(
        [jnp.concatenate([p[i] for p in parts], axis=1) for i in range(2)], axis=0
    )


def apply_nt(x, weight, modes):
    return folded(dot(by_mode(x, modes), weight, NT), x.shape[0])


def forward_values(before, solved_ref, wg_ref, modes):
    values = []
    for j in range(solved_ref.shape[0]):
        before = solved_ref[j] - apply(before, wg_ref[j], modes)
        values.append(before)
    return values


def backward_values(values, after, wp_ref, wh_ref, modes):
    slabs = len(values)
    out = [None] * slabs
    out[-1] = values[-1] - apply(after, wp_ref[slabs - 1], modes)
    for j in range(slabs - 2, -1, -1):
        out[j] = values[j] - apply(out[j + 1], wh_ref[j], modes)
    return out


def forward_kernel(
    modes, mode_total, at, hub, got_ref, far_ref, msg_ref, pprev_ref, ship_ref, solved_ref, y_ref, wp_ref, wg_ref, wh_ref, we_ref,
    before_ref, values_ref, out_ref,
):
    rows, size = solved_ref.shape[1:]
    slabs = solved_ref.shape[0]
    lam = wave(mode_total, (rows, size), modes)

    @pl.when(lax.axis_index("elem") == at)
    def _():
        if at > 0:
            weight = previous_weight(pprev_ref, modes)
            before = got_ref[0] - apply_nt(msg_ref[1], weight, modes)
            before_ref[...] = before
            values = forward_values(before, solved_ref, wg_ref, modes)
        else:
            before_ref[...] = jnp.zeros((rows, size), F32)
            values = [y_ref[j] for j in range(slabs)]
        for j in range(slabs):
            values_ref[j] = values[j]
        if not hub:
            out_ref[0] = values[-1]
        else:
            final = values[-1] - apply(far_ref[1], wp_ref[slabs - 1], modes)
            weight = jnp.concatenate([wide(ship_ref[k]) for k in range(modes)], axis=0)
            back = far_ref[0] + apply(final, weight, modes)
            found = backward_values(values, back, wp_ref, wh_ref, modes)
            out_ref[0] = msg_ref[1] + face_lift(found[0], we_ref[...], lam)
            out_ref[1] = final
            out_ref[2] = back


def backward_kernel(modes, mode_total, at, got_ref, msg_ref, y_ref, wp_ref, wh_ref, we_ref, out_ref):
    rows, size = y_ref.shape[1:]
    lam = wave(mode_total, (rows, size), modes)

    @pl.when(lax.axis_index("elem") == at)
    def _():
        values = [y_ref[j] for j in range(y_ref.shape[0])]
        found = backward_values(values, got_ref[0], wp_ref, wh_ref, modes)
        out_ref[0] = msg_ref[1] + face_lift(found[0], we_ref[...], lam)


def final_kernel(
    modes, mode_total,
    zsrc_ref, before_ref, y_ref, after_ref, solved_ref, pprev_ref, wp_ref, wg_ref, wh_ref, we_ref, face_ref, radt_ref, reig_ref,
    axial_ref, aeig_ref, coup_ref,
    out_ref, x_ref,
):
    slabs, inner = aeig_ref.shape
    rows, size = before_ref.shape
    lam = wave(mode_total, (rows, size), modes)
    elem, last = lax.axis_index("elem"), lax.axis_size("elem") - 1

    def finish(before, found):
        for j in range(slabs):
            x_ref[j + 1] = found[j]
        weight = previous_weight(pprev_ref, modes)
        back = face_lift(found[0], we_ref[...], lam)
        x_ref[0] = before - apply_nt(back, weight, modes)

    @pl.when(elem == last)
    def _():
        before = before_ref[...]
        values = forward_values(before, solved_ref, wg_ref, modes)
        found = [None] * slabs
        found[-1] = values[-1]
        for j in range(slabs - 2, -1, -1):
            found[j] = values[j] - apply(found[j + 1], wh_ref[j], modes)
        finish(before, found)

    @pl.when(elem != last)
    def _():
        values = [y_ref[j] for j in range(slabs)]
        found = backward_values(values, after_ref[...], wp_ref, wh_ref, modes)
        finish(before_ref[...], found)

    @pl.when(elem == 0)
    def _():
        x_ref[0] = jnp.zeros((rows, size), F32)

    for j in range(slabs):
        lifted = [face_lift(x_ref[j + side], face_ref[j, side], lam) for side in range(2)]
        kept = []
        for b in range(inner):
            total = None
            for side in range(2):
                weight = coup_ref[j, side, 0] * axial_ref[j, 0, b]
                for a in range(1, inner):
                    weight = weight + coup_ref[j, side, a] * axial_ref[j, a, b]
                term = lifted[side] * weight
                total = term if total is None else total + term
            kept.append(zsrc_ref[j, b] - total / (aeig_ref[j, b] + reig_ref[j : j + 1] + lam))
        values = []
        for a in range(inner):
            value = kept[0] * axial_ref[j, a, 0]
            for b in range(1, inner):
                value = value + kept[b] * axial_ref[j, a, b]
            values.append(value)
        result = folded(dot(tall(jnp.concatenate(values, axis=0)), radt_ref[j]), inner * rows)
        for a in range(inner):
            at = (j * (inner + 1) + a) * size
            out_ref[:, at : at + size] = result[a * rows : (a + 1) * rows]
        at = (j * (inner + 1) + inner) * size
        out_ref[:, at : at + size] = x_ref[j + 1]


def dft_table(planes):
    row, col = np.arange(planes)[:, None], np.arange(planes)[None]
    angle = row // 2 * col % planes * (2.0 * math.pi / planes)
    table = np.where(row % 2 == 0, np.cos(angle), -np.sin(angle)) / math.sqrt(planes)
    table = jnp.asarray(table, F32)
    high, low = split(table)
    return jnp.concatenate([high, low, high], axis=1)


def body(
    rhs_phys, radial_basis, axial_basis, radial_eig, axial_eig, face_stiff, face_mass, axial_coupling, face_numbering,
    band_panels, inverse_panels,
):
    planes, nodes = rhs_phys.shape
    modes, slabs, size, _ = inverse_panels.shape
    inner = axial_basis.shape[1]
    devices = lax.axis_size("mode")
    elems = lax.axis_size("elem")
    mode_total = modes * devices
    rows = 2 * modes
    hub = elems - 2
    here = lax.axis_index("elem")

    def shape(*dims):
        return jax.ShapeDtypeStruct(dims, F32)

    def half(*dims):
        return jax.ShapeDtypeStruct(dims, BF16)

    spectrum = call(dft_kernel, [shape(planes, nodes)], [dft_table(planes), rhs_phys])[0]
    spectrum = lax.all_to_all(spectrum.reshape(devices, rows, nodes), "mode", 0, 0, tiled=False)
    if nodes % size:
        spectrum = jnp.swapaxes(spectrum, 0, 1).reshape(1, rows, devices * nodes)
    wp, wg, wh, we, rad, radt, face, ship = call(
        functools.partial(maps_kernel, modes, mode_total),
        [
            half(slabs, modes * size, 2 * size),
            half(slabs, modes * size, 2 * size),
            half(slabs - 1, modes * size, 2 * size),
            half(size, 4 * size),
            half(slabs, size, 2 * size),
            half(slabs, size, 2 * size),
            half(slabs, 2, size, 4 * size),
            shape(modes, size, size),
        ],
        [inverse_panels, band_panels, radial_basis, face_stiff, face_mass, face_numbering],
    )
    pprev = lax.ppermute(ship, "elem", [(i, i + 1) for i in range(elems - 1)])
    far_map = lax.ppermute(ship, "elem", [(elems - 1, hub)])
    zsrc, solved, y, msg = call(
        functools.partial(inner_kernel, modes, mode_total),
        [shape(slabs, inner, rows, size), shape(slabs, rows, size), shape(slabs, rows, size), shape(2, rows, size)],
        [spectrum, rad, face, wp, wg, wh, we, radial_eig, axial_basis, axial_eig, axial_coupling],
        smem=3,
    )
    far = lax.ppermute(msg, "elem", [(elems - 1, hub)])
    before = jnp.zeros((rows, size), F32)
    send = msg[:1]
    values = y
    for at in range(hub + 1):
        got = lax.ppermute(send, "elem", [(at - 1, at)]) if at > 0 else send
        if at == 0 and hub > 0:
            continue
        before_new, values_new, out = call(
            functools.partial(forward_kernel, modes, mode_total, at, at == hub),
            [shape(rows, size), shape(slabs, rows, size), shape(3 if at == hub else 1, rows, size)],
            [got, far, msg, pprev, far_map, solved, y, wp, wg, wh, we],
        )
        before = jnp.where(here == at, before_new, before)
        values = jnp.where(here == at, values_new, values)
        send = out
    after = jnp.where(here == hub, out[2], 0.0)
    final = lax.ppermute(out[1], "elem", [(hub, elems - 1)])
    before = jnp.where(here == elems - 1, final, before)
    send = out[:1]
    for at in range(hub - 1, -1, -1):
        got = lax.ppermute(send, "elem", [(at + 1, at)])
        after = jnp.where(here == at, got[0], after)
        if at > 0:
            send = call(
                functools.partial(backward_kernel, modes, mode_total, at),
                [shape(1, rows, size)],
                [got, msg, values, wp, wh, we],
            )[0]
    return call(
        functools.partial(final_kernel, modes, mode_total),
        [shape(rows, slabs * (inner + 1) * size), shape(slabs + 1, rows, size)],
        [zsrc, before, values, after, solved, pprev, wp, wg, wh, we, face, radt, radial_eig, axial_basis, axial_eig, axial_coupling],
        smem=3,
    )[0]


def solution(mesh):
    placed = (
        P(None, ("elem", "mode")),
        P("elem", None, None),
        P("elem", None, None),
        P("elem", None),
        P("elem", None),
        P("elem", None, None),
        P("elem", None, None),
        P("elem", None, None),
        P("elem", None, None),
        P(None, "elem", None, None),
        P("mode", "elem", None, None),
    )
    return jax.shard_map(
        body, mesh=mesh, in_specs=placed, out_specs=P("mode", "elem"), check_vma=False
    )
```

```python
import functools
import math

import jax
import jax.numpy as jnp
import numpy as np
from jax import lax
from jax.experimental import pallas as pl
from jax.experimental.pallas import tpu as pltpu
from jax.sharding import PartitionSpec as P

F32 = jnp.float32
BF16 = jnp.bfloat16
VMEM = pl.BlockSpec(memory_space=pltpu.VMEM)
SMEM = pl.BlockSpec(memory_space=pltpu.SMEM)
HBM = pl.BlockSpec(memory_space=pltpu.HBM)
COST_INNER = 2**24
NN = (((1,), (0,)), ((), ()))
NT = (((1,), (1,)), ((), ()))


def call(kernel, outs, args, smem=0, anywhere=0, outside=0, scratch=(), aliases=None, cost=0):
    inside = len(args) - smem - anywhere
    spaces = [pltpu.HBM] * anywhere + [pltpu.VMEM] * inside + [pltpu.SMEM] * smem
    args = [pltpu.with_memory_space_constraint(arg, space) for arg, space in zip(args, spaces)]
    return pl.pallas_call(
        kernel,
        out_shape=outs,
        in_specs=[HBM] * anywhere + [VMEM] * inside + [SMEM] * smem,
        out_specs=[HBM if getattr(out, "memory_space", None) is pltpu.HBM else VMEM for out in outs[: len(outs) - outside]]
        + [SMEM] * outside,
        scratch_shapes=scratch,
        input_output_aliases=aliases or {},
        cost_estimate=pl.CostEstimate(flops=0, bytes_accessed=cost, transcendentals=0),
        compiler_params=pltpu.CompilerParams(vmem_limit_bytes=16 * 2**20),
    )(*args)


def split(x):
    high = x.astype(BF16)
    return high, (x - high.astype(F32)).astype(BF16)


def dot(a, b, dims=NN):
    return lax.dot_general(a, b, dims, preferred_element_type=F32)


def wide(x):
    return jnp.concatenate(split(x), axis=1)


def tall(x):
    return jnp.concatenate(split(x), axis=0)


def product(left, right):
    size = right.shape[1] // 2
    high, low = split(left)
    upper, lower = right[:, :size], right[:, size:]
    return dot(
        jnp.concatenate([high, low, high], axis=1), jnp.concatenate([upper, upper, lower], axis=0)
    )


def by_mode(x, modes):
    mode_of = lax.broadcasted_iota(jnp.int32, x.shape, 0) // 2
    spread = jnp.concatenate([jnp.where(mode_of == k, x, 0.0) for k in range(modes)], axis=1)
    return tall(spread)


def folded(out, rows):
    size = out.shape[1] // 2
    return out[:rows, :size] + out[:rows, size:] + out[rows:, :size]


def apply(x, weight, modes):
    return folded(dot(by_mode(x, modes), weight), x.shape[0])


def wave(mode_total, shape, modes, axis=0):
    first = lax.axis_index("mode") * modes
    index = first + lax.broadcasted_iota(jnp.int32, shape, axis) // 2
    number = index.astype(F32) / mode_total
    return 4.0 * number * number


def wave_of(k, mode_total, modes):
    number = (jnp.full((1, 1), lax.axis_index("mode") * modes + k, jnp.int32)).astype(F32) / mode_total
    return 4.0 * number * number


class Weights:
    def __init__(self, size, *entries):
        self.size, self.rows = size, {}
        self.total = 0
        for name, count, rows in entries:
            self.rows[name] = (self.total, rows)
            self.total += count * rows

    def at(self, name, index, mode=None):
        start, rows = self.rows[name]
        if mode is None:
            return pl.ds(start + index * rows, rows)
        return pl.ds(start + index * rows + mode * self.size, self.size)

    def pair(self, ref, name, index):
        return jnp.concatenate([ref[self.at(name, index)], ref[self.at(name, index + 1)]], axis=1)

    def face(self, ref, slab, side):
        return self.pair(ref, "face", 4 * slab + 2 * side)


def band_of(ref, slab):
    return jnp.concatenate([ref[2 * slab], ref[2 * slab + 1]], axis=1)


def whole(weight):
    size = weight.shape[1] // 2
    value = weight.astype(F32)
    return value[:, :size] + value[:, size:]


def start_copies(pairs, sems):
    copies = [pltpu.make_async_copy(src, dst, sems.at[i]) for i, (src, dst) in enumerate(pairs)]
    for copy in copies:
        copy.start()
    return copies


def transform(rhs_ref, table_ref, out_ref, rhs_buf, table_buf, sems):
    for copy in start_copies([(rhs_ref, rhs_buf), (table_ref, table_buf)], sems):
        copy.wait()
    high, low = split(rhs_buf[...])
    rhs_buf[...] = dot(table_buf[...], jnp.concatenate([high, high, low], axis=0))
    for copy in start_copies([(rhs_buf, out_ref)], sems):
        copy.wait()


def dft_kernel(rhs_ref, table_ref, old_ref, out_ref, rhs_buf, table_buf, sems):
    @pl.when(lax.axis_index("elem") != 0)
    def _():
        transform(rhs_ref, table_ref, out_ref, rhs_buf, table_buf, sems)


def far_kernel(
    modes, mode_total, panels_ref, band_ref, rhs_ref, table_ref, ship_ref, out_ref, panels_buf, band_buf, rhs_buf, table_buf, sems
):
    slabs, size = panels_ref.shape[1:3]
    elem, last = lax.axis_index("elem"), lax.axis_size("elem") - 1
    line = (panels_ref.at[:, slabs - 1], ship_ref)
    parts = sems.at[pl.ds(2, slabs + 1)]

    @pl.when(elem != last)
    def _():
        start_copies([line], parts)

    @pl.when(elem == 0)
    def _():
        transform(rhs_ref, table_ref, out_ref, rhs_buf, table_buf, sems)

    @pl.when(elem != last)
    def _():
        pltpu.make_async_copy(*line, sems.at[2]).wait()

    @pl.when(elem == last)
    def _():
        copies = start_copies(
            [(band_ref, band_buf)] + [(panels_ref.at[:, j], panels_buf.at[j]) for j in range(slabs)], parts
        )
        copies[0].wait()
        band_t = [(band_buf[0, j].T, band_buf[1, j].T) for j in range(slabs)]
        lam = [wave_of(k, mode_total, modes) for k in range(modes)]
        forward, weights = [], []
        for j in range(slabs):
            copies[1 + j].wait()
            weights.append([wide(panels_buf[j, k].T) for k in range(modes)])
            steps = [product(band_t[j][0] + lam[k] * band_t[j][1], weights[j][k]) for k in range(modes)]
            if j == 0:
                forward.append([-step for step in steps])
            else:
                forward.append([-product(forward[-1][k], wide(steps[k])) for k in range(modes)])
        current = forward[-1]
        for j in range(slabs - 2, -1, -1):
            steps = [
                product(band_buf[0, j + 1] + lam[k] * band_buf[1, j + 1], weights[j][k]) for k in range(modes)
            ]
            current = [forward[j][k] - product(current[k], wide(steps[k])) for k in range(modes)]
        for k in range(modes):
            ship_ref[k] = product(current[k], wide(band_buf[0, 0] + lam[k] * band_buf[1, 0]))


def maps_kernel(
    modes, mode_total, hub, place, panels_ref, band_ref, radial_ref, stiff_ref, mass_ref, number_ref, reig_ref, axial_ref, aeig_ref,
    coup_ref, bands_ref, front_ref, w_ref, reig_out, axial_out, weight_out, aeig_out,
    panels_buf, band_buf, radial_buf, stiff_buf, mass_buf, number_buf, axial_buf, coup_buf, bands_buf, front_buf, sems,
):
    slabs, size = panels_ref.shape[1:3]
    inner = aeig_ref.shape[1]
    copies = start_copies(
        [(radial_ref, radial_buf), (stiff_ref, stiff_buf), (mass_ref, mass_buf), (number_ref, number_buf), (band_ref, band_buf)]
        + [(panels_ref.at[:, j], panels_buf.at[j]) for j in range(slabs)]
        + [(axial_ref, axial_buf), (coup_ref, coup_buf), (aeig_ref, aeig_out), (reig_ref, reig_out)],
        sems,
    )
    for copy in copies[:4]:
        copy.wait()
    for j in range(slabs):
        radial = wide(radial_buf[j])
        w_ref[place.at("radial", j)] = radial
        parts = [wide(product(ref[j].T, radial)) for ref in (stiff_buf, mass_buf)]
        for side in range(2):
            spot = lax.broadcasted_iota(jnp.int32, (size, size), 0)
            onehot = jnp.where(number_buf[j, side : side + 1] == spot, 1.0, 0.0).astype(BF16)
            for i in range(2):
                both = jnp.concatenate([p[:, i * size : (i + 1) * size] for p in parts], axis=1)
                w_ref[place.at("face", 4 * j + 2 * side + i)] = dot(onehot, both).astype(BF16)
    copies[4].wait()
    for j in range(slabs):
        bands = wide(jnp.concatenate([band_buf[0, j], band_buf[1, j]], axis=1))
        for i in range(2):
            bands_buf[2 * j + i] = bands[:, 2 * i * size : 2 * (i + 1) * size]
    bands_copy = start_copies([(bands_buf, bands_ref)], sems)[0]
    for j in range(slabs):
        copies[5 + j].wait()
        for k in range(modes):
            w_ref[place.at("panel", j, k)] = wide(panels_buf[j, k].T)
    for copy in copies[5 + slabs :]:
        copy.wait()
    for j in range(slabs):
        for b in range(inner):
            for a in range(inner):
                axial_out[j, a, b] = axial_buf[j, a, b]
            for side in range(2):
                weight = coup_buf[j, side, 0] * axial_buf[j, 0, b]
                for a in range(1, inner):
                    weight = weight + coup_buf[j, side, a] * axial_buf[j, a, b]
                weight_out[j, side, b] = weight

    @pl.when((lax.axis_index("elem") > 0) & (lax.axis_index("elem") <= hub))
    def _():
        lam = [wave_of(k, mode_total, modes) for k in range(modes)]
        current = None
        for j in range(slabs):
            first, second = band_buf[0, j].T, band_buf[1, j].T
            steps = [product(first + lam[k] * second, w_ref[place.at("panel", j, k)]) for k in range(modes)]
            if current is None:
                current = [-step for step in steps]
            else:
                current = [-product(current[k], wide(steps[k])) for k in range(modes)]
        for k in range(modes):
            front_buf[pl.ds(k * size, size)] = wide(current[k])
        for copy in start_copies([(front_buf, front_ref)], sems.at[pl.ds(1, 1)]):
            copy.wait()

    bands_copy.wait()


def face_push(values, weight, lam):
    rows, size = values.shape
    high, low = split(values)
    blocks = [weight[:, i * size : (i + 1) * size] for i in range(4)]
    out = dot(
        jnp.concatenate([high, low], axis=0), jnp.concatenate(blocks, axis=0), NT
    )
    out = out[:rows, : 2 * size] + out[:rows, 2 * size :] + out[rows:, : 2 * size]
    return out[:, :size] + lam * out[:, size:]


def face_lift(values, weight, lam):
    rows, size = values.shape
    out = folded(dot(tall(values), weight), rows)
    return out[:, :size] + lam * out[:, size:]


def block_of(spec_ref, index, size):
    per = spec_ref.shape[2] // size
    at = index % per * size
    return spec_ref[index // per, :, at : at + size]


def band_step(values, weight, lam):
    return face_push(values, weight, lam)


def inner_kernel(
    modes, mode_total, place, first_call, bands_ref, spec_ref, w_ref, reig_ref, *refs
):
    axial_ref, weight_ref, aeig_ref, bands_out, zsrc_ref, inv_ref, reduced_ref, y_ref, out_ref, sems = refs[-10:]

    @pl.when((lax.axis_index("elem") == 0) == first_call)
    def _():
        inner_part(
            modes, mode_total, place, first_call, bands_ref, spec_ref, w_ref, reig_ref, axial_ref, weight_ref, aeig_ref,
            bands_out, zsrc_ref, inv_ref, reduced_ref, y_ref, out_ref, sems,
        )


def inner_part(
    modes, mode_total, place, first_call, bands_ref, spec_ref, w_ref, reig_ref, axial_ref, weight_ref, aeig_ref,
    bands_out, zsrc_ref, inv_ref, solved_ref, y_ref, out_ref, sems,
):
    slabs, inner, rows, size = zsrc_ref.shape
    lam = wave(mode_total, (rows, size), modes)
    elem, last = lax.axis_index("elem"), lax.axis_size("elem") - 1
    bands_copy = start_copies([(bands_ref, bands_out)], sems)[0]
    pushed = []
    for j in range(slabs):
        source = jnp.concatenate(
            [block_of(spec_ref, j * (inner + 1) + a, size) for a in range(inner)], axis=0
        )
        first = folded(dot(tall(source), w_ref[place.at("radial", j)]), inner * rows)
        first = [first[a * rows : (a + 1) * rows] for a in range(inner)]
        sums = [None, None]
        for b in range(inner):
            value = first[0] * axial_ref[j, 0, b]
            for a in range(1, inner):
                value = value + first[a] * axial_ref[j, a, b]
            inverse = 1.0 / (aeig_ref[j, b] + reig_ref[j : j + 1] + lam)
            inv_ref[j, b] = inverse
            value = value * inverse
            zsrc_ref[j, b] = value
            for side in range(2):
                term = value * weight_ref[j, side, b]
                sums[side] = term if sums[side] is None else sums[side] + term
        pushed.append([face_push(sums[side], place.face(w_ref, j, side), lam) for side in range(2)])
    load = pushed[0][0]
    bands_copy.wait()
    values = []
    for j in range(slabs):
        reduced = block_of(spec_ref, j * (inner + 1) + inner, size) - pushed[j][1]
        if j + 1 < slabs:
            reduced = reduced - pushed[j + 1][0]
        panel = w_ref[place.at("panel", j)]
        solved_ref[j] = reduced
        if j > 0:
            reduced = reduced - band_step(values[-1], band_of(bands_out, j), lam)
        values.append(apply(reduced, panel, modes))
        y_ref[j] = values[j]
    if first_call:
        out_ref[...] = values[slabs - 1]
        return
    out_ref[1] = load

    @pl.when(elem == last)
    def _():
        current = values[slabs - 1]
        for j in range(slabs - 2, -1, -1):
            step = face_lift(current, band_of(bands_out, j + 1), lam)
            current = values[j] - apply(step, w_ref[place.at("panel", j)], modes)
        out_ref[0] = load + face_lift(current, band_of(bands_out, 0), lam)


def previous_weight(panel_ref, modes):
    parts = [split(panel_ref[k]) for k in range(modes)]
    return jnp.concatenate(
        [jnp.concatenate([p[i] for p in parts], axis=1) for i in range(2)], axis=0
    )


def apply_nt(x, weight, modes):
    return folded(dot(by_mode(x, modes), weight, NT), x.shape[0])


def forward_values(before, solved_ref, ahead_ref, modes):
    values = []
    for j in range(solved_ref.shape[0]):
        before = solved_ref[j] - apply(before, ahead_ref[j], modes)
        values.append(before)
    return values


def backward_values(values, after, panel, behind_ref, modes):
    slabs = len(values)
    out = [None] * slabs
    out[-1] = values[-1]
    if after is not None:
        out[-1] = out[-1] - apply(after, panel, modes)
    for j in range(slabs - 2, -1, -1):
        out[j] = values[j] - apply(out[j + 1], behind_ref[j], modes)
    return out


def push_kernel(modes, hub, pprev_ref, front_ref, load_ref, front_out, prev_ref, push_ref, prev_buf, sems):
    elem = lax.axis_index("elem")

    @pl.when((elem > 0) & (elem <= hub))
    def _():
        for copy in start_copies([(pprev_ref, prev_buf), (front_ref, front_out)], sems):
            copy.wait()
        weight = previous_weight(prev_buf, modes)
        prev_ref[...] = weight
        push_ref[...] = apply_nt(load_ref[1], weight, modes)


def forward_kernel(modes, at, got_ref, push_ref, y_ref, front_ref, old_ref, state_ref, send_ref):
    @pl.when(lax.axis_index("elem") == at)
    def _():
        before = got_ref[...] - push_ref[...]
        state_ref[0] = before
        send_ref[...] = y_ref[y_ref.shape[0] - 1] + apply(before, front_ref[...], modes)


def backward_map_kernel(modes, mode_total, hub, hub_call, *refs):
    inputs, outputs = refs[:9], refs[-(12 if hub_call else 13) :]

    @pl.when((lax.axis_index("elem") == hub) == hub_call)
    def _():
        backward_maps(modes, mode_total, hub, hub_call, *inputs, *outputs)


def backward_maps(
    modes, mode_total, hub, hub_call, band_ref, radial_ref, map_ref, state_ref, load_ref, reduced_ref, y_ref, panel_ref, bands_ref,
    ahead_ref, behind_ref, radt_ref, solved_ref, back_ref, base_ref, *rest,
):
    *rest, band_buf, radial_buf, map_buf, sems = rest
    elem = lax.axis_index("elem")
    slabs, rows, size = reduced_ref.shape
    lam = wave(mode_total, (rows, size), modes)
    waves = [wave_of(k, mode_total, modes) for k in range(modes)]
    pairs = [(band_ref, band_buf), (radial_ref, radial_buf)]
    copies = start_copies(pairs + [(map_ref, map_buf)] if hub_call else pairs, sems)

    def part(k):
        return pl.ds(k * size, size)

    for j in range(slabs):
        solved_ref[j] = apply(reduced_ref[j], panel_ref[pl.ds(j * modes * size, modes * size)], modes)
    for copy in copies[:2]:
        copy.wait()
    for j in range(slabs):
        radt_ref[j] = wide(radial_buf[j].T)
    for j in range(slabs):
        first, second = band_buf[0, j].T, band_buf[1, j].T
        for k in range(modes):
            ahead_ref[j, part(k)] = wide(product(first + waves[k] * second, panel_ref[part(j * modes + k)]))
    for j in range(slabs - 1):
        for k in range(modes):
            behind_ref[j, part(k)] = wide(
                product(band_buf[0, j + 1] + waves[k] * band_buf[1, j + 1], panel_ref[part(j * modes + k)])
            )

    def entry(k):
        return wide(band_buf[0, 0] + waves[k] * band_buf[1, 0])

    def back_maps(outs):
        current = [-whole(panel_ref[part((slabs - 1) * modes + k)]) for k in range(modes)]
        for j in range(slabs - 2, -1, -1):
            current = [-product(current[k], behind_ref[j, part(k)]) for k in range(modes)]
            for k in range(modes):
                if outs:
                    outs[j][part(k)] = wide(current[k])

        @pl.when(elem > 0)
        def _():
            for k in range(modes):
                back_ref[part(k)] = wide(product(current[k], entry(k)))

    def base(values, found_ref):
        found = backward_values(values, None, None, behind_ref, modes)
        if found_ref is not None:
            for j in range(slabs):
                found_ref[j] = found[j]
        base_ref[...] = load_ref[1] + face_lift(found[0], band_of(bands_ref, 0), lam)

    if hub_call:
        cross_ref, far_weight_ref = rest
        base([y_ref[j] for j in range(slabs)], None)
        back_maps(None)
        forward = [[-whole(ahead_ref[0, part(k)]) for k in range(modes)]]
        for j in range(1, slabs):
            forward.append([-product(forward[-1][k], ahead_ref[j, part(k)]) for k in range(modes)])
        current = forward[-1]
        for j in range(slabs - 2, -1, -1):
            current = [forward[j][k] - product(current[k], behind_ref[j, part(k)]) for k in range(modes)]
        for k in range(modes):
            cross_ref[part(k)] = wide(product(current[k], entry(k)))
        copies[2].wait()
        for k in range(modes):
            far_weight_ref[part(k)] = wide(map_buf[k])
        return
    near_ref, mid_ref, found_ref = rest

    @pl.when(elem < hub)
    def _():
        back_maps({0: near_ref, 1: mid_ref})

    @pl.when(elem == 0)
    def _():
        base([y_ref[j] for j in range(slabs)], found_ref)

    @pl.when((elem > 0) & (elem < hub))
    def _():
        base(forward_values(state_ref[0], solved_ref, ahead_ref, modes), found_ref)


def hub_kernel(
    modes, at, place, got_ref, push_ref, far_ref, far_weight_ref, y_ref, front_ref, back_ref, cross_ref, base_ref, w_ref, old_ref,
    state_ref, send_ref, last_ref,
):
    slabs = y_ref.shape[0]

    @pl.when(lax.axis_index("elem") == at)
    def _():
        panel = w_ref[place.at("panel", slabs - 1)]
        load = apply(far_ref[1], panel, modes)
        value = y_ref[slabs - 1]
        out = base_ref[...]
        if at > 0:
            before = got_ref[...] - push_ref[...]
            state_ref[0] = before
            value = value + apply(before, front_ref[...], modes)
            out = out + apply(before, cross_ref[...], modes)
        final = value - load
        after = far_ref[0] + apply(final, far_weight_ref[...], modes)
        state_ref[1] = after
        send_ref[...] = out + apply(after, back_ref[...], modes)
        last_ref[0] = final
        last_ref[1] = value - apply(after, panel, modes)


def backward_kernel(modes, at, got_ref, base_ref, back_ref, old_ref, state_ref, send_ref):
    @pl.when(lax.axis_index("elem") == at)
    def _():
        after = got_ref[...]
        state_ref[1] = after
        send_ref[...] = base_ref[...] + apply(after, back_ref[...], modes)


def final_kernel(
    modes, mode_total, hub, place, zsrc_ref, inv_ref, state_ref, got_ref, last_ref, found_ref, near_ref, mid_ref, solved_ref, prev_ref, w_ref, bands_ref, ahead_ref,
    behind_ref, radt_ref, axial_ref, weight_ref, out_ref, x_ref,
):
    slabs, inner, rows, size = zsrc_ref.shape
    lam = wave(mode_total, (rows, size), modes)
    elem, last = lax.axis_index("elem"), lax.axis_size("elem") - 1
    maps = {0: near_ref, 1: mid_ref}

    def backward(after):
        for j in range(slabs - 1):
            x_ref[j + 1] = found_ref[j] + apply(after, maps[j][...], modes)
        x_ref[slabs] = found_ref[slabs - 1] - apply(after, w_ref[place.at("panel", slabs - 1)], modes)

    def before_first(before):
        back = face_lift(x_ref[1], band_of(bands_ref, 0), lam)
        x_ref[0] = before - apply_nt(back, prev_ref[...], modes)

    @pl.when(elem == 0)
    def _():
        x_ref[0] = jnp.zeros((rows, size), F32)
        backward(got_ref[...])

    @pl.when((elem > 0) & (elem < hub))
    def _():
        backward(state_ref[1])
        before_first(state_ref[0])

    @pl.when(elem == hub)
    def _():
        values = forward_values(state_ref[0], solved_ref, ahead_ref, modes)
        found = backward_values(values, state_ref[1], w_ref[place.at("panel", slabs - 1)], behind_ref, modes)
        for j in range(slabs):
            x_ref[j + 1] = found[j]
        before_first(state_ref[0])

    @pl.when(elem == last)
    def _():
        values = forward_values(last_ref[0], solved_ref, ahead_ref, modes)
        found = backward_values(values, None, None, behind_ref, modes)
        for j in range(slabs):
            x_ref[j + 1] = found[j]
        x_ref[0] = last_ref[1]

    for j in range(slabs):
        lifted = [face_lift(x_ref[j + side], place.face(w_ref, j, side), lam) for side in range(2)]
        kept = []
        for b in range(inner):
            total = lifted[0] * weight_ref[j, 0, b] + lifted[1] * weight_ref[j, 1, b]
            kept.append(zsrc_ref[j, b] - total * inv_ref[j, b])
        values = []
        for a in range(inner):
            value = kept[0] * axial_ref[j, a, 0]
            for b in range(1, inner):
                value = value + kept[b] * axial_ref[j, a, b]
            values.append(value)
        result = dot(tall(jnp.concatenate(values, axis=0)), radt_ref[j])
        result = folded(result, inner * rows)
        for a in range(inner):
            at = (j * (inner + 1) + a) * size
            out_ref[:, at : at + size] = result[a * rows : (a + 1) * rows]
        at = (j * (inner + 1) + inner) * size
        out_ref[:, at : at + size] = x_ref[j + 1]


def dft_table(planes):
    row, col = np.arange(planes)[:, None], np.arange(planes)[None]
    angle = row // 2 * col % planes * (2.0 * math.pi / planes)
    table = np.where(row % 2 == 0, np.cos(angle), -np.sin(angle)) / math.sqrt(planes)
    table = jnp.asarray(table, F32)
    high, low = split(table)
    return jnp.concatenate([high, low, high], axis=1)


def body(
    rhs_phys, radial_basis, axial_basis, radial_eig, axial_eig, face_stiff, face_mass, axial_coupling, face_numbering,
    band_panels, inverse_panels,
):
    planes, nodes = rhs_phys.shape
    modes, slabs, size, _ = inverse_panels.shape
    inner = axial_basis.shape[1]
    devices = lax.axis_size("mode")
    elems = lax.axis_size("elem")
    mode_total = modes * devices
    rows = 2 * modes
    hub = elems - 2
    last = elems - 1

    def shape(*dims):
        return jax.ShapeDtypeStruct(dims, F32)

    def kept(*dims):
        return pltpu.VMEM(dims, F32)

    def half(*dims):
        return pltpu.VMEM(dims, BF16)

    table = dft_table(planes)
    many = modes * size
    place = Weights(size, ("panel", slabs, many), ("radial", slabs, size), ("face", 4 * slabs, size))
    ship, spectrum = call(
        functools.partial(far_kernel, modes, mode_total),
        [shape(modes, size, size), pltpu.HBM((planes, nodes), F32)],
        [inverse_panels, band_panels, rhs_phys, table],
        anywhere=4,
        scratch=[
            pltpu.VMEM((slabs, modes, size, size), F32),
            pltpu.VMEM(band_panels.shape, F32),
            pltpu.VMEM(rhs_phys.shape, F32),
            pltpu.VMEM(table.shape, BF16),
            pltpu.SemaphoreType.DMA((slabs + 3,)),
        ],
    )
    far_map = lax.ppermute(ship, "elem", [(last, hub)])
    pprev = lax.ppermute(ship, "elem", [(i, i + 1) for i in range(hub)])
    spectrum = call(
        dft_kernel,
        [pltpu.HBM((planes, nodes), F32)],
        [rhs_phys, table, spectrum],
        anywhere=3,
        scratch=[pltpu.VMEM(rhs_phys.shape, F32), pltpu.VMEM(table.shape, BF16), pltpu.SemaphoreType.DMA((2,))],
        aliases={2: 0},
    )[0]
    spectrum = lax.all_to_all(spectrum.reshape(devices, rows, nodes), "mode", 0, 0, tiled=False)
    if nodes % size:
        spectrum = jnp.swapaxes(spectrum, 0, 1).reshape(1, rows, devices * nodes)
    vector = (rows, size)
    matrix = half(many, 2 * size)
    bands, front, w, reig, axial, weight, aeig = call(
        functools.partial(maps_kernel, modes, mode_total, hub, place),
        [
            pltpu.HBM((2 * slabs, size, 2 * size), BF16),
            pltpu.HBM((many, 2 * size), BF16),
            half(place.total, 2 * size),
            kept(*radial_eig.shape),
            pltpu.SMEM(axial_basis.shape, F32),
            pltpu.SMEM((slabs, 2, inner), F32),
            pltpu.SMEM(axial_eig.shape, F32),
        ],
        [
            inverse_panels, band_panels, radial_basis, face_stiff, face_mass, face_numbering,
            radial_eig, axial_basis, axial_eig, axial_coupling,
        ],
        anywhere=10,
        outside=3,
        scratch=[
            pltpu.VMEM((slabs, modes, size, size), F32),
            pltpu.VMEM(band_panels.shape, F32),
            pltpu.VMEM(radial_basis.shape, F32),
            pltpu.VMEM(face_stiff.shape, F32),
            pltpu.VMEM(face_mass.shape, F32),
            pltpu.VMEM(face_numbering.shape, jnp.int32),
            pltpu.SMEM(axial_basis.shape, F32),
            pltpu.SMEM(axial_coupling.shape, F32),
            pltpu.VMEM((2 * slabs, size, 2 * size), BF16),
            pltpu.VMEM((many, 2 * size), BF16),
            pltpu.SemaphoreType.DMA((slabs + 9,)),
        ],
    )
    solves = [
        half(2 * slabs, size, 2 * size), kept(slabs, inner, *vector), kept(slabs, inner, *vector), kept(slabs, *vector),
        kept(slabs, *vector),
    ]
    *solve, send = call(
        functools.partial(inner_kernel, modes, mode_total, place, True),
        solves + [kept(*vector)],
        [bands, spectrum, w, reig, axial, weight, aeig],
        anywhere=1,
        smem=3,
        scratch=[pltpu.SemaphoreType.DMA((1,))],
    )
    got = lax.ppermute(send, "elem", [(0, 1)])
    bands, zsrc, inv, reduced, y, load = call(
        functools.partial(inner_kernel, modes, mode_total, place, False),
        solves + [kept(2, *vector)],
        [bands, spectrum, w, reig, *solve, axial, weight, aeig],
        anywhere=1,
        smem=3,
        scratch=[pltpu.SemaphoreType.DMA((1,))],
        aliases={4 + i: i for i in range(5)},
    )
    far = lax.ppermute(load, "elem", [(last, hub)])
    front, prev, push = call(
        functools.partial(push_kernel, modes, hub),
        [matrix, half(2 * size, many), kept(*vector)],
        [pprev, front, load],
        anywhere=2,
        scratch=[pltpu.VMEM((modes, size, size), F32), pltpu.SemaphoreType.DMA((2,))],
    )
    state = jnp.zeros((2, *vector), F32)
    for at in range(1, hub):
        state, send = call(
            functools.partial(forward_kernel, modes, at),
            [kept(*state.shape), shape(*vector)],
            [got, push, y, front, state],
            aliases={4: 0},
        )
        got = lax.ppermute(send, "elem", [(at, at + 1)])
    maps = [
        half(slabs, many, 2 * size), half(slabs - 1, many, 2 * size), half(slabs, size, 2 * size), kept(slabs, *vector),
        matrix, kept(*vector),
    ]
    scratch = [
        pltpu.VMEM(band_panels.shape, F32),
        pltpu.VMEM(radial_basis.shape, F32),
        pltpu.VMEM((modes, size, size), F32),
        pltpu.SemaphoreType.DMA((3,)),
    ]
    *known, cross, far_weight = call(
        functools.partial(backward_map_kernel, modes, mode_total, hub, True),
        maps + [matrix, matrix],
        [band_panels, radial_basis, far_map, state, load, reduced, y, w, bands],
        anywhere=3,
        scratch=scratch,
    )
    state, send, final = call(
        functools.partial(hub_kernel, modes, hub, place),
        [kept(*state.shape), shape(*vector), shape(2, *vector)],
        [got, push, far, far_weight, y, front, known[4], cross, known[5], w, state],
        aliases={10: 0},
    )
    ahead, behind, radt, solved, back, base, near, mid, found = call(
        functools.partial(backward_map_kernel, modes, mode_total, hub, False),
        maps + [matrix, matrix, kept(slabs, *vector)],
        [band_panels, radial_basis, far_map, state, load, reduced, y, w, bands, *known],
        anywhere=3,
        scratch=scratch,
        aliases={9 + i: i for i in range(6)},
    )
    got = send
    for at in range(hub - 1, -1, -1):
        got = lax.ppermute(send, "elem", [(at + 1, at)])
        if at > 0:
            state, send = call(
                functools.partial(backward_kernel, modes, at),
                [kept(*state.shape), shape(*vector)],
                [got, base, back, state],
                aliases={3: 0},
            )
    final = lax.ppermute(final, "elem", [(hub, last)])
    return call(
        functools.partial(final_kernel, modes, mode_total, hub, place),
        [shape(rows, slabs * (inner + 1) * size)],
        [zsrc, inv, state, got, final, found, near, mid, solved, prev, w, bands, ahead, behind, radt, axial, weight],
        smem=2,
        scratch=[pltpu.VMEM((slabs + 1, *vector), F32)],
    )[0]


def solution(mesh):
    placed = (
        P(None, ("elem", "mode")),
        P("elem", None, None),
        P("elem", None, None),
        P("elem", None),
        P("elem", None),
        P("elem", None, None),
        P("elem", None, None),
        P("elem", None, None),
        P("elem", None, None),
        P(None, "elem", None, None),
        P("mode", "elem", None, None),
    )
    return jax.shard_map(
        body, mesh=mesh, in_specs=placed, out_specs=P("mode", "elem"), check_vma=False
    )
```

```python
import functools
import math

import jax
import jax.numpy as jnp
import numpy as np
from jax import lax
from jax.experimental import pallas as pl
from jax.experimental.pallas import tpu as pltpu
from jax.sharding import PartitionSpec as P

F32 = jnp.float32
BF16 = jnp.bfloat16
VMEM = pl.BlockSpec(memory_space=pltpu.VMEM)
SMEM = pl.BlockSpec(memory_space=pltpu.SMEM)
HBM = pl.BlockSpec(memory_space=pltpu.HBM)
ANY = pl.BlockSpec(memory_space=pl.ANY)
NN = (((1,), (0,)), ((), ()))
NT = (((1,), (1,)), ((), ()))


def call(kernel, outs, args, smem=0, anywhere=0, free=0, outside=0, scratch=(), aliases=None):
    inside = len(args) - smem - anywhere - free
    spaces = [None] * free + [pltpu.HBM] * anywhere + [pltpu.VMEM] * inside + [pltpu.SMEM] * smem
    args = [arg if space is None else pltpu.with_memory_space_constraint(arg, space) for arg, space in zip(args, spaces)]
    return pl.pallas_call(
        kernel,
        out_shape=outs,
        in_specs=[ANY] * free + [HBM] * anywhere + [VMEM] * inside + [SMEM] * smem,
        out_specs=[HBM if getattr(out, "memory_space", None) is pltpu.HBM else VMEM for out in outs[: len(outs) - outside]]
        + [SMEM] * outside,
        scratch_shapes=scratch,
        input_output_aliases=aliases or {},
        compiler_params=pltpu.CompilerParams(vmem_limit_bytes=16 * 2**20),
    )(*args)


def split(x):
    high = x.astype(BF16)
    return high, (x - high.astype(F32)).astype(BF16)


def dot(a, b, dims=NN):
    return lax.dot_general(a, b, dims, preferred_element_type=F32)


def wide(x):
    return jnp.concatenate(split(x), axis=1)


def tall(x):
    return jnp.concatenate(split(x), axis=0)


def product(left, right):
    size = right.shape[1] // 2
    out = dot(wide(left), jnp.concatenate([right, right], axis=0))
    return out[:, :size] + out[:, size:]


def by_mode(x, modes):
    mode_of = lax.broadcasted_iota(jnp.int32, x.shape, 0) // 2
    spread = jnp.concatenate([jnp.where(mode_of == k, x, 0.0) for k in range(modes)], axis=1)
    return tall(spread)


def folded(out, rows):
    size = out.shape[1] // 2
    return out[:rows, :size] + out[:rows, size:] + out[rows:, :size]


def apply(x, weight, modes):
    return folded(dot(by_mode(x, modes), weight), x.shape[0])


def wave(mode_total, shape, modes, axis=0):
    first = lax.axis_index("mode") * modes
    index = first + lax.broadcasted_iota(jnp.int32, shape, axis) // 2
    number = index.astype(F32) / mode_total
    return 4.0 * number * number


def wave_of(k, mode_total, modes):
    number = (jnp.full((1, 1), lax.axis_index("mode") * modes + k, jnp.int32)).astype(F32) / mode_total
    return 4.0 * number * number


class Weights:
    def __init__(self, size, *entries):
        self.size, self.rows = size, {}
        self.total = 0
        for name, count, rows in entries:
            self.rows[name] = (self.total, rows)
            self.total += count * rows

    def at(self, name, index, mode=None):
        start, rows = self.rows[name]
        if mode is None:
            return pl.ds(start + index * rows, rows)
        return pl.ds(start + index * rows + mode * self.size, self.size)

    def pair(self, ref, name, index):
        return jnp.concatenate([ref[self.at(name, index)], ref[self.at(name, index + 1)]], axis=1)

    def band(self, ref, slab):
        return self.pair(ref, "band", 2 * (slab - 1))

    def face(self, ref, slab, side):
        return self.pair(ref, "face", 4 * slab + 2 * side)


def band_wide(stiff, mass):
    return wide(jnp.concatenate([stiff, mass], axis=1))


def whole(weight):
    size = weight.shape[1] // 2
    value = weight.astype(F32)
    return value[:, :size] + value[:, size:]


def start_copies(pairs, sems):
    copies = [pltpu.make_async_copy(src, dst, sems.at[i]) for i, (src, dst) in enumerate(pairs)]
    for copy in copies:
        copy.start()
    return copies


def transform(rhs_ref, table_ref, out_ref, rhs_buf, table_buf, sems):
    for copy in start_copies([(rhs_ref, rhs_buf), (table_ref, table_buf)], sems):
        copy.wait()
    high, low = split(rhs_buf[...])
    rhs_buf[...] = dot(table_buf[...], jnp.concatenate([high, high, low], axis=0))
    for copy in start_copies([(rhs_buf, out_ref)], sems):
        copy.wait()


def copy_panels(panels_ref, ship_buf, ship_ref, sems, meanwhile):
    fetch = start_copies([(panels_ref.at[:, panels_ref.shape[1] - 1], ship_buf)], sems.at[pl.ds(2, 1)])
    meanwhile()
    fetch[0].wait()
    for copy in start_copies([(ship_buf, ship_ref)], sems.at[pl.ds(2, 1)]):
        copy.wait()


def ends_kernel(
    modes, mode_total, panels_ref, band_ref, rhs_ref, table_ref, ship_ref, out_ref,
    panels_buf, band_buf, ship_buf, rhs_buf, table_buf, sems,
):
    slabs, size = panels_ref.shape[1:3]
    elem, last = lax.axis_index("elem"), lax.axis_size("elem") - 1

    @pl.when(elem == 0)
    def _():
        copy_panels(panels_ref, ship_buf, ship_ref, sems, lambda: transform(rhs_ref, table_ref, out_ref, rhs_buf, table_buf, sems))

    @pl.when(elem == last)
    def _():
        copies = start_copies(
            [(band_ref, band_buf)] + [(panels_ref.at[:, j], panels_buf.at[j]) for j in range(slabs)],
            sems.at[pl.ds(2, slabs + 1)],
        )
        transform(rhs_ref, table_ref, out_ref, rhs_buf, table_buf, sems)
        copies[0].wait()
        band_t = [(band_buf[0, j].T, band_buf[1, j].T) for j in range(slabs)]
        lam = [wave_of(k, mode_total, modes) for k in range(modes)]
        forward = []
        for j in range(slabs):
            copies[1 + j].wait()
            steps = [
                product(panels_buf[j, k], wide(band_buf[0, j] + lam[k] * band_buf[1, j])) for k in range(modes)
            ]
            if j == 0:
                forward.append([-step for step in steps])
            else:
                forward.append([-product(steps[k], wide(forward[-1][k])) for k in range(modes)])
        current = forward[-1]
        for j in range(slabs - 2, -1, -1):
            steps = [
                product(panels_buf[j, k], wide(band_t[j + 1][0] + lam[k] * band_t[j + 1][1])) for k in range(modes)
            ]
            current = [forward[j][k] - product(steps[k], wide(current[k])) for k in range(modes)]
        for k in range(modes):
            ship_buf[k] = product(band_t[0][0] + lam[k] * band_t[0][1], wide(current[k]))
        for copy in start_copies([(ship_buf, ship_ref)], sems):
            copy.wait()


def between_kernel(hub, panels_ref, rhs_ref, table_ref, old_ref, ship_ref, out_ref, ship_buf, rhs_buf, table_buf, sems):
    elem = lax.axis_index("elem")

    @pl.when((elem > 0) & (elem < hub))
    def _():
        copy_panels(panels_ref, ship_buf, ship_ref, sems, lambda: transform(rhs_ref, table_ref, out_ref, rhs_buf, table_buf, sems))


def late_kernel(hub, rhs_ref, table_ref, old_ref, out_ref, rhs_buf, table_buf, sems):
    @pl.when(lax.axis_index("elem") == hub)
    def _():
        transform(rhs_ref, table_ref, out_ref, rhs_buf, table_buf, sems)


def maps_kernel(
    modes, mode_total, hub, place, panels_ref, band_ref, radial_ref, stiff_ref, mass_ref, number_ref, reig_ref, axial_ref, aeig_ref,
    coup_ref, front_ref, back_ref, w_ref, reig_out, axial_out, weight_out, aeig_out,
    panels_buf, band_buf, radial_buf, stiff_buf, mass_buf, number_buf, axial_buf, coup_buf, front_buf, back_buf, sems,
):
    slabs, size = panels_ref.shape[1:3]
    inner = aeig_ref.shape[1]
    copies = start_copies(
        [(radial_ref, radial_buf), (stiff_ref, stiff_buf), (mass_ref, mass_buf), (number_ref, number_buf), (band_ref, band_buf)]
        + [(panels_ref.at[:, j], panels_buf.at[j]) for j in range(slabs)]
        + [(axial_ref, axial_buf), (coup_ref, coup_buf), (aeig_ref, aeig_out), (reig_ref, reig_out)],
        sems,
    )
    for copy in copies[:4]:
        copy.wait()
    for j in range(slabs):
        radial = wide(radial_buf[j])
        w_ref[place.at("radial", j)] = radial
        parts = [wide(product(ref[j].T, radial)) for ref in (stiff_buf, mass_buf)]
        for side in range(2):
            spot = lax.broadcasted_iota(jnp.int32, (size, size), 0)
            onehot = jnp.where(number_buf[j, side : side + 1] == spot, 1.0, 0.0).astype(BF16)
            for i in range(2):
                both = jnp.concatenate([p[:, i * size : (i + 1) * size] for p in parts], axis=1)
                w_ref[place.at("face", 4 * j + 2 * side + i)] = dot(onehot, both).astype(BF16)
    copies[4].wait()
    for j in range(1, slabs):
        bands = band_wide(band_buf[0, j], band_buf[1, j])
        for i in range(2):
            w_ref[place.at("band", 2 * (j - 1) + i)] = bands[:, 2 * i * size : 2 * (i + 1) * size]
    for j in range(slabs):
        copies[5 + j].wait()
        for k in range(modes):
            w_ref[place.at("panel", j, k)] = wide(panels_buf[j, k].T)
    for copy in copies[5 + slabs :]:
        copy.wait()
    for j in range(slabs):
        for b in range(inner):
            for a in range(inner):
                axial_out[j, a, b] = axial_buf[j, a, b]
            for side in range(2):
                weight = coup_buf[j, side, 0] * axial_buf[j, 0, b]
                for a in range(1, inner):
                    weight = weight + coup_buf[j, side, a] * axial_buf[j, a, b]
                weight_out[j, side, b] = weight

    @pl.when((lax.axis_index("elem") > 0) & (lax.axis_index("elem") <= hub))
    def _():
        lam = [wave_of(k, mode_total, modes) for k in range(modes)]
        current = None
        for j in range(slabs):
            first, second = band_buf[0, j].T, band_buf[1, j].T
            steps = [product(first + lam[k] * second, w_ref[place.at("panel", j, k)]) for k in range(modes)]
            if current is None:
                current = [-step for step in steps]
            else:
                current = [-product(current[k], wide(steps[k])) for k in range(modes)]
        for k in range(modes):
            front_buf[pl.ds(k * size, size)] = wide(current[k])
        start_copies([(front_buf, front_ref)], sems.at[pl.ds(1, 1)])

        @pl.when(lax.axis_index("elem") <= hub)
        def _():
            current = [-whole(w_ref[place.at("panel", slabs - 1, k)]) for k in range(modes)]
            for j in range(slabs - 2, -1, -1):
                steps = [
                    product(band_buf[0, j + 1] + lam[k] * band_buf[1, j + 1], w_ref[place.at("panel", j, k)]) for k in range(modes)
                ]
                current = [-product(current[k], wide(steps[k])) for k in range(modes)]
            for k in range(modes):
                back_buf[pl.ds(k * size, size)] = wide(product(current[k], wide(band_buf[0, 0] + lam[k] * band_buf[1, 0])))
            for copy in start_copies([(back_buf, back_ref)], sems):
                copy.wait()

        pltpu.make_async_copy(front_buf, front_ref, sems.at[1]).wait()


def face_push(values, weight, lam):
    rows, size = values.shape
    high, low = split(values)
    blocks = [weight[:, i * size : (i + 1) * size] for i in range(4)]
    out = dot(
        jnp.concatenate([high, low], axis=0), jnp.concatenate(blocks, axis=0), NT
    )
    out = out[:rows, : 2 * size] + out[:rows, 2 * size :] + out[rows:, : 2 * size]
    return out[:, :size] + lam * out[:, size:]


def face_lift(values, weight, lam):
    rows, size = values.shape
    out = folded(dot(tall(values), weight), rows)
    return out[:, :size] + lam * out[:, size:]


def block_of(spec_ref, index, size):
    per = spec_ref.shape[2] // size
    at = index % per * size
    return spec_ref[index // per, :, at : at + size]


def band_step(values, weight, lam):
    return face_push(values, weight, lam)


def inner_kernel(modes, mode_total, place, hub, first_call, band_ref, front_ref, *refs):
    elem = lax.axis_index("elem")
    if first_call:
        spec_ref, w_ref, reig_ref, axial_ref, weight_ref, aeig_ref, zsrc_ref, inv_ref, reduced_ref, y_ref, send_ref = refs
    else:
        spec_ref, w_ref, reig_ref = refs[:3]
        axial_ref, weight_ref, aeig_ref, zsrc_ref, inv_ref, reduced_ref, y_ref, load_ref, front_out, band_buf, sems = refs[7:]
        inside = (elem > 0) & (elem <= hub)
        early = (front_ref, front_out)
        late = (band_ref.at[:, 0], band_buf)

        @pl.when(inside)
        def _():
            start_copies([early], sems.at[pl.ds(1, 1)])

        @pl.when(elem == lax.axis_size("elem") - 1)
        def _():
            start_copies([late], sems)

    @pl.when((elem == 0) == first_call)
    def _():
        load, values = inner_part(
            modes, mode_total, place, spec_ref, w_ref, reig_ref, axial_ref, weight_ref, aeig_ref, zsrc_ref, inv_ref, reduced_ref, y_ref
        )
        if first_call:
            send_ref[...] = values[-1]
            return
        load_ref[1] = load

        @pl.when(inside)
        def _():
            pltpu.make_async_copy(*early, sems.at[1]).wait()

        @pl.when(elem == lax.axis_size("elem") - 1)
        def _():
            lam = wave(mode_total, load.shape, modes)
            current = values[-1]
            for j in range(len(values) - 2, -1, -1):
                step = face_lift(current, place.band(w_ref, j + 1), lam)
                current = values[j] - apply(step, w_ref[place.at("panel", j)], modes)
            pltpu.make_async_copy(*late, sems.at[0]).wait()
            load_ref[0] = load + face_lift(current, band_wide(band_buf[0], band_buf[1]), lam)


def inner_part(
    modes, mode_total, place, spec_ref, w_ref, reig_ref, axial_ref, weight_ref, aeig_ref, zsrc_ref, inv_ref, solved_ref, y_ref
):
    slabs, inner, rows, size = zsrc_ref.shape
    lam = wave(mode_total, (rows, size), modes)
    pushed = []
    for j in range(slabs):
        source = jnp.concatenate(
            [block_of(spec_ref, j * (inner + 1) + a, size) for a in range(inner)], axis=0
        )
        first = product(source, w_ref[place.at("radial", j)])
        first = [first[a * rows : (a + 1) * rows] for a in range(inner)]
        sums = [None, None]
        for b in range(inner):
            value = first[0] * axial_ref[j, 0, b]
            for a in range(1, inner):
                value = value + first[a] * axial_ref[j, a, b]
            inverse = 1.0 / (aeig_ref[j, b] + reig_ref[j : j + 1] + lam)
            inv_ref[j, b] = inverse
            value = value * inverse
            zsrc_ref[j, b] = value
            for side in range(2):
                term = value * weight_ref[j, side, b]
                sums[side] = term if sums[side] is None else sums[side] + term
        pushed.append([face_push(sums[side], place.face(w_ref, j, side), lam) for side in range(2)])
    load = pushed[0][0]
    values = []
    for j in range(slabs):
        reduced = block_of(spec_ref, j * (inner + 1) + inner, size) - pushed[j][1]
        if j + 1 < slabs:
            reduced = reduced - pushed[j + 1][0]
        panel = w_ref[place.at("panel", j)]
        solved_ref[j] = reduced
        if j > 0:
            reduced = reduced - band_step(values[-1], place.band(w_ref, j), lam)
        values.append(apply(reduced, panel, modes))
        y_ref[j] = values[j]
    return load, values


def previous_weight(panel_ref, modes):
    parts = [split(panel_ref[k]) for k in range(modes)]
    return jnp.concatenate(
        [jnp.concatenate([p[i] for p in parts], axis=1) for i in range(2)], axis=0
    )


def apply_nt(x, weight, modes):
    return folded(dot(by_mode(x, modes), weight, NT), x.shape[0])


def backward_values(values, after, panel, behind_ref, modes):
    slabs = len(values)
    out = [None] * slabs
    out[-1] = values[-1]
    if after is not None:
        out[-1] = out[-1] - apply(after, panel, modes)
    for j in range(slabs - 2, -1, -1):
        out[j] = values[j] - apply(out[j + 1], behind_ref[j], modes)
    return out


def push_kernel(modes, first_ref, load_ref, prev_ref, push_ref, prev_buf, sems):
    @pl.when(lax.axis_index("elem") == 1)
    def _():
        for copy in start_copies([(first_ref, prev_buf)], sems):
            copy.wait()
        weight = previous_weight(prev_buf, modes)
        prev_ref[...] = weight
        push_ref[...] = apply_nt(load_ref[1], weight, modes)


def forward_kernel(modes, at, got_ref, push_ref, y_ref, front_ref, old_ref, state_ref, send_ref):
    @pl.when(lax.axis_index("elem") == at)
    def _():
        before = got_ref[...] - push_ref[...]
        state_ref[0] = before
        send_ref[...] = y_ref[y_ref.shape[0] - 1] + apply(before, front_ref[...], modes)


def base_kernel(
    modes, mode_total, hub, place, band_ref, map_ref, state_ref, load_ref, reduced_ref, y_ref, w_ref,
    base_ref, found_ref, back_ref, band_buf, sems,
):
    elem = lax.axis_index("elem")
    slabs, rows, size = reduced_ref.shape
    lam = wave(mode_total, (rows, size), modes)

    @pl.when((elem > 0) & (elem < hub))
    def _():
        copies = start_copies([(band_ref.at[:, 0], band_buf), (map_ref, back_ref)], sems)
        copies[0].wait()
        first = band_wide(band_buf[0], band_buf[1])
        bands = [first] + [place.band(w_ref, j) for j in range(1, slabs)]
        panels = [w_ref[place.at("panel", j)] for j in range(slabs)]
        values = []
        for j in range(slabs):
            step = face_push(values[-1] if j > 0 else state_ref[0], bands[j], lam)
            values.append(apply(reduced_ref[j] - step, panels[j], modes))
        found = values[-1]
        found_ref[slabs - 1] = found
        for j in range(slabs - 2, -1, -1):
            found = values[j] - apply(face_lift(found, bands[j + 1], lam), panels[j], modes)
            found_ref[j] = found
        base_ref[...] = load_ref[1] + face_lift(found, first, lam)
        copies[1].wait()


def ahead_maps(ahead_ref, band_buf, waves, w_ref, place):
    slabs, many, _ = ahead_ref.shape
    for j in range(slabs):
        first, second = band_buf[0, j].T, band_buf[1, j].T
        for k, lam in enumerate(waves):
            ahead_ref[j, pl.ds(k * place.size, place.size)] = wide(product(first + lam * second, w_ref[place.at("panel", j, k)]))


def behind_maps(behind_ref, band_buf, waves, w_ref, place):
    for j in range(behind_ref.shape[0]):
        for k, lam in enumerate(waves):
            step = product(band_buf[0, j + 1] + lam * band_buf[1, j + 1], w_ref[place.at("panel", j, k)])
            behind_ref[j, pl.ds(k * place.size, place.size)] = wide(step)


def hub_map_kernel(
    modes, mode_total, hub, place, map_ref, pprev_ref, band_ref, given_ref, load_ref, y_ref, w_ref, front_ref, old_prev_ref, old_push_ref,
    prev_ref, push_ref, ahead_ref, behind_ref, back_ref, base_ref, cross_ref, far_ref, band_buf, map_buf, prev_buf, sems,
):
    slabs, rows, size = y_ref.shape
    lam = wave(mode_total, (rows, size), modes)
    inside = (lax.axis_index("elem") > 1) & (lax.axis_index("elem") <= hub)

    @pl.when(inside)
    def _():
        start_copies([(pprev_ref, prev_buf)], sems.at[pl.ds(2, 1)])

    @pl.when(lax.axis_index("elem") == hub)
    def _():
        copies = start_copies([(band_ref, band_buf), (map_ref, map_buf)], sems)
        given = start_copies([(given_ref, back_ref)], sems.at[pl.ds(3, 1)])[0]
        waves = [wave_of(k, mode_total, modes) for k in range(modes)]

        def part(k):
            return pl.ds(k * size, size)

        copies[0].wait()
        ahead_maps(ahead_ref, band_buf, waves, w_ref, place)
        behind_maps(behind_ref, band_buf, waves, w_ref, place)
        entry = [wide(band_buf[0, 0] + waves[k] * band_buf[1, 0]) for k in range(modes)]
        forward = [[-whole(ahead_ref[0, part(k)]) for k in range(modes)]]
        for j in range(1, slabs - 1):
            forward.append([-product(forward[-1][k], ahead_ref[j, part(k)]) for k in range(modes)])
        cross = [whole(front_ref[part(k)]) for k in range(modes)]
        for j in range(slabs - 2, -1, -1):
            cross = [forward[j][k] - product(cross[k], behind_ref[j, part(k)]) for k in range(modes)]
        for k in range(modes):
            cross_ref[part(k)] = wide(product(cross[k], entry[k]))
        found = backward_values([y_ref[j] for j in range(slabs)], None, None, behind_ref, modes)
        base_ref[...] = load_ref[1] + face_lift(found[0], band_wide(band_buf[0, 0], band_buf[1, 0]), lam)
        copies[1].wait()
        far_ref[...] = previous_weight(map_buf, modes)
        given.wait()

    @pl.when(inside)
    def _():
        pltpu.make_async_copy(pprev_ref, prev_buf, sems.at[2]).wait()
        weight = previous_weight(prev_buf, modes)
        prev_ref[...] = weight
        push_ref[...] = apply_nt(load_ref[1], weight, modes)


def hub_kernel(
    modes, at, place, got_ref, push_ref, far_ref, far_weight_ref, y_ref, front_ref, back_ref, cross_ref, base_ref, w_ref, old_ref,
    state_ref, send_ref, last_ref,
):
    slabs = y_ref.shape[0]

    @pl.when(lax.axis_index("elem") == at)
    def _():
        panel = w_ref[place.at("panel", slabs - 1)]
        load = apply(far_ref[1], panel, modes)
        before = got_ref[...] - push_ref[...]
        state_ref[0] = before
        value = y_ref[slabs - 1] + apply(before, front_ref[...], modes)
        out = base_ref[...] + apply(before, cross_ref[...], modes)
        final = value - load
        after = far_ref[0] + apply_nt(final, far_weight_ref[...], modes)
        state_ref[1] = after
        send_ref[...] = out + apply(after, back_ref[...], modes)
        last_ref[0] = final
        last_ref[1] = value - apply(after, panel, modes)


def own_map_kernel(
    modes, mode_total, hub, place, band_ref, radial_ref, state_ref, reduced_ref, y_ref, w_ref, prev_ref, ahead_ref, behind_ref, old_ref,
    found_ref, own_ref, before_ref, radt_ref, ahead_buf, behind_buf, band_buf, radial_buf, sems,
):
    slabs, rows, size = reduced_ref.shape
    elem, last = lax.axis_index("elem"), lax.axis_size("elem") - 1
    lam = wave(mode_total, (rows, size), modes)
    waves = [wave_of(k, mode_total, modes) for k in range(modes)]
    copies = start_copies([(band_ref, band_buf), (radial_ref, radial_buf)], sems)

    def part(k):
        return pl.ds(k * size, size)

    copies[0].wait()

    @pl.when(elem == hub)
    def _():
        panels = [w_ref[place.at("panel", j)] for j in range(slabs)]
        before, values = state_ref[0], []
        for j in range(slabs):
            solved = apply(reduced_ref[j], panels[j], modes)
            values.append(solved - apply(values[-1] if j > 0 else before, ahead_ref[j], modes))
        found = backward_values(values, state_ref[1], panels[-1], behind_ref, modes)
        for j in range(slabs):
            found_ref[j] = found[j]
        back = face_lift(found[0], band_wide(band_buf[0, 0], band_buf[1, 0]), lam)
        before_ref[...] = before - apply_nt(back, prev_ref[...], modes)

    @pl.when(elem != hub)
    def _():
        behind_maps(behind_buf, band_buf, waves, w_ref, place)

    @pl.when(elem < hub)
    def _():
        current = [-whole(w_ref[place.at("panel", slabs - 1, k)]) for k in range(modes)]
        for k in range(modes):
            own_ref[slabs - 1, part(k)] = -w_ref[place.at("panel", slabs - 1, k)]
        for j in range(slabs - 2, -1, -1):
            current = [-product(current[k], behind_buf[j, part(k)]) for k in range(modes)]
            for k in range(modes):
                own_ref[j, part(k)] = wide(current[k])

    @pl.when(elem == last)
    def _():
        ahead_maps(ahead_buf, band_buf, waves, w_ref, place)
        forward = [[-whole(ahead_buf[0, part(k)]) for k in range(modes)]]
        for j in range(1, slabs):
            forward.append([-product(forward[-1][k], ahead_buf[j, part(k)]) for k in range(modes)])
        current = forward[-1]
        for k in range(modes):
            own_ref[slabs - 1, part(k)] = wide(current[k])
        for j in range(slabs - 2, -1, -1):
            current = [forward[j][k] - product(current[k], behind_buf[j, part(k)]) for k in range(modes)]
            for k in range(modes):
                own_ref[j, part(k)] = wide(current[k])

    @pl.when((elem == 0) | (elem == last))
    def _():
        found = backward_values([y_ref[j] for j in range(slabs)], None, None, behind_buf, modes)
        for j in range(slabs):
            found_ref[j] = found[j]

    copies[1].wait()
    for j in range(slabs):
        radt_ref[j] = wide(radial_buf[j].T)


def backward_kernel(modes, at, got_ref, base_ref, back_ref, old_ref, state_ref, send_ref):
    @pl.when(lax.axis_index("elem") == at)
    def _():
        after = got_ref[...]
        state_ref[1] = after
        send_ref[...] = base_ref[...] + apply(after, back_ref[...], modes)


def final_kernel(
    modes, mode_total, hub, place, zsrc_ref, inv_ref, state_ref, got_ref, base_ref, last_ref, load_ref, found_ref, own_ref, back_ref, before_ref, prev_ref, w_ref, radt_ref, axial_ref, weight_ref,
    out_ref, x_ref, out_buf, sems,
):
    slabs, inner, rows, size = zsrc_ref.shape
    lam = wave(mode_total, (rows, size), modes)
    elem, last = lax.axis_index("elem"), lax.axis_size("elem") - 1

    def values(given):
        for j in range(slabs):
            x_ref[j + 1] = found_ref[j] + apply(given, own_ref[j], modes)

    @pl.when(elem == 0)
    def _():
        x_ref[0] = jnp.zeros((rows, size), F32)
        values(got_ref[...])

    @pl.when((elem > 0) & (elem < hub))
    def _():
        after = state_ref[1]
        values(after)
        back = base_ref[...] - load_ref[1] + apply(after, back_ref[...], modes)
        x_ref[0] = state_ref[0] - apply_nt(back, prev_ref[...], modes)

    @pl.when(elem == hub)
    def _():
        for j in range(slabs):
            x_ref[j + 1] = found_ref[j]
        x_ref[0] = before_ref[...]

    @pl.when(elem == last)
    def _():
        values(last_ref[0])
        x_ref[0] = last_ref[1]

    copies = []
    for j in range(slabs):
        lifted = [face_lift(x_ref[j + side], place.face(w_ref, j, side), lam) for side in range(2)]
        kept = []
        for b in range(inner):
            total = lifted[0] * weight_ref[j, 0, b] + lifted[1] * weight_ref[j, 1, b]
            kept.append(zsrc_ref[j, b] - total * inv_ref[j, b])
        values = []
        for a in range(inner):
            value = kept[0] * axial_ref[j, a, 0]
            for b in range(1, inner):
                value = value + kept[b] * axial_ref[j, a, b]
            values.append(value)
        result = product(jnp.concatenate(values, axis=0), radt_ref[j])
        for a in range(inner):
            out_buf[j, :, a * size : (a + 1) * size] = result[a * rows : (a + 1) * rows]
        out_buf[j, :, inner * size :] = x_ref[j + 1]
        width = (inner + 1) * size
        copies += start_copies([(out_buf.at[j], out_ref.at[:, pl.ds(j * width, width)])], sems.at[pl.ds(j, 1)])
    for copy in copies:
        copy.wait()


def dft_table(planes):
    row, col = np.arange(planes)[:, None], np.arange(planes)[None]
    angle = row // 2 * col % planes * (2.0 * math.pi / planes)
    table = np.where(row % 2 == 0, np.cos(angle), -np.sin(angle)) / math.sqrt(planes)
    table = jnp.asarray(table, F32)
    high, low = split(table)
    return jnp.concatenate([high, low, high], axis=1)


def body(
    rhs_phys, radial_basis, axial_basis, radial_eig, axial_eig, face_stiff, face_mass, axial_coupling, face_numbering,
    band_panels, inverse_panels,
):
    planes, nodes = rhs_phys.shape
    modes, slabs, size, _ = inverse_panels.shape
    inner = axial_basis.shape[1]
    devices = lax.axis_size("mode")
    elems = lax.axis_size("elem")
    mode_total = modes * devices
    rows = 2 * modes
    hub = elems - 2
    last = elems - 1

    def shape(*dims):
        return jax.ShapeDtypeStruct(dims, F32)

    def kept(*dims):
        return pltpu.VMEM(dims, F32)

    def half(*dims):
        return pltpu.VMEM(dims, BF16)

    table = dft_table(planes)
    many = modes * size
    place = Weights(size, ("panel", slabs, many), ("radial", slabs, size), ("face", 4 * slabs, size), ("band", 2 * (slabs - 1), size))
    buffers = [pltpu.VMEM((planes, nodes), F32), pltpu.VMEM(table.shape, BF16), pltpu.SemaphoreType.DMA((slabs + 3,))]
    whole_spectrum = pltpu.HBM((planes, nodes), F32)
    whole_panels = pltpu.HBM((modes, size, size), F32)
    panels_buffer = pltpu.VMEM((modes, size, size), F32)
    ship, spectrum = call(
        functools.partial(ends_kernel, modes, mode_total),
        [whole_panels, whole_spectrum],
        [inverse_panels, band_panels, rhs_phys, table],
        anywhere=4,
        scratch=[pltpu.VMEM((slabs, modes, size, size), F32), pltpu.VMEM(band_panels.shape, F32), panels_buffer] + buffers,
    )
    if hub > 1:
        first = far_map = lax.ppermute(ship, "elem", [(0, 1), (last, hub)])
    else:
        first, far_map = lax.ppermute(ship, "elem", [(0, 1)]), lax.ppermute(ship, "elem", [(last, hub)])
    ship, spectrum = call(
        functools.partial(between_kernel, hub),
        [whole_panels, whole_spectrum],
        [inverse_panels, rhs_phys, table, spectrum],
        anywhere=4,
        scratch=[panels_buffer] + buffers,
        aliases={3: 1},
    )
    pprev = lax.ppermute(ship, "elem", [(i, i + 1) for i in range(1, hub)]) if hub > 1 else first
    spectrum = call(
        functools.partial(late_kernel, hub),
        [whole_spectrum],
        [rhs_phys, table, spectrum],
        anywhere=3,
        scratch=buffers,
        aliases={2: 0},
    )[0]
    spectrum = lax.all_to_all(spectrum.reshape(devices, rows, nodes), "mode", 0, 0, tiled=False)
    if nodes % size:
        spectrum = jnp.swapaxes(spectrum, 0, 1).reshape(1, rows, devices * nodes)
    vector = (rows, size)
    matrix = half(many, 2 * size)
    front, back_map, w, reig, axial, weight, aeig = call(
        functools.partial(maps_kernel, modes, mode_total, hub, place),
        [
            pltpu.HBM((many, 2 * size), BF16),
            pltpu.HBM((many, 2 * size), BF16),
            half(place.total, 2 * size),
            kept(*radial_eig.shape),
            pltpu.SMEM(axial_basis.shape, F32),
            pltpu.SMEM((slabs, 2, inner), F32),
            pltpu.SMEM(axial_eig.shape, F32),
        ],
        [
            inverse_panels, band_panels, radial_basis, face_stiff, face_mass, face_numbering,
            radial_eig, axial_basis, axial_eig, axial_coupling,
        ],
        anywhere=10,
        outside=3,
        scratch=[
            pltpu.VMEM((slabs, modes, size, size), F32),
            pltpu.VMEM(band_panels.shape, F32),
            pltpu.VMEM(radial_basis.shape, F32),
            pltpu.VMEM(face_stiff.shape, F32),
            pltpu.VMEM(face_mass.shape, F32),
            pltpu.VMEM(face_numbering.shape, jnp.int32),
            pltpu.SMEM(axial_basis.shape, F32),
            pltpu.SMEM(axial_coupling.shape, F32),
            pltpu.VMEM((many, 2 * size), BF16),
            pltpu.VMEM((many, 2 * size), BF16),
            pltpu.SemaphoreType.DMA((slabs + 9,)),
        ],
    )
    solves = [kept(slabs, inner, *vector), kept(slabs, inner, *vector), kept(slabs, *vector), kept(slabs, *vector)]
    *solve, send = call(
        functools.partial(inner_kernel, modes, mode_total, place, hub, True),
        solves + [kept(*vector)],
        [band_panels, front, spectrum, w, reig, axial, weight, aeig],
        anywhere=2,
        smem=3,
    )
    got = lax.ppermute(send, "elem", [(0, 1)])
    zsrc, inv, reduced, y, load, front = call(
        functools.partial(inner_kernel, modes, mode_total, place, hub, False),
        solves + [kept(2, *vector), matrix],
        [band_panels, front, spectrum, w, reig, *solve, axial, weight, aeig],
        anywhere=2,
        smem=3,
        scratch=[
            pltpu.VMEM((2, size, size), F32),
            pltpu.SemaphoreType.DMA((2,)),
        ],
        aliases={5 + i: i for i in range(4)},
    )
    far = lax.ppermute(load, "elem", [(last, hub)])
    prev, push = call(
        functools.partial(push_kernel, modes),
        [half(2 * size, many), kept(*vector)],
        [first, load],
        free=1,
        scratch=[panels_buffer, pltpu.SemaphoreType.DMA((1,))],
    )
    prev, later_push, ahead, behind, hub_back, hub_base, cross, far_weight = call(
        functools.partial(hub_map_kernel, modes, mode_total, hub, place),
        [
            half(2 * size, many), kept(*vector), half(slabs, many, 2 * size), half(slabs - 1, many, 2 * size), matrix,
            kept(*vector), matrix, half(2 * size, many),
        ],
        [far_map, pprev, band_panels, back_map, load, y, w, front, prev, push],
        free=2,
        anywhere=2,
        scratch=[pltpu.VMEM(band_panels.shape, F32), panels_buffer, panels_buffer, pltpu.SemaphoreType.DMA((4,))],
        aliases={8: 0, 9: 1},
    )
    state = jnp.zeros((2, *vector), F32)
    for at in range(1, hub):
        state, send = call(
            functools.partial(forward_kernel, modes, at),
            [kept(*state.shape), shape(*vector)],
            [got, push if at == 1 else later_push, y, front, state],
            aliases={4: 0},
        )
        got = lax.ppermute(send, "elem", [(at, at + 1)])
    state, send, final = call(
        functools.partial(hub_kernel, modes, hub, place),
        [kept(*state.shape), shape(*vector), shape(2, *vector)],
        [got, push if hub == 1 else later_push, far, far_weight, y, front, hub_back, cross, hub_base, w, state],
        aliases={10: 0},
    )
    base, found, back = call(
        functools.partial(base_kernel, modes, mode_total, hub, place),
        [kept(*vector), kept(slabs, *vector), matrix],
        [band_panels, back_map, state, load, reduced, y, w],
        anywhere=2,
        scratch=[pltpu.VMEM((2, size, size), F32), pltpu.SemaphoreType.DMA((2,))],
    )
    for at in range(hub - 1, 0, -1):
        got = lax.ppermute(send, "elem", [(at + 1, at)])
        state, send = call(
            functools.partial(backward_kernel, modes, at),
            [kept(*state.shape), shape(*vector)],
            [got, base, back, state],
            aliases={3: 0},
        )
    got = lax.ppermute(send, "elem", [(1, 0)])
    found, own, before, radt = call(
        functools.partial(own_map_kernel, modes, mode_total, hub, place),
        [kept(slabs, *vector), half(slabs, many, 2 * size), kept(*vector), half(slabs, size, 2 * size)],
        [band_panels, radial_basis, state, reduced, y, w, prev, ahead, behind, found],
        anywhere=2,
        scratch=[
            pltpu.VMEM((slabs, many, 2 * size), BF16),
            pltpu.VMEM((slabs - 1, many, 2 * size), BF16),
            pltpu.VMEM(band_panels.shape, F32),
            pltpu.VMEM(radial_basis.shape, F32),
            pltpu.SemaphoreType.DMA((2,)),
        ],
        aliases={9: 0},
    )
    final = lax.ppermute(final, "elem", [(hub, last)])
    return call(
        functools.partial(final_kernel, modes, mode_total, hub, place),
        [pltpu.HBM((rows, slabs * (inner + 1) * size), F32)],
        [
            zsrc, inv, state, got, base, final, load, found, own, back, before, prev, w, radt, axial, weight,
        ],
        smem=2,
        scratch=[
            pltpu.VMEM((slabs + 1, *vector), F32),
            pltpu.VMEM((slabs, rows, (inner + 1) * size), F32),
            pltpu.SemaphoreType.DMA((slabs,)),
        ],
    )[0]


def solution(mesh):
    placed = (
        P(None, ("elem", "mode")),
        P("elem", None, None),
        P("elem", None, None),
        P("elem", None),
        P("elem", None),
        P("elem", None, None),
        P("elem", None, None),
        P("elem", None, None),
        P("elem", None, None),
        P(None, "elem", None, None),
        P("mode", "elem", None, None),
    )
    return jax.shard_map(
        body, mesh=mesh, in_specs=placed, out_specs=P("mode", "elem"), check_vma=False
    )
```

```python
import functools
import math

import jax
import jax.numpy as jnp
import numpy as np
from jax import lax
from jax.experimental import pallas as pl
from jax.experimental.pallas import tpu as pltpu
from jax.sharding import PartitionSpec as P

F32 = jnp.float32
BF16 = jnp.bfloat16
VMEM = pl.BlockSpec(memory_space=pltpu.VMEM)
SMEM = pl.BlockSpec(memory_space=pltpu.SMEM)
HBM = pl.BlockSpec(memory_space=pltpu.HBM)
ANY = pl.BlockSpec(memory_space=pl.ANY)
NN = (((1,), (0,)), ((), ()))
NT = (((1,), (1,)), ((), ()))


def call(kernel, outs, args, smem=0, anywhere=0, free=0, outside=0, scratch=(), aliases=None):
    inside = len(args) - smem - anywhere - free
    spaces = [None] * free + [pltpu.HBM] * anywhere + [pltpu.VMEM] * inside + [pltpu.SMEM] * smem
    args = [arg if space is None else pltpu.with_memory_space_constraint(arg, space) for arg, space in zip(args, spaces)]
    return pl.pallas_call(
        kernel,
        out_shape=outs,
        in_specs=[ANY] * free + [HBM] * anywhere + [VMEM] * inside + [SMEM] * smem,
        out_specs=[HBM if getattr(out, "memory_space", None) is pltpu.HBM else VMEM for out in outs[: len(outs) - outside]]
        + [SMEM] * outside,
        scratch_shapes=scratch,
        input_output_aliases=aliases or {},
        compiler_params=pltpu.CompilerParams(vmem_limit_bytes=16 * 2**20),
    )(*args)


def split(x):
    high = x.astype(BF16)
    return high, (x - high.astype(F32)).astype(BF16)


def dot(a, b, dims=NN):
    return lax.dot_general(a, b, dims, preferred_element_type=F32)


def wide(x):
    return jnp.concatenate(split(x), axis=1)


def tall(x):
    return jnp.concatenate(split(x), axis=0)


def product(left, right):
    size = right.shape[1] // 2
    out = dot(wide(left), jnp.concatenate([right, right], axis=0))
    return out[:, :size] + out[:, size:]


def by_mode(x, modes):
    mode_of = lax.broadcasted_iota(jnp.int32, x.shape, 0) // 2
    spread = jnp.concatenate([jnp.where(mode_of == k, x, 0.0) for k in range(modes)], axis=1)
    return tall(spread)


def folded(out, rows):
    size = out.shape[1] // 2
    return out[:rows, :size] + out[:rows, size:] + out[rows:, :size]


def apply(x, weight, modes):
    return folded(dot(by_mode(x, modes), weight), x.shape[0])


def wave(mode_total, shape, modes, axis=0):
    first = lax.axis_index("mode") * modes
    index = first + lax.broadcasted_iota(jnp.int32, shape, axis) // 2
    number = index.astype(F32) / mode_total
    return 4.0 * number * number


def wave_of(k, mode_total, modes):
    number = (jnp.full((1, 1), lax.axis_index("mode") * modes + k, jnp.int32)).astype(F32) / mode_total
    return 4.0 * number * number


class Weights:
    def __init__(self, size, *entries):
        self.size, self.rows = size, {}
        self.total = 0
        for name, count, rows in entries:
            self.rows[name] = (self.total, rows)
            self.total += count * rows

    def at(self, name, index, mode=None):
        start, rows = self.rows[name]
        if mode is None:
            return pl.ds(start + index * rows, rows)
        return pl.ds(start + index * rows + mode * self.size, self.size)

    def pair(self, ref, name, index):
        return jnp.concatenate([ref[self.at(name, index)], ref[self.at(name, index + 1)]], axis=1)

    def band(self, ref, slab):
        return self.pair(ref, "band", 2 * (slab - 1))

    def face(self, ref, slab, side):
        return self.pair(ref, "face", 4 * slab + 2 * side)


def band_wide(stiff, mass):
    return wide(jnp.concatenate([stiff, mass], axis=1))


def whole(weight):
    size = weight.shape[1] // 2
    value = weight.astype(F32)
    return value[:, :size] + value[:, size:]


def start_copies(pairs, sems):
    copies = [pltpu.make_async_copy(src, dst, sems.at[i]) for i, (src, dst) in enumerate(pairs)]
    for copy in copies:
        copy.start()
    return copies


def transform(rhs_ref, table_ref, out_ref, rhs_buf, table_buf, sems):
    for copy in start_copies([(rhs_ref, rhs_buf), (table_ref, table_buf)], sems):
        copy.wait()
    high, low = split(rhs_buf[...])
    rhs_buf[...] = dot(table_buf[...], jnp.concatenate([high, high, low], axis=0))
    return start_copies([(rhs_buf, out_ref)], sems)[0]


def panels_and_transform(panels_ref, ship_ref, rhs_ref, table_ref, out_ref, ship_buf, rhs_buf, table_buf, sems):
    fetch = start_copies([(panels_ref.at[:, panels_ref.shape[1] - 1], ship_buf)], sems.at[pl.ds(2, 1)])[0]
    result = transform(rhs_ref, table_ref, out_ref, rhs_buf, table_buf, sems)
    fetch.wait()
    ship = start_copies([(ship_buf, ship_ref)], sems.at[pl.ds(2, 1)])[0]
    result.wait()
    ship.wait()


def ends_kernel(
    modes, mode_total, panels_ref, band_ref, rhs_ref, table_ref, ship_ref, out_ref,
    panels_buf, band_buf, ship_buf, rhs_buf, table_buf, sems,
):
    slabs, size = panels_ref.shape[1:3]
    elem, last = lax.axis_index("elem"), lax.axis_size("elem") - 1

    @pl.when(elem == 0)
    def _():
        panels_and_transform(panels_ref, ship_ref, rhs_ref, table_ref, out_ref, ship_buf, rhs_buf, table_buf, sems)

    @pl.when(elem == last)
    def _():
        copies = start_copies(
            [(band_ref, band_buf)] + [(panels_ref.at[:, j], panels_buf.at[j]) for j in range(slabs)],
            sems.at[pl.ds(2, slabs + 1)],
        )
        result = transform(rhs_ref, table_ref, out_ref, rhs_buf, table_buf, sems)
        copies[0].wait()
        band_t = [(band_buf[0, j].T, band_buf[1, j].T) for j in range(slabs)]
        lam = [wave_of(k, mode_total, modes) for k in range(modes)]
        forward = []
        for j in range(slabs):
            copies[1 + j].wait()
            steps = [
                product(panels_buf[j, k], wide(band_buf[0, j] + lam[k] * band_buf[1, j])) for k in range(modes)
            ]
            if j == 0:
                forward.append([-step for step in steps])
            else:
                forward.append([-product(steps[k], wide(forward[-1][k])) for k in range(modes)])
        current = forward[-1]
        for j in range(slabs - 2, -1, -1):
            steps = [
                product(panels_buf[j, k], wide(band_t[j + 1][0] + lam[k] * band_t[j + 1][1])) for k in range(modes)
            ]
            current = [forward[j][k] - product(steps[k], wide(current[k])) for k in range(modes)]
        for k in range(modes):
            ship_buf[k] = product(band_t[0][0] + lam[k] * band_t[0][1], wide(current[k]))
        for copy in start_copies([(ship_buf, ship_ref)], sems.at[pl.ds(1, 1)]):
            copy.wait()
        result.wait()


def between_kernel(hub, panels_ref, rhs_ref, table_ref, old_ref, ship_ref, out_ref, ship_buf, rhs_buf, table_buf, sems):
    elem = lax.axis_index("elem")

    @pl.when((elem > 0) & (elem < hub))
    def _():
        panels_and_transform(panels_ref, ship_ref, rhs_ref, table_ref, out_ref, ship_buf, rhs_buf, table_buf, sems)


def late_kernel(hub, rhs_ref, table_ref, old_ref, out_ref, rhs_buf, table_buf, sems):
    @pl.when(lax.axis_index("elem") == hub)
    def _():
        transform(rhs_ref, table_ref, out_ref, rhs_buf, table_buf, sems).wait()


def maps_kernel(
    modes, mode_total, hub, place, panels_ref, band_ref, radial_ref, stiff_ref, mass_ref, number_ref, reig_ref, axial_ref, aeig_ref,
    coup_ref, front_ref, back_ref, behind_ref, w_ref, reig_out, axial_out, weight_out, aeig_out,
    panels_buf, band_buf, radial_buf, stiff_buf, mass_buf, number_buf, axial_buf, coup_buf, front_buf, back_buf, behind_buf, sems,
):
    slabs, size = panels_ref.shape[1:3]
    inner = aeig_ref.shape[1]
    copies = start_copies(
        [(radial_ref, radial_buf), (stiff_ref, stiff_buf), (mass_ref, mass_buf), (number_ref, number_buf), (band_ref, band_buf)]
        + [(panels_ref.at[:, j], panels_buf.at[j]) for j in range(slabs)]
        + [(axial_ref, axial_buf), (coup_ref, coup_buf), (aeig_ref, aeig_out), (reig_ref, reig_out)],
        sems,
    )
    for copy in copies[:4]:
        copy.wait()
    for j in range(slabs):
        radial = wide(radial_buf[j])
        w_ref[place.at("radial", j)] = radial
        parts = [wide(product(ref[j].T, radial)) for ref in (stiff_buf, mass_buf)]
        for side in range(2):
            spot = lax.broadcasted_iota(jnp.int32, (size, size), 0)
            onehot = jnp.where(number_buf[j, side : side + 1] == spot, 1.0, 0.0).astype(BF16)
            for i in range(2):
                both = jnp.concatenate([p[:, i * size : (i + 1) * size] for p in parts], axis=1)
                w_ref[place.at("face", 4 * j + 2 * side + i)] = dot(onehot, both).astype(BF16)
    copies[4].wait()
    for j in range(1, slabs):
        bands = band_wide(band_buf[0, j], band_buf[1, j])
        for i in range(2):
            w_ref[place.at("band", 2 * (j - 1) + i)] = bands[:, 2 * i * size : 2 * (i + 1) * size]
    for j in range(slabs):
        copies[5 + j].wait()
        for k in range(modes):
            w_ref[place.at("panel", j, k)] = wide(panels_buf[j, k].T)
    for copy in copies[5 + slabs :]:
        copy.wait()
    for j in range(slabs):
        for b in range(inner):
            for a in range(inner):
                axial_out[j, a, b] = axial_buf[j, a, b]
            for side in range(2):
                weight = coup_buf[j, side, 0] * axial_buf[j, 0, b]
                for a in range(1, inner):
                    weight = weight + coup_buf[j, side, a] * axial_buf[j, a, b]
                weight_out[j, side, b] = weight

    @pl.when((lax.axis_index("elem") > 0) & (lax.axis_index("elem") <= hub))
    def _():
        lam = [wave_of(k, mode_total, modes) for k in range(modes)]
        current = None
        for j in range(slabs):
            first, second = band_buf[0, j].T, band_buf[1, j].T
            steps = [product(first + lam[k] * second, w_ref[place.at("panel", j, k)]) for k in range(modes)]
            if current is None:
                current = [-step for step in steps]
            else:
                current = [-product(current[k], wide(steps[k])) for k in range(modes)]
        for k in range(modes):
            front_buf[pl.ds(k * size, size)] = wide(current[k])
        start_copies([(front_buf, front_ref)], sems.at[pl.ds(1, 1)])

        @pl.when(lax.axis_index("elem") <= hub)
        def _():
            current = [-whole(w_ref[place.at("panel", slabs - 1, k)]) for k in range(modes)]
            for j in range(slabs - 2, -1, -1):
                steps = [
                    product(band_buf[0, j + 1] + lam[k] * band_buf[1, j + 1], w_ref[place.at("panel", j, k)]) for k in range(modes)
                ]
                current = [-product(current[k], wide(steps[k])) for k in range(modes)]
            for k in range(modes):
                back_buf[pl.ds(k * size, size)] = wide(product(current[k], wide(band_buf[0, 0] + lam[k] * band_buf[1, 0])))
            for copy in start_copies([(back_buf, back_ref)], sems):
                copy.wait()

        pltpu.make_async_copy(front_buf, front_ref, sems.at[1]).wait()

    @pl.when(lax.axis_index("elem") == lax.axis_size("elem") - 1)
    def _():
        behind_maps(behind_buf, band_buf, [wave_of(k, mode_total, modes) for k in range(modes)], w_ref, place)
        for copy in start_copies([(behind_buf, behind_ref)], sems):
            copy.wait()


def face_push(values, weight, lam):
    rows, size = values.shape
    high, low = split(values)
    blocks = [weight[:, i * size : (i + 1) * size] for i in range(4)]
    out = dot(
        jnp.concatenate([high, low], axis=0), jnp.concatenate(blocks, axis=0), NT
    )
    out = out[:rows, : 2 * size] + out[:rows, 2 * size :] + out[rows:, : 2 * size]
    return out[:, :size] + lam * out[:, size:]


def face_lift(values, weight, lam):
    rows, size = values.shape
    out = folded(dot(tall(values), weight), rows)
    return out[:, :size] + lam * out[:, size:]


def block_of(spec_ref, index, size):
    per = spec_ref.shape[2] // size
    at = index % per * size
    return spec_ref[index // per, :, at : at + size]


def band_step(values, weight, lam):
    return face_push(values, weight, lam)


def inner_kernel(modes, mode_total, place, hub, first_call, band_ref, front_ref, behind_ref, *refs):
    elem = lax.axis_index("elem")
    if first_call:
        spec_ref, w_ref, reig_ref, axial_ref, weight_ref, aeig_ref, zsrc_ref, inv_ref, reduced_ref, y_ref, send_ref = refs
    else:
        spec_ref, w_ref, reig_ref = refs[:3]
        axial_ref, weight_ref, aeig_ref, zsrc_ref, inv_ref, reduced_ref, y_ref, load_ref, front_out, band_buf, behind_buf, sems = refs[7:]
        inside = (elem > 0) & (elem <= hub)
        early = (front_ref, front_out)
        late = [(band_ref.at[:, 0], band_buf), (behind_ref, behind_buf)]

        @pl.when(inside)
        def _():
            start_copies([early], sems.at[pl.ds(1, 1)])

        @pl.when(elem == lax.axis_size("elem") - 1)
        def _():
            start_copies(late, sems)

    @pl.when((elem == 0) == first_call)
    def _():
        load, values = inner_part(
            modes, mode_total, place, spec_ref, w_ref, reig_ref, axial_ref, weight_ref, aeig_ref, zsrc_ref, inv_ref, reduced_ref, y_ref
        )
        if first_call:
            send_ref[...] = values[-1]
            return
        load_ref[1] = load

        @pl.when(inside)
        def _():
            pltpu.make_async_copy(*early, sems.at[1]).wait()

        @pl.when(elem == lax.axis_size("elem") - 1)
        def _():
            lam = wave(mode_total, load.shape, modes)
            current = values[-1]
            for i, pair in enumerate(late):
                pltpu.make_async_copy(*pair, sems.at[i]).wait()
            for j in range(len(values) - 2, -1, -1):
                current = values[j] - apply(current, behind_buf[j], modes)
            load_ref[0] = load + face_lift(current, band_wide(band_buf[0], band_buf[1]), lam)


def inner_part(
    modes, mode_total, place, spec_ref, w_ref, reig_ref, axial_ref, weight_ref, aeig_ref, zsrc_ref, inv_ref, solved_ref, y_ref
):
    slabs, inner, rows, size = zsrc_ref.shape
    lam = wave(mode_total, (rows, size), modes)
    pushed = []
    for j in range(slabs):
        source = jnp.concatenate(
            [block_of(spec_ref, j * (inner + 1) + a, size) for a in range(inner)], axis=0
        )
        first = product(source, w_ref[place.at("radial", j)])
        first = [first[a * rows : (a + 1) * rows] for a in range(inner)]
        sums = [None, None]
        for b in range(inner):
            value = first[0] * axial_ref[j, 0, b]
            for a in range(1, inner):
                value = value + first[a] * axial_ref[j, a, b]
            inverse = 1.0 / (aeig_ref[j, b] + reig_ref[j : j + 1] + lam)
            inv_ref[j, b] = inverse
            value = value * inverse
            zsrc_ref[j, b] = value
            for side in range(2):
                term = value * weight_ref[j, side, b]
                sums[side] = term if sums[side] is None else sums[side] + term
        pushed.append([face_push(sums[side], place.face(w_ref, j, side), lam) for side in range(2)])
    load = pushed[0][0]
    values = []
    for j in range(slabs):
        reduced = block_of(spec_ref, j * (inner + 1) + inner, size) - pushed[j][1]
        if j + 1 < slabs:
            reduced = reduced - pushed[j + 1][0]
        panel = w_ref[place.at("panel", j)]
        solved_ref[j] = reduced
        if j > 0:
            reduced = reduced - band_step(values[-1], place.band(w_ref, j), lam)
        values.append(apply(reduced, panel, modes))
        y_ref[j] = values[j]
    return load, values


def previous_weight(panel_ref, modes):
    parts = [split(panel_ref[k]) for k in range(modes)]
    return jnp.concatenate(
        [jnp.concatenate([p[i] for p in parts], axis=1) for i in range(2)], axis=0
    )


def apply_nt(x, weight, modes):
    return folded(dot(by_mode(x, modes), weight, NT), x.shape[0])


def backward_values(values, after, panel, behind_ref, modes):
    slabs = len(values)
    out = [None] * slabs
    out[-1] = values[-1]
    if after is not None:
        out[-1] = out[-1] - apply(after, panel, modes)
    for j in range(slabs - 2, -1, -1):
        out[j] = values[j] - apply(out[j + 1], behind_ref[j], modes)
    return out


def push_kernel(modes, first_ref, load_ref, prev_ref, push_ref, prev_buf, sems):
    @pl.when(lax.axis_index("elem") == 1)
    def _():
        for copy in start_copies([(first_ref, prev_buf)], sems):
            copy.wait()
        weight = previous_weight(prev_buf, modes)
        prev_ref[...] = weight
        push_ref[...] = apply_nt(load_ref[1], weight, modes)


def forward_kernel(modes, at, got_ref, push_ref, y_ref, front_ref, old_ref, state_ref, send_ref):
    @pl.when(lax.axis_index("elem") == at)
    def _():
        before = got_ref[...] - push_ref[...]
        state_ref[0] = before
        send_ref[...] = y_ref[y_ref.shape[0] - 1] + apply(before, front_ref[...], modes)


def base_kernel(
    modes, mode_total, hub, place, band_ref, map_ref, state_ref, load_ref, reduced_ref, y_ref, w_ref,
    base_ref, found_ref, back_ref, band_buf, sems,
):
    elem = lax.axis_index("elem")
    slabs, rows, size = reduced_ref.shape
    lam = wave(mode_total, (rows, size), modes)

    @pl.when((elem > 0) & (elem < hub))
    def _():
        copies = start_copies([(band_ref.at[:, 0], band_buf), (map_ref, back_ref)], sems)
        copies[0].wait()
        first = band_wide(band_buf[0], band_buf[1])
        bands = [first] + [place.band(w_ref, j) for j in range(1, slabs)]
        panels = [w_ref[place.at("panel", j)] for j in range(slabs)]
        values = []
        for j in range(slabs):
            step = face_push(values[-1] if j > 0 else state_ref[0], bands[j], lam)
            values.append(apply(reduced_ref[j] - step, panels[j], modes))
        found = values[-1]
        found_ref[slabs - 1] = found
        for j in range(slabs - 2, -1, -1):
            found = values[j] - apply(face_lift(found, bands[j + 1], lam), panels[j], modes)
            found_ref[j] = found
        base_ref[...] = load_ref[1] + face_lift(found, first, lam)
        copies[1].wait()


def ahead_maps(ahead_ref, band_buf, waves, w_ref, place):
    slabs, many, _ = ahead_ref.shape
    for j in range(slabs):
        first, second = band_buf[0, j].T, band_buf[1, j].T
        for k, lam in enumerate(waves):
            ahead_ref[j, pl.ds(k * place.size, place.size)] = wide(product(first + lam * second, w_ref[place.at("panel", j, k)]))


def behind_maps(behind_ref, band_buf, waves, w_ref, place):
    for j in range(behind_ref.shape[0]):
        for k, lam in enumerate(waves):
            step = product(band_buf[0, j + 1] + lam * band_buf[1, j + 1], w_ref[place.at("panel", j, k)])
            behind_ref[j, pl.ds(k * place.size, place.size)] = wide(step)


def hub_map_kernel(
    modes, mode_total, hub, place, map_ref, pprev_ref, band_ref, given_ref, load_ref, y_ref, w_ref, front_ref, old_prev_ref, old_push_ref,
    prev_ref, push_ref, ahead_ref, behind_ref, back_ref, base_ref, cross_ref, far_ref, band_buf, map_buf, prev_buf, sems,
):
    slabs, rows, size = y_ref.shape
    lam = wave(mode_total, (rows, size), modes)
    inside = (lax.axis_index("elem") > 1) & (lax.axis_index("elem") <= hub)

    @pl.when(inside)
    def _():
        start_copies([(pprev_ref, prev_buf)], sems.at[pl.ds(2, 1)])

    @pl.when(lax.axis_index("elem") == hub)
    def _():
        copies = start_copies([(band_ref, band_buf), (map_ref, map_buf)], sems)
        given = start_copies([(given_ref, back_ref)], sems.at[pl.ds(3, 1)])[0]
        waves = [wave_of(k, mode_total, modes) for k in range(modes)]

        def part(k):
            return pl.ds(k * size, size)

        copies[0].wait()
        ahead_maps(ahead_ref, band_buf, waves, w_ref, place)
        behind_maps(behind_ref, band_buf, waves, w_ref, place)
        entry = [wide(band_buf[0, 0] + waves[k] * band_buf[1, 0]) for k in range(modes)]
        forward = [[-whole(ahead_ref[0, part(k)]) for k in range(modes)]]
        for j in range(1, slabs - 1):
            forward.append([-product(forward[-1][k], ahead_ref[j, part(k)]) for k in range(modes)])
        cross = [whole(front_ref[part(k)]) for k in range(modes)]
        for j in range(slabs - 2, -1, -1):
            cross = [forward[j][k] - product(cross[k], behind_ref[j, part(k)]) for k in range(modes)]
        for k in range(modes):
            cross_ref[part(k)] = wide(product(cross[k], entry[k]))
        found = backward_values([y_ref[j] for j in range(slabs)], None, None, behind_ref, modes)
        base_ref[...] = load_ref[1] + face_lift(found[0], band_wide(band_buf[0, 0], band_buf[1, 0]), lam)
        copies[1].wait()
        far_ref[...] = previous_weight(map_buf, modes)
        given.wait()

    @pl.when(inside)
    def _():
        pltpu.make_async_copy(pprev_ref, prev_buf, sems.at[2]).wait()
        weight = previous_weight(prev_buf, modes)
        prev_ref[...] = weight
        push_ref[...] = apply_nt(load_ref[1], weight, modes)


def hub_kernel(
    modes, at, place, got_ref, push_ref, far_ref, far_weight_ref, y_ref, front_ref, back_ref, cross_ref, base_ref, w_ref, old_ref,
    state_ref, send_ref, last_ref,
):
    slabs = y_ref.shape[0]

    @pl.when(lax.axis_index("elem") == at)
    def _():
        panel = w_ref[place.at("panel", slabs - 1)]
        load = apply(far_ref[1], panel, modes)
        before = got_ref[...] - push_ref[...]
        state_ref[0] = before
        value = y_ref[slabs - 1] + apply(before, front_ref[...], modes)
        out = base_ref[...] + apply(before, cross_ref[...], modes)
        final = value - load
        after = far_ref[0] + apply_nt(final, far_weight_ref[...], modes)
        state_ref[1] = after
        send_ref[...] = out + apply(after, back_ref[...], modes)
        last_ref[0] = final
        last_ref[1] = value - apply(after, panel, modes)


def own_map_kernel(
    modes, mode_total, hub, place, band_ref, radial_ref, state_ref, reduced_ref, y_ref, w_ref, prev_ref, ahead_ref, behind_ref, old_ref,
    found_ref, own_ref, before_ref, radt_ref, ahead_buf, behind_buf, band_buf, radial_buf, sems,
):
    slabs, rows, size = reduced_ref.shape
    elem, last = lax.axis_index("elem"), lax.axis_size("elem") - 1
    lam = wave(mode_total, (rows, size), modes)
    waves = [wave_of(k, mode_total, modes) for k in range(modes)]
    copies = start_copies([(band_ref, band_buf), (radial_ref, radial_buf)], sems)

    def part(k):
        return pl.ds(k * size, size)

    copies[0].wait()

    @pl.when(elem == hub)
    def _():
        panels = [w_ref[place.at("panel", j)] for j in range(slabs)]
        before, values = state_ref[0], []
        for j in range(slabs):
            solved = apply(reduced_ref[j], panels[j], modes)
            values.append(solved - apply(values[-1] if j > 0 else before, ahead_ref[j], modes))
        found = backward_values(values, state_ref[1], panels[-1], behind_ref, modes)
        for j in range(slabs):
            found_ref[j] = found[j]
        back = face_lift(found[0], band_wide(band_buf[0, 0], band_buf[1, 0]), lam)
        before_ref[...] = before - apply_nt(back, prev_ref[...], modes)

    @pl.when(elem != hub)
    def _():
        behind_maps(behind_buf, band_buf, waves, w_ref, place)

    @pl.when(elem < hub)
    def _():
        current = [-whole(w_ref[place.at("panel", slabs - 1, k)]) for k in range(modes)]
        for k in range(modes):
            own_ref[slabs - 1, part(k)] = -w_ref[place.at("panel", slabs - 1, k)]
        for j in range(slabs - 2, -1, -1):
            current = [-product(current[k], behind_buf[j, part(k)]) for k in range(modes)]
            for k in range(modes):
                own_ref[j, part(k)] = wide(current[k])

    @pl.when(elem == last)
    def _():
        ahead_maps(ahead_buf, band_buf, waves, w_ref, place)
        forward = [[-whole(ahead_buf[0, part(k)]) for k in range(modes)]]
        for j in range(1, slabs):
            forward.append([-product(forward[-1][k], ahead_buf[j, part(k)]) for k in range(modes)])
        current = forward[-1]
        for k in range(modes):
            own_ref[slabs - 1, part(k)] = wide(current[k])
        for j in range(slabs - 2, -1, -1):
            current = [forward[j][k] - product(current[k], behind_buf[j, part(k)]) for k in range(modes)]
            for k in range(modes):
                own_ref[j, part(k)] = wide(current[k])

    @pl.when((elem == 0) | (elem == last))
    def _():
        found = backward_values([y_ref[j] for j in range(slabs)], None, None, behind_buf, modes)
        for j in range(slabs):
            found_ref[j] = found[j]

    copies[1].wait()
    for j in range(slabs):
        radt_ref[j] = wide(radial_buf[j].T)


def backward_kernel(modes, at, got_ref, base_ref, back_ref, old_ref, state_ref, send_ref):
    @pl.when(lax.axis_index("elem") == at)
    def _():
        after = got_ref[...]
        state_ref[1] = after
        send_ref[...] = base_ref[...] + apply(after, back_ref[...], modes)


def final_kernel(
    modes, mode_total, hub, place, zsrc_ref, inv_ref, state_ref, got_ref, base_ref, last_ref, load_ref, found_ref, own_ref, back_ref, before_ref, prev_ref, w_ref, radt_ref, axial_ref, weight_ref,
    out_ref, x_ref, out_buf, sems,
):
    slabs, inner, rows, size = zsrc_ref.shape
    lam = wave(mode_total, (rows, size), modes)
    elem, last = lax.axis_index("elem"), lax.axis_size("elem") - 1

    def values(given):
        for j in range(slabs):
            x_ref[j + 1] = found_ref[j] + apply(given, own_ref[j], modes)

    @pl.when(elem == 0)
    def _():
        x_ref[0] = jnp.zeros((rows, size), F32)
        values(got_ref[...])

    @pl.when((elem > 0) & (elem < hub))
    def _():
        after = state_ref[1]
        values(after)
        back = base_ref[...] - load_ref[1] + apply(after, back_ref[...], modes)
        x_ref[0] = state_ref[0] - apply_nt(back, prev_ref[...], modes)

    @pl.when(elem == hub)
    def _():
        for j in range(slabs):
            x_ref[j + 1] = found_ref[j]
        x_ref[0] = before_ref[...]

    @pl.when(elem == last)
    def _():
        values(last_ref[0])
        x_ref[0] = last_ref[1]

    copies = []
    for j in range(slabs):
        lifted = [face_lift(x_ref[j + side], place.face(w_ref, j, side), lam) for side in range(2)]
        kept = []
        for b in range(inner):
            total = lifted[0] * weight_ref[j, 0, b] + lifted[1] * weight_ref[j, 1, b]
            kept.append(zsrc_ref[j, b] - total * inv_ref[j, b])
        values = []
        for a in range(inner):
            value = kept[0] * axial_ref[j, a, 0]
            for b in range(1, inner):
                value = value + kept[b] * axial_ref[j, a, b]
            values.append(value)
        result = product(jnp.concatenate(values, axis=0), radt_ref[j])
        for a in range(inner):
            out_buf[j, :, a * size : (a + 1) * size] = result[a * rows : (a + 1) * rows]
        out_buf[j, :, inner * size :] = x_ref[j + 1]
        width = (inner + 1) * size
        copies += start_copies([(out_buf.at[j], out_ref.at[:, pl.ds(j * width, width)])], sems.at[pl.ds(j, 1)])
    for copy in copies:
        copy.wait()


def dft_table(planes):
    row, col = np.arange(planes)[:, None], np.arange(planes)[None]
    angle = row // 2 * col % planes * (2.0 * math.pi / planes)
    table = np.where(row % 2 == 0, np.cos(angle), -np.sin(angle)) / math.sqrt(planes)
    table = jnp.asarray(table, F32)
    high, low = split(table)
    return jnp.concatenate([high, low, high], axis=1)


def body(
    rhs_phys, radial_basis, axial_basis, radial_eig, axial_eig, face_stiff, face_mass, axial_coupling, face_numbering,
    band_panels, inverse_panels,
):
    planes, nodes = rhs_phys.shape
    modes, slabs, size, _ = inverse_panels.shape
    inner = axial_basis.shape[1]
    devices = lax.axis_size("mode")
    elems = lax.axis_size("elem")
    mode_total = modes * devices
    rows = 2 * modes
    hub = elems - 2
    last = elems - 1

    def shape(*dims):
        return jax.ShapeDtypeStruct(dims, F32)

    def kept(*dims):
        return pltpu.VMEM(dims, F32)

    def half(*dims):
        return pltpu.VMEM(dims, BF16)

    table = dft_table(planes)
    many = modes * size
    place = Weights(size, ("panel", slabs, many), ("radial", slabs, size), ("face", 4 * slabs, size), ("band", 2 * (slabs - 1), size))
    buffers = [pltpu.VMEM((planes, nodes), F32), pltpu.VMEM(table.shape, BF16), pltpu.SemaphoreType.DMA((slabs + 3,))]
    whole_spectrum = pltpu.HBM((planes, nodes), F32)
    whole_panels = pltpu.HBM((modes, size, size), F32)
    panels_buffer = pltpu.VMEM((modes, size, size), F32)
    ship, spectrum = call(
        functools.partial(ends_kernel, modes, mode_total),
        [whole_panels, whole_spectrum],
        [inverse_panels, band_panels, rhs_phys, table],
        anywhere=4,
        scratch=[pltpu.VMEM((slabs, modes, size, size), F32), pltpu.VMEM(band_panels.shape, F32), panels_buffer] + buffers,
    )
    if hub > 1:
        first = far_map = lax.ppermute(ship, "elem", [(0, 1), (last, hub)])
    else:
        first, far_map = lax.ppermute(ship, "elem", [(0, 1)]), lax.ppermute(ship, "elem", [(last, hub)])
    ship, spectrum = call(
        functools.partial(between_kernel, hub),
        [whole_panels, whole_spectrum],
        [inverse_panels, rhs_phys, table, spectrum],
        anywhere=4,
        scratch=[panels_buffer] + buffers,
        aliases={3: 1},
    )
    pprev = lax.ppermute(ship, "elem", [(i, i + 1) for i in range(1, hub)]) if hub > 1 else first
    spectrum = call(
        functools.partial(late_kernel, hub),
        [whole_spectrum],
        [rhs_phys, table, spectrum],
        anywhere=3,
        scratch=buffers,
        aliases={2: 0},
    )[0]
    spectrum = lax.all_to_all(spectrum.reshape(devices, rows, nodes), "mode", 0, 0, tiled=False)
    if nodes % size:
        spectrum = jnp.swapaxes(spectrum, 0, 1).reshape(1, rows, devices * nodes)
    vector = (rows, size)
    matrix = half(many, 2 * size)
    front, back_map, later, w, reig, axial, weight, aeig = call(
        functools.partial(maps_kernel, modes, mode_total, hub, place),
        [
            pltpu.HBM((many, 2 * size), BF16),
            pltpu.HBM((many, 2 * size), BF16),
            pltpu.HBM((slabs - 1, many, 2 * size), BF16),
            half(place.total, 2 * size),
            kept(*radial_eig.shape),
            pltpu.SMEM(axial_basis.shape, F32),
            pltpu.SMEM((slabs, 2, inner), F32),
            pltpu.SMEM(axial_eig.shape, F32),
        ],
        [
            inverse_panels, band_panels, radial_basis, face_stiff, face_mass, face_numbering,
            radial_eig, axial_basis, axial_eig, axial_coupling,
        ],
        anywhere=10,
        outside=3,
        scratch=[
            pltpu.VMEM((slabs, modes, size, size), F32),
            pltpu.VMEM(band_panels.shape, F32),
            pltpu.VMEM(radial_basis.shape, F32),
            pltpu.VMEM(face_stiff.shape, F32),
            pltpu.VMEM(face_mass.shape, F32),
            pltpu.VMEM(face_numbering.shape, jnp.int32),
            pltpu.SMEM(axial_basis.shape, F32),
            pltpu.SMEM(axial_coupling.shape, F32),
            pltpu.VMEM((many, 2 * size), BF16),
            pltpu.VMEM((many, 2 * size), BF16),
            pltpu.VMEM((slabs - 1, many, 2 * size), BF16),
            pltpu.SemaphoreType.DMA((slabs + 9,)),
        ],
    )
    solves = [kept(slabs, inner, *vector), kept(slabs, inner, *vector), kept(slabs, *vector), kept(slabs, *vector)]
    *solve, send = call(
        functools.partial(inner_kernel, modes, mode_total, place, hub, True),
        solves + [kept(*vector)],
        [band_panels, front, later, spectrum, w, reig, axial, weight, aeig],
        anywhere=3,
        smem=3,
    )
    got = lax.ppermute(send, "elem", [(0, 1)])
    zsrc, inv, reduced, y, load, front = call(
        functools.partial(inner_kernel, modes, mode_total, place, hub, False),
        solves + [kept(2, *vector), matrix],
        [band_panels, front, later, spectrum, w, reig, *solve, axial, weight, aeig],
        anywhere=3,
        smem=3,
        scratch=[
            pltpu.VMEM((2, size, size), F32),
            pltpu.VMEM((slabs - 1, many, 2 * size), BF16),
            pltpu.SemaphoreType.DMA((2,)),
        ],
        aliases={6 + i: i for i in range(4)},
    )
    far = lax.ppermute(load, "elem", [(last, hub)])
    prev, push = call(
        functools.partial(push_kernel, modes),
        [half(2 * size, many), kept(*vector)],
        [first, load],
        free=1,
        scratch=[panels_buffer, pltpu.SemaphoreType.DMA((1,))],
    )
    prev, later_push, ahead, behind, hub_back, hub_base, cross, far_weight = call(
        functools.partial(hub_map_kernel, modes, mode_total, hub, place),
        [
            half(2 * size, many), kept(*vector), half(slabs, many, 2 * size), half(slabs - 1, many, 2 * size), matrix,
            kept(*vector), matrix, half(2 * size, many),
        ],
        [far_map, pprev, band_panels, back_map, load, y, w, front, prev, push],
        free=2,
        anywhere=2,
        scratch=[pltpu.VMEM(band_panels.shape, F32), panels_buffer, panels_buffer, pltpu.SemaphoreType.DMA((4,))],
        aliases={8: 0, 9: 1},
    )
    state = jnp.zeros((2, *vector), F32)
    for at in range(1, hub):
        state, send = call(
            functools.partial(forward_kernel, modes, at),
            [kept(*state.shape), shape(*vector)],
            [got, push if at == 1 else later_push, y, front, state],
            aliases={4: 0},
        )
        got = lax.ppermute(send, "elem", [(at, at + 1)])
    state, send, final = call(
        functools.partial(hub_kernel, modes, hub, place),
        [kept(*state.shape), shape(*vector), shape(2, *vector)],
        [got, push if hub == 1 else later_push, far, far_weight, y, front, hub_back, cross, hub_base, w, state],
        aliases={10: 0},
    )
    base, found, back = call(
        functools.partial(base_kernel, modes, mode_total, hub, place),
        [kept(*vector), kept(slabs, *vector), matrix],
        [band_panels, back_map, state, load, reduced, y, w],
        anywhere=2,
        scratch=[pltpu.VMEM((2, size, size), F32), pltpu.SemaphoreType.DMA((2,))],
    )
    for at in range(hub - 1, 0, -1):
        got = lax.ppermute(send, "elem", [(at + 1, at)])
        state, send = call(
            functools.partial(backward_kernel, modes, at),
            [kept(*state.shape), shape(*vector)],
            [got, base, back, state],
            aliases={3: 0},
        )
    got = lax.ppermute(send, "elem", [(1, 0)])
    found, own, before, radt = call(
        functools.partial(own_map_kernel, modes, mode_total, hub, place),
        [kept(slabs, *vector), half(slabs, many, 2 * size), kept(*vector), half(slabs, size, 2 * size)],
        [band_panels, radial_basis, state, reduced, y, w, prev, ahead, behind, found],
        anywhere=2,
        scratch=[
            pltpu.VMEM((slabs, many, 2 * size), BF16),
            pltpu.VMEM((slabs - 1, many, 2 * size), BF16),
            pltpu.VMEM(band_panels.shape, F32),
            pltpu.VMEM(radial_basis.shape, F32),
            pltpu.SemaphoreType.DMA((2,)),
        ],
        aliases={9: 0},
    )
    final = lax.ppermute(final, "elem", [(hub, last)])
    return call(
        functools.partial(final_kernel, modes, mode_total, hub, place),
        [pltpu.HBM((rows, slabs * (inner + 1) * size), F32)],
        [
            zsrc, inv, state, got, base, final, load, found, own, back, before, prev, w, radt, axial, weight,
        ],
        smem=2,
        scratch=[
            pltpu.VMEM((slabs + 1, *vector), F32),
            pltpu.VMEM((slabs, rows, (inner + 1) * size), F32),
            pltpu.SemaphoreType.DMA((slabs,)),
        ],
    )[0]


def solution(mesh):
    placed = (
        P(None, ("elem", "mode")),
        P("elem", None, None),
        P("elem", None, None),
        P("elem", None),
        P("elem", None),
        P("elem", None, None),
        P("elem", None, None),
        P("elem", None, None),
        P("elem", None, None),
        P(None, "elem", None, None),
        P("mode", "elem", None, None),
    )
    return jax.shard_map(
        body, mesh=mesh, in_specs=placed, out_specs=P("mode", "elem"), check_vma=False
    )
```

```python
import functools
import math

import jax
import jax.numpy as jnp
import numpy as np
from jax import lax
from jax.experimental import pallas as pl
from jax.experimental.pallas import tpu as pltpu
from jax.sharding import PartitionSpec as P

F32 = jnp.float32
BF16 = jnp.bfloat16
VMEM = pl.BlockSpec(memory_space=pltpu.VMEM)
SMEM = pl.BlockSpec(memory_space=pltpu.SMEM)
HBM = pl.BlockSpec(memory_space=pltpu.HBM)
ANY = pl.BlockSpec(memory_space=pl.ANY)
NN = (((1,), (0,)), ((), ()))
NT = (((1,), (1,)), ((), ()))


def call(kernel, outs, args, smem=0, anywhere=0, free=0, outside=0, scratch=(), aliases=None):
    inside = len(args) - smem - anywhere - free
    spaces = [None] * free + [pltpu.HBM] * anywhere + [pltpu.VMEM] * inside + [pltpu.SMEM] * smem
    args = [arg if space is None else pltpu.with_memory_space_constraint(arg, space) for arg, space in zip(args, spaces)]
    return pl.pallas_call(
        kernel,
        out_shape=outs,
        in_specs=[ANY] * free + [HBM] * anywhere + [VMEM] * inside + [SMEM] * smem,
        out_specs=[HBM if getattr(out, "memory_space", None) is pltpu.HBM else VMEM for out in outs[: len(outs) - outside]]
        + [SMEM] * outside,
        scratch_shapes=scratch,
        input_output_aliases=aliases or {},
        compiler_params=pltpu.CompilerParams(vmem_limit_bytes=16 * 2**20),
    )(*args)


def split(x):
    high = x.astype(BF16)
    return high, (x - high.astype(F32)).astype(BF16)


def dot(a, b, dims=NN):
    return lax.dot_general(a, b, dims, preferred_element_type=F32)


def wide(x):
    return jnp.concatenate(split(x), axis=1)


def tall(x):
    return jnp.concatenate(split(x), axis=0)


def product(left, right):
    size = right.shape[1] // 2
    out = dot(wide(left), jnp.concatenate([right, right], axis=0))
    return out[:, :size] + out[:, size:]


def by_mode(x, modes):
    mode_of = lax.broadcasted_iota(jnp.int32, x.shape, 0) // 2
    spread = jnp.concatenate([jnp.where(mode_of == k, x, 0.0) for k in range(modes)], axis=1)
    return tall(spread)


def folded(out, rows):
    size = out.shape[1] // 2
    return out[:rows, :size] + out[:rows, size:] + out[rows:, :size]


def apply(x, weight, modes):
    return folded(dot(by_mode(x, modes), weight), x.shape[0])


def wave(mode_total, shape, modes, axis=0):
    first = lax.axis_index("mode") * modes
    index = first + lax.broadcasted_iota(jnp.int32, shape, axis) // 2
    number = index.astype(F32) / mode_total
    return 4.0 * number * number


def wave_of(k, mode_total, modes):
    number = (jnp.full((1, 1), lax.axis_index("mode") * modes + k, jnp.int32)).astype(F32) / mode_total
    return 4.0 * number * number


class Weights:
    def __init__(self, size, *entries):
        self.size, self.rows = size, {}
        self.total = 0
        for name, count, rows in entries:
            self.rows[name] = (self.total, rows)
            self.total += count * rows

    def at(self, name, index, mode=None):
        start, rows = self.rows[name]
        if mode is None:
            return pl.ds(start + index * rows, rows)
        return pl.ds(start + index * rows + mode * self.size, self.size)

    def pair(self, ref, name, index):
        return jnp.concatenate([ref[self.at(name, index)], ref[self.at(name, index + 1)]], axis=1)

    def band(self, ref, slab):
        return self.pair(ref, "band", 2 * (slab - 1))

    def face(self, ref, slab, side):
        return self.pair(ref, "face", 4 * slab + 2 * side)


def band_wide(stiff, mass):
    return wide(jnp.concatenate([stiff, mass], axis=1))


def whole(weight):
    size = weight.shape[1] // 2
    value = weight.astype(F32)
    return value[:, :size] + value[:, size:]


def start_copies(pairs, sems):
    copies = [pltpu.make_async_copy(src, dst, sems.at[i]) for i, (src, dst) in enumerate(pairs)]
    for copy in copies:
        copy.start()
    return copies


def transform(rhs_ref, table_ref, out_ref, rhs_buf, table_buf, sems, started=None):
    for copy in started or start_copies([(rhs_ref, rhs_buf), (table_ref, table_buf)], sems):
        copy.wait()
    high, low = split(rhs_buf[...])
    rhs_buf[...] = dot(table_buf[...], jnp.concatenate([high, high, low], axis=0))
    return start_copies([(rhs_buf, out_ref)], sems)[0]


def panels_and_transform(panels_ref, ship_ref, rhs_ref, table_ref, out_ref, ship_buf, rhs_buf, table_buf, sems):
    half = ship_buf.shape[0] // 2
    parts = [pl.ds(0, half), pl.ds(half, ship_buf.shape[0] - half)]
    fetch = start_copies([(panels_ref.at[part, panels_ref.shape[1] - 1], ship_buf.at[part]) for part in parts], sems.at[pl.ds(2, 2)])
    result = transform(rhs_ref, table_ref, out_ref, rhs_buf, table_buf, sems)
    ship = []
    for i, part in enumerate(parts):
        fetch[i].wait()
        ship += start_copies([(ship_buf.at[part], ship_ref.at[part])], sems.at[pl.ds(2 + i, 1)])
    for copy in [result] + ship:
        copy.wait()


def ends_kernel(
    modes, mode_total, panels_ref, band_ref, rhs_ref, table_ref, ship_ref, out_ref,
    panels_buf, band_buf, ship_buf, rhs_buf, table_buf, sems,
):
    slabs, size = panels_ref.shape[1:3]
    elem, last = lax.axis_index("elem"), lax.axis_size("elem") - 1

    @pl.when(elem == 0)
    def _():
        panels_and_transform(panels_ref, ship_ref, rhs_ref, table_ref, out_ref, ship_buf, rhs_buf, table_buf, sems)

    @pl.when(elem == last)
    def _():
        copies = start_copies(
            [(band_ref, band_buf)] + [(panels_ref.at[:, j], panels_buf.at[j]) for j in range(slabs)],
            sems.at[pl.ds(2, slabs + 1)],
        )
        started = start_copies([(rhs_ref, rhs_buf), (table_ref, table_buf)], sems)
        copies[0].wait()
        band_t = [(band_buf[0, j].T, band_buf[1, j].T) for j in range(slabs)]
        lam = [wave_of(k, mode_total, modes) for k in range(modes)]
        forward = []
        for j in range(slabs):
            copies[1 + j].wait()
            steps = [
                product(panels_buf[j, k], wide(band_buf[0, j] + lam[k] * band_buf[1, j])) for k in range(modes)
            ]
            if j == 0:
                forward.append([-step for step in steps])
            else:
                forward.append([-product(steps[k], wide(forward[-1][k])) for k in range(modes)])
        current = forward[-1]
        for j in range(slabs - 2, -1, -1):
            steps = [
                product(panels_buf[j, k], wide(band_t[j + 1][0] + lam[k] * band_t[j + 1][1])) for k in range(modes)
            ]
            current = [forward[j][k] - product(steps[k], wide(current[k])) for k in range(modes)]
        ship = [transform(rhs_ref, table_ref, out_ref, rhs_buf, table_buf, sems, started)]
        half = modes // 2
        for i, part in enumerate((range(half), range(half, modes))):
            for k in part:
                ship_buf[k] = product(band_t[0][0] + lam[k] * band_t[0][1], wide(current[k]))
            rows = pl.ds(part.start, len(part))
            ship += start_copies([(ship_buf.at[rows], ship_ref.at[rows])], sems.at[pl.ds(2 + i, 1)])
        for copy in ship:
            copy.wait()


def between_kernel(hub, panels_ref, rhs_ref, table_ref, old_ref, ship_ref, out_ref, ship_buf, rhs_buf, table_buf, sems):
    elem = lax.axis_index("elem")

    @pl.when((elem > 0) & (elem < hub))
    def _():
        panels_and_transform(panels_ref, ship_ref, rhs_ref, table_ref, out_ref, ship_buf, rhs_buf, table_buf, sems)


def late_kernel(hub, rhs_ref, table_ref, old_ref, out_ref, rhs_buf, table_buf, sems):
    @pl.when(lax.axis_index("elem") == hub)
    def _():
        transform(rhs_ref, table_ref, out_ref, rhs_buf, table_buf, sems).wait()


def maps_kernel(
    modes, mode_total, hub, place, panels_ref, band_ref, radial_ref, stiff_ref, mass_ref, number_ref, reig_ref, axial_ref, aeig_ref,
    coup_ref, front_ref, back_ref, behind_ref, w_ref, reig_out, axial_out, weight_out, aeig_out,
    panels_buf, band_buf, radial_buf, stiff_buf, mass_buf, number_buf, axial_buf, coup_buf, front_buf, back_buf, behind_buf, sems,
):
    slabs, size = panels_ref.shape[1:3]
    inner = aeig_ref.shape[1]
    copies = start_copies(
        [(radial_ref, radial_buf), (stiff_ref, stiff_buf), (mass_ref, mass_buf), (number_ref, number_buf), (band_ref, band_buf)]
        + [(panels_ref.at[:, j], panels_buf.at[j]) for j in range(slabs)]
        + [(axial_ref, axial_buf), (coup_ref, coup_buf), (aeig_ref, aeig_out), (reig_ref, reig_out)],
        sems,
    )
    for copy in copies[:4]:
        copy.wait()
    for j in range(slabs):
        radial = wide(radial_buf[j])
        w_ref[place.at("radial", j)] = radial
        parts = [wide(product(ref[j].T, radial)) for ref in (stiff_buf, mass_buf)]
        for side in range(2):
            spot = lax.broadcasted_iota(jnp.int32, (size, size), 0)
            onehot = jnp.where(number_buf[j, side : side + 1] == spot, 1.0, 0.0).astype(BF16)
            for i in range(2):
                both = jnp.concatenate([p[:, i * size : (i + 1) * size] for p in parts], axis=1)
                w_ref[place.at("face", 4 * j + 2 * side + i)] = dot(onehot, both).astype(BF16)
    copies[4].wait()
    for j in range(1, slabs):
        bands = band_wide(band_buf[0, j], band_buf[1, j])
        for i in range(2):
            w_ref[place.at("band", 2 * (j - 1) + i)] = bands[:, 2 * i * size : 2 * (i + 1) * size]
    for j in range(slabs):
        copies[5 + j].wait()
        for k in range(modes):
            w_ref[place.at("panel", j, k)] = wide(panels_buf[j, k].T)
    for copy in copies[5 + slabs :]:
        copy.wait()
    for j in range(slabs):
        for b in range(inner):
            for a in range(inner):
                axial_out[j, a, b] = axial_buf[j, a, b]
            for side in range(2):
                weight = coup_buf[j, side, 0] * axial_buf[j, 0, b]
                for a in range(1, inner):
                    weight = weight + coup_buf[j, side, a] * axial_buf[j, a, b]
                weight_out[j, side, b] = weight

    @pl.when((lax.axis_index("elem") > 0) & (lax.axis_index("elem") <= hub))
    def _():
        lam = [wave_of(k, mode_total, modes) for k in range(modes)]
        current = None
        for j in range(slabs):
            first, second = band_buf[0, j].T, band_buf[1, j].T
            steps = [product(first + lam[k] * second, w_ref[place.at("panel", j, k)]) for k in range(modes)]
            if current is None:
                current = [-step for step in steps]
            else:
                current = [-product(current[k], wide(steps[k])) for k in range(modes)]
        for k in range(modes):
            front_buf[pl.ds(k * size, size)] = wide(current[k])
        start_copies([(front_buf, front_ref)], sems.at[pl.ds(1, 1)])

        @pl.when(lax.axis_index("elem") <= hub)
        def _():
            current = [-whole(w_ref[place.at("panel", slabs - 1, k)]) for k in range(modes)]
            for j in range(slabs - 2, -1, -1):
                steps = [
                    product(band_buf[0, j + 1] + lam[k] * band_buf[1, j + 1], w_ref[place.at("panel", j, k)]) for k in range(modes)
                ]
                current = [-product(current[k], wide(steps[k])) for k in range(modes)]
            for k in range(modes):
                back_buf[pl.ds(k * size, size)] = wide(product(current[k], wide(band_buf[0, 0] + lam[k] * band_buf[1, 0])))
            for copy in start_copies([(back_buf, back_ref)], sems):
                copy.wait()

        pltpu.make_async_copy(front_buf, front_ref, sems.at[1]).wait()

    @pl.when(lax.axis_index("elem") == lax.axis_size("elem") - 1)
    def _():
        behind_maps(behind_buf, band_buf, [wave_of(k, mode_total, modes) for k in range(modes)], w_ref, place)
        for copy in start_copies([(behind_buf, behind_ref)], sems):
            copy.wait()


def face_push(values, weight, lam):
    rows, size = values.shape
    high, low = split(values)
    blocks = [weight[:, i * size : (i + 1) * size] for i in range(4)]
    out = dot(
        jnp.concatenate([high, low], axis=0), jnp.concatenate(blocks, axis=0), NT
    )
    out = out[:rows, : 2 * size] + out[:rows, 2 * size :] + out[rows:, : 2 * size]
    return out[:, :size] + lam * out[:, size:]


def face_lift(values, weight, lam):
    rows, size = values.shape
    out = folded(dot(tall(values), weight), rows)
    return out[:, :size] + lam * out[:, size:]


def block_of(spec_ref, index, size):
    per = spec_ref.shape[2] // size
    at = index % per * size
    return spec_ref[index // per, :, at : at + size]


def band_step(values, weight, lam):
    return face_push(values, weight, lam)


def inner_kernel(modes, mode_total, place, hub, first_call, band_ref, front_ref, behind_ref, *refs):
    elem = lax.axis_index("elem")
    if first_call:
        spec_ref, w_ref, reig_ref, axial_ref, weight_ref, aeig_ref, zsrc_ref, inv_ref, reduced_ref, y_ref, send_ref = refs
    else:
        spec_ref, w_ref, reig_ref = refs[:3]
        axial_ref, weight_ref, aeig_ref, zsrc_ref, inv_ref, reduced_ref, y_ref, load_ref, front_out, band_buf, behind_buf, sems = refs[7:]
        inside = (elem > 0) & (elem <= hub)
        early = (front_ref, front_out)
        late = [(band_ref.at[:, 0], band_buf), (behind_ref, behind_buf)]

        @pl.when(inside)
        def _():
            start_copies([early], sems.at[pl.ds(1, 1)])

        @pl.when(elem == lax.axis_size("elem") - 1)
        def _():
            start_copies(late, sems)

    @pl.when((elem == 0) == first_call)
    def _():
        load, values = inner_part(
            modes, mode_total, place, spec_ref, w_ref, reig_ref, axial_ref, weight_ref, aeig_ref, zsrc_ref, inv_ref, reduced_ref, y_ref
        )
        if first_call:
            send_ref[...] = values[-1]
            return
        load_ref[1] = load

        @pl.when(inside)
        def _():
            pltpu.make_async_copy(*early, sems.at[1]).wait()

        @pl.when(elem == lax.axis_size("elem") - 1)
        def _():
            lam = wave(mode_total, load.shape, modes)
            current = values[-1]
            for i, pair in enumerate(late):
                pltpu.make_async_copy(*pair, sems.at[i]).wait()
            for j in range(len(values) - 2, -1, -1):
                current = values[j] - apply(current, behind_buf[j], modes)
            load_ref[0] = load + face_lift(current, band_wide(band_buf[0], band_buf[1]), lam)


def inner_part(
    modes, mode_total, place, spec_ref, w_ref, reig_ref, axial_ref, weight_ref, aeig_ref, zsrc_ref, inv_ref, solved_ref, y_ref
):
    slabs, inner, rows, size = zsrc_ref.shape
    lam = wave(mode_total, (rows, size), modes)
    pushed = []
    for j in range(slabs):
        source = jnp.concatenate(
            [block_of(spec_ref, j * (inner + 1) + a, size) for a in range(inner)], axis=0
        )
        first = product(source, w_ref[place.at("radial", j)])
        first = [first[a * rows : (a + 1) * rows] for a in range(inner)]
        sums = [None, None]
        for b in range(inner):
            value = first[0] * axial_ref[j, 0, b]
            for a in range(1, inner):
                value = value + first[a] * axial_ref[j, a, b]
            inverse = 1.0 / (aeig_ref[j, b] + reig_ref[j : j + 1] + lam)
            inv_ref[j, b] = inverse
            value = value * inverse
            zsrc_ref[j, b] = value
            for side in range(2):
                term = value * weight_ref[j, side, b]
                sums[side] = term if sums[side] is None else sums[side] + term
        pushed.append([face_push(sums[side], place.face(w_ref, j, side), lam) for side in range(2)])
    load = pushed[0][0]
    values = []
    for j in range(slabs):
        reduced = block_of(spec_ref, j * (inner + 1) + inner, size) - pushed[j][1]
        if j + 1 < slabs:
            reduced = reduced - pushed[j + 1][0]
        panel = w_ref[place.at("panel", j)]
        solved_ref[j] = reduced
        if j > 0:
            reduced = reduced - band_step(values[-1], place.band(w_ref, j), lam)
        values.append(apply(reduced, panel, modes))
        y_ref[j] = values[j]
    return load, values


def previous_weight(panel_ref, modes):
    parts = [split(panel_ref[k]) for k in range(modes)]
    return jnp.concatenate(
        [jnp.concatenate([p[i] for p in parts], axis=1) for i in range(2)], axis=0
    )


def apply_nt(x, weight, modes):
    return folded(dot(by_mode(x, modes), weight, NT), x.shape[0])


def backward_values(values, after, panel, behind_ref, modes):
    slabs = len(values)
    out = [None] * slabs
    out[-1] = values[-1]
    if after is not None:
        out[-1] = out[-1] - apply(after, panel, modes)
    for j in range(slabs - 2, -1, -1):
        out[j] = values[j] - apply(out[j + 1], behind_ref[j], modes)
    return out


def push_kernel(modes, first_ref, load_ref, prev_ref, push_ref, prev_buf, sems):
    @pl.when(lax.axis_index("elem") == 1)
    def _():
        for copy in start_copies([(first_ref, prev_buf)], sems):
            copy.wait()
        weight = previous_weight(prev_buf, modes)
        prev_ref[...] = weight
        push_ref[...] = apply_nt(load_ref[1], weight, modes)


def forward_kernel(modes, at, got_ref, push_ref, y_ref, front_ref, old_ref, state_ref, send_ref):
    @pl.when(lax.axis_index("elem") == at)
    def _():
        before = got_ref[...] - push_ref[...]
        state_ref[0] = before
        send_ref[...] = y_ref[y_ref.shape[0] - 1] + apply(before, front_ref[...], modes)


def base_kernel(
    modes, mode_total, hub, place, band_ref, map_ref, state_ref, load_ref, reduced_ref, y_ref, w_ref,
    base_ref, found_ref, back_ref, band_buf, sems,
):
    elem = lax.axis_index("elem")
    slabs, rows, size = reduced_ref.shape
    lam = wave(mode_total, (rows, size), modes)

    @pl.when((elem > 0) & (elem < hub))
    def _():
        copies = start_copies([(band_ref.at[:, 0], band_buf), (map_ref, back_ref)], sems)
        copies[0].wait()
        first = band_wide(band_buf[0], band_buf[1])
        bands = [first] + [place.band(w_ref, j) for j in range(1, slabs)]
        panels = [w_ref[place.at("panel", j)] for j in range(slabs)]
        values = []
        for j in range(slabs):
            step = face_push(values[-1] if j > 0 else state_ref[0], bands[j], lam)
            values.append(apply(reduced_ref[j] - step, panels[j], modes))
        found = values[-1]
        found_ref[slabs - 1] = found
        for j in range(slabs - 2, -1, -1):
            found = values[j] - apply(face_lift(found, bands[j + 1], lam), panels[j], modes)
            found_ref[j] = found
        base_ref[...] = load_ref[1] + face_lift(found, first, lam)
        copies[1].wait()


def ahead_maps(ahead_ref, band_buf, waves, w_ref, place):
    slabs, many, _ = ahead_ref.shape
    for j in range(slabs):
        first, second = band_buf[0, j].T, band_buf[1, j].T
        for k, lam in enumerate(waves):
            ahead_ref[j, pl.ds(k * place.size, place.size)] = wide(product(first + lam * second, w_ref[place.at("panel", j, k)]))


def behind_maps(behind_ref, band_buf, waves, w_ref, place):
    for j in range(behind_ref.shape[0]):
        for k, lam in enumerate(waves):
            step = product(band_buf[0, j + 1] + lam * band_buf[1, j + 1], w_ref[place.at("panel", j, k)])
            behind_ref[j, pl.ds(k * place.size, place.size)] = wide(step)


def hub_map_kernel(
    modes, mode_total, hub, place, map_ref, pprev_ref, band_ref, given_ref, load_ref, y_ref, w_ref, front_ref, old_prev_ref, old_push_ref,
    prev_ref, push_ref, ahead_ref, behind_ref, back_ref, base_ref, cross_ref, far_ref, band_buf, map_buf, prev_buf, sems,
):
    slabs, rows, size = y_ref.shape
    lam = wave(mode_total, (rows, size), modes)
    inside = (lax.axis_index("elem") > 1) & (lax.axis_index("elem") <= hub)

    @pl.when(inside)
    def _():
        start_copies([(pprev_ref, prev_buf)], sems.at[pl.ds(2, 1)])

    @pl.when(lax.axis_index("elem") == hub)
    def _():
        copies = start_copies([(band_ref, band_buf), (map_ref, map_buf)], sems)
        given = start_copies([(given_ref, back_ref)], sems.at[pl.ds(3, 1)])[0]
        waves = [wave_of(k, mode_total, modes) for k in range(modes)]

        def part(k):
            return pl.ds(k * size, size)

        copies[0].wait()
        ahead_maps(ahead_ref, band_buf, waves, w_ref, place)
        behind_maps(behind_ref, band_buf, waves, w_ref, place)
        entry = [wide(band_buf[0, 0] + waves[k] * band_buf[1, 0]) for k in range(modes)]
        forward = [[-whole(ahead_ref[0, part(k)]) for k in range(modes)]]
        for j in range(1, slabs - 1):
            forward.append([-product(forward[-1][k], ahead_ref[j, part(k)]) for k in range(modes)])
        cross = [whole(front_ref[part(k)]) for k in range(modes)]
        for j in range(slabs - 2, -1, -1):
            cross = [forward[j][k] - product(cross[k], behind_ref[j, part(k)]) for k in range(modes)]
        for k in range(modes):
            cross_ref[part(k)] = wide(product(cross[k], entry[k]))
        found = backward_values([y_ref[j] for j in range(slabs)], None, None, behind_ref, modes)
        base_ref[...] = load_ref[1] + face_lift(found[0], band_wide(band_buf[0, 0], band_buf[1, 0]), lam)
        copies[1].wait()
        far_ref[...] = previous_weight(map_buf, modes)
        given.wait()

    @pl.when(inside)
    def _():
        pltpu.make_async_copy(pprev_ref, prev_buf, sems.at[2]).wait()
        weight = previous_weight(prev_buf, modes)
        prev_ref[...] = weight
        push_ref[...] = apply_nt(load_ref[1], weight, modes)


def hub_kernel(
    modes, at, place, got_ref, push_ref, far_ref, far_weight_ref, y_ref, front_ref, back_ref, cross_ref, base_ref, w_ref, old_ref,
    state_ref, send_ref, last_ref,
):
    slabs = y_ref.shape[0]

    @pl.when(lax.axis_index("elem") == at)
    def _():
        panel = w_ref[place.at("panel", slabs - 1)]
        load = apply(far_ref[1], panel, modes)
        before = got_ref[...] - push_ref[...]
        state_ref[0] = before
        value = y_ref[slabs - 1] + apply(before, front_ref[...], modes)
        out = base_ref[...] + apply(before, cross_ref[...], modes)
        final = value - load
        after = far_ref[0] + apply_nt(final, far_weight_ref[...], modes)
        state_ref[1] = after
        send_ref[...] = out + apply(after, back_ref[...], modes)
        last_ref[0] = final
        last_ref[1] = value - apply(after, panel, modes)


def own_map_kernel(
    modes, mode_total, hub, place, band_ref, radial_ref, state_ref, reduced_ref, y_ref, w_ref, front_ref, prev_ref, ahead_ref, behind_ref, old_ref,
    found_ref, own_ref, before_ref, radt_ref, ahead_buf, behind_buf, band_buf, radial_buf, sems,
):
    slabs, rows, size = reduced_ref.shape
    elem, last = lax.axis_index("elem"), lax.axis_size("elem") - 1
    lam = wave(mode_total, (rows, size), modes)
    waves = [wave_of(k, mode_total, modes) for k in range(modes)]
    copies = start_copies([(band_ref, band_buf), (radial_ref, radial_buf)], sems)

    def part(k):
        return pl.ds(k * size, size)

    copies[0].wait()

    @pl.when(elem == hub)
    def _():
        panels = [w_ref[place.at("panel", j)] for j in range(slabs)]
        before, values = state_ref[0], []
        for j in range(slabs):
            if j == slabs - 1:
                values.append(y_ref[j] + apply(before, front_ref[...], modes))
                continue
            solved = apply(reduced_ref[j], panels[j], modes)
            values.append(solved - apply(values[-1] if j > 0 else before, ahead_ref[j], modes))
        found = backward_values(values, state_ref[1], panels[-1], behind_ref, modes)
        for j in range(slabs):
            found_ref[j] = found[j]
        back = face_lift(found[0], band_wide(band_buf[0, 0], band_buf[1, 0]), lam)
        before_ref[...] = before - apply_nt(back, prev_ref[...], modes)

    @pl.when(elem != hub)
    def _():
        behind_maps(behind_buf, band_buf, waves, w_ref, place)

    @pl.when(elem < hub)
    def _():
        current = [-whole(w_ref[place.at("panel", slabs - 1, k)]) for k in range(modes)]
        for k in range(modes):
            own_ref[slabs - 1, part(k)] = -w_ref[place.at("panel", slabs - 1, k)]
        for j in range(slabs - 2, -1, -1):
            current = [-product(current[k], behind_buf[j, part(k)]) for k in range(modes)]
            for k in range(modes):
                own_ref[j, part(k)] = wide(current[k])

    @pl.when(elem == last)
    def _():
        ahead_maps(ahead_buf, band_buf, waves, w_ref, place)
        forward = [[-whole(ahead_buf[0, part(k)]) for k in range(modes)]]
        for j in range(1, slabs):
            forward.append([-product(forward[-1][k], ahead_buf[j, part(k)]) for k in range(modes)])
        current = forward[-1]
        for k in range(modes):
            own_ref[slabs - 1, part(k)] = wide(current[k])
        for j in range(slabs - 2, -1, -1):
            current = [forward[j][k] - product(current[k], behind_buf[j, part(k)]) for k in range(modes)]
            for k in range(modes):
                own_ref[j, part(k)] = wide(current[k])

    @pl.when((elem == 0) | (elem == last))
    def _():
        found = backward_values([y_ref[j] for j in range(slabs)], None, None, behind_buf, modes)
        for j in range(slabs):
            found_ref[j] = found[j]

    copies[1].wait()
    for j in range(slabs):
        radt_ref[j] = wide(radial_buf[j].T)


def backward_kernel(modes, at, got_ref, base_ref, back_ref, old_ref, state_ref, send_ref):
    @pl.when(lax.axis_index("elem") == at)
    def _():
        after = got_ref[...]
        state_ref[1] = after
        send_ref[...] = base_ref[...] + apply(after, back_ref[...], modes)


def final_kernel(
    modes, mode_total, hub, place, zsrc_ref, inv_ref, state_ref, got_ref, base_ref, last_ref, load_ref, found_ref, own_ref, back_ref, before_ref, prev_ref, w_ref, radt_ref, axial_ref, weight_ref,
    out_ref, x_ref, out_buf, sems,
):
    slabs, inner, rows, size = zsrc_ref.shape
    lam = wave(mode_total, (rows, size), modes)
    elem, last = lax.axis_index("elem"), lax.axis_size("elem") - 1

    def values(given):
        for j in range(slabs):
            x_ref[j + 1] = found_ref[j] + apply(given, own_ref[j], modes)

    @pl.when(elem == 0)
    def _():
        x_ref[0] = jnp.zeros((rows, size), F32)
        values(got_ref[...])

    @pl.when((elem > 0) & (elem < hub))
    def _():
        after = state_ref[1]
        values(after)
        back = base_ref[...] - load_ref[1] + apply(after, back_ref[...], modes)
        x_ref[0] = state_ref[0] - apply_nt(back, prev_ref[...], modes)

    @pl.when(elem == hub)
    def _():
        for j in range(slabs):
            x_ref[j + 1] = found_ref[j]
        x_ref[0] = before_ref[...]

    @pl.when(elem == last)
    def _():
        values(last_ref[0])
        x_ref[0] = last_ref[1]

    copies = []
    for j in range(slabs):
        lifted = [face_lift(x_ref[j + side], place.face(w_ref, j, side), lam) for side in range(2)]
        kept = []
        for b in range(inner):
            total = lifted[0] * weight_ref[j, 0, b] + lifted[1] * weight_ref[j, 1, b]
            kept.append(zsrc_ref[j, b] - total * inv_ref[j, b])
        values = []
        for a in range(inner):
            value = kept[0] * axial_ref[j, a, 0]
            for b in range(1, inner):
                value = value + kept[b] * axial_ref[j, a, b]
            values.append(value)
        result = product(jnp.concatenate(values, axis=0), radt_ref[j])
        for a in range(inner):
            out_buf[j, :, a * size : (a + 1) * size] = result[a * rows : (a + 1) * rows]
        out_buf[j, :, inner * size :] = x_ref[j + 1]
        width = (inner + 1) * size
        copies += start_copies([(out_buf.at[j], out_ref.at[:, pl.ds(j * width, width)])], sems.at[pl.ds(j, 1)])
    for copy in copies:
        copy.wait()


def dft_table(planes):
    row, col = np.arange(planes)[:, None], np.arange(planes)[None]
    angle = row // 2 * col % planes * (2.0 * math.pi / planes)
    table = np.where(row % 2 == 0, np.cos(angle), -np.sin(angle)) / math.sqrt(planes)
    table = jnp.asarray(table, F32)
    high, low = split(table)
    return jnp.concatenate([high, low, high], axis=1)


def body(
    rhs_phys, radial_basis, axial_basis, radial_eig, axial_eig, face_stiff, face_mass, axial_coupling, face_numbering,
    band_panels, inverse_panels,
):
    planes, nodes = rhs_phys.shape
    modes, slabs, size, _ = inverse_panels.shape
    inner = axial_basis.shape[1]
    devices = lax.axis_size("mode")
    elems = lax.axis_size("elem")
    mode_total = modes * devices
    rows = 2 * modes
    hub = elems - 2
    last = elems - 1

    def shape(*dims):
        return jax.ShapeDtypeStruct(dims, F32)

    def kept(*dims):
        return pltpu.VMEM(dims, F32)

    def half(*dims):
        return pltpu.VMEM(dims, BF16)

    table = dft_table(planes)
    many = modes * size
    place = Weights(size, ("panel", slabs, many), ("radial", slabs, size), ("face", 4 * slabs, size), ("band", 2 * (slabs - 1), size))
    buffers = [pltpu.VMEM((planes, nodes), F32), pltpu.VMEM(table.shape, BF16), pltpu.SemaphoreType.DMA((slabs + 3,))]
    whole_spectrum = pltpu.HBM((planes, nodes), F32)
    whole_panels = pltpu.HBM((modes, size, size), F32)
    panels_buffer = pltpu.VMEM((modes, size, size), F32)
    ship, spectrum = call(
        functools.partial(ends_kernel, modes, mode_total),
        [whole_panels, whole_spectrum],
        [inverse_panels, band_panels, rhs_phys, table],
        anywhere=4,
        scratch=[pltpu.VMEM((slabs, modes, size, size), F32), pltpu.VMEM(band_panels.shape, F32), panels_buffer] + buffers,
    )
    if hub > 1:
        first = far_map = lax.ppermute(ship, "elem", [(0, 1), (last, hub)])
    else:
        first, far_map = lax.ppermute(ship, "elem", [(0, 1)]), lax.ppermute(ship, "elem", [(last, hub)])
    ship, spectrum = call(
        functools.partial(between_kernel, hub),
        [whole_panels, whole_spectrum],
        [inverse_panels, rhs_phys, table, spectrum],
        anywhere=4,
        scratch=[panels_buffer] + buffers,
        aliases={3: 1},
    )
    pprev = lax.ppermute(ship, "elem", [(i, i + 1) for i in range(1, hub)]) if hub > 1 else first
    spectrum = call(
        functools.partial(late_kernel, hub),
        [whole_spectrum],
        [rhs_phys, table, spectrum],
        anywhere=3,
        scratch=buffers,
        aliases={2: 0},
    )[0]
    spectrum = lax.all_to_all(spectrum.reshape(devices, rows, nodes), "mode", 0, 0, tiled=False)
    if nodes % size:
        spectrum = jnp.swapaxes(spectrum, 0, 1).reshape(1, rows, devices * nodes)
    vector = (rows, size)
    matrix = half(many, 2 * size)
    front, back_map, later, w, reig, axial, weight, aeig = call(
        functools.partial(maps_kernel, modes, mode_total, hub, place),
        [
            pltpu.HBM((many, 2 * size), BF16),
            pltpu.HBM((many, 2 * size), BF16),
            pltpu.HBM((slabs - 1, many, 2 * size), BF16),
            half(place.total, 2 * size),
            kept(*radial_eig.shape),
            pltpu.SMEM(axial_basis.shape, F32),
            pltpu.SMEM((slabs, 2, inner), F32),
            pltpu.SMEM(axial_eig.shape, F32),
        ],
        [
            inverse_panels, band_panels, radial_basis, face_stiff, face_mass, face_numbering,
            radial_eig, axial_basis, axial_eig, axial_coupling,
        ],
        anywhere=10,
        outside=3,
        scratch=[
            pltpu.VMEM((slabs, modes, size, size), F32),
            pltpu.VMEM(band_panels.shape, F32),
            pltpu.VMEM(radial_basis.shape, F32),
            pltpu.VMEM(face_stiff.shape, F32),
            pltpu.VMEM(face_mass.shape, F32),
            pltpu.VMEM(face_numbering.shape, jnp.int32),
            pltpu.SMEM(axial_basis.shape, F32),
            pltpu.SMEM(axial_coupling.shape, F32),
            pltpu.VMEM((many, 2 * size), BF16),
            pltpu.VMEM((many, 2 * size), BF16),
            pltpu.VMEM((slabs - 1, many, 2 * size), BF16),
            pltpu.SemaphoreType.DMA((slabs + 9,)),
        ],
    )
    solves = [kept(slabs, inner, *vector), kept(slabs, inner, *vector), kept(slabs, *vector), kept(slabs, *vector)]
    *solve, send = call(
        functools.partial(inner_kernel, modes, mode_total, place, hub, True),
        solves + [kept(*vector)],
        [band_panels, front, later, spectrum, w, reig, axial, weight, aeig],
        anywhere=3,
        smem=3,
    )
    got = lax.ppermute(send, "elem", [(0, 1)])
    zsrc, inv, reduced, y, load, front = call(
        functools.partial(inner_kernel, modes, mode_total, place, hub, False),
        solves + [kept(2, *vector), matrix],
        [band_panels, front, later, spectrum, w, reig, *solve, axial, weight, aeig],
        anywhere=3,
        smem=3,
        scratch=[
            pltpu.VMEM((2, size, size), F32),
            pltpu.VMEM((slabs - 1, many, 2 * size), BF16),
            pltpu.SemaphoreType.DMA((2,)),
        ],
        aliases={6 + i: i for i in range(4)},
    )
    far = lax.ppermute(load, "elem", [(last, hub)])
    prev, push = call(
        functools.partial(push_kernel, modes),
        [half(2 * size, many), kept(*vector)],
        [first, load],
        free=1,
        scratch=[panels_buffer, pltpu.SemaphoreType.DMA((1,))],
    )
    prev, later_push, ahead, behind, hub_back, hub_base, cross, far_weight = call(
        functools.partial(hub_map_kernel, modes, mode_total, hub, place),
        [
            half(2 * size, many), kept(*vector), half(slabs - 1, many, 2 * size), half(slabs - 1, many, 2 * size), matrix,
            kept(*vector), matrix, half(2 * size, many),
        ],
        [far_map, pprev, band_panels, back_map, load, y, w, front, prev, push],
        free=2,
        anywhere=2,
        scratch=[pltpu.VMEM(band_panels.shape, F32), panels_buffer, panels_buffer, pltpu.SemaphoreType.DMA((4,))],
        aliases={8: 0, 9: 1},
    )
    state = jnp.zeros((2, *vector), F32)
    for at in range(1, hub):
        state, send = call(
            functools.partial(forward_kernel, modes, at),
            [kept(*state.shape), shape(*vector)],
            [got, push if at == 1 else later_push, y, front, state],
            aliases={4: 0},
        )
        got = lax.ppermute(send, "elem", [(at, at + 1)])
    state, send, final = call(
        functools.partial(hub_kernel, modes, hub, place),
        [kept(*state.shape), shape(*vector), shape(2, *vector)],
        [got, push if hub == 1 else later_push, far, far_weight, y, front, hub_back, cross, hub_base, w, state],
        aliases={10: 0},
    )
    base, found, back = call(
        functools.partial(base_kernel, modes, mode_total, hub, place),
        [kept(*vector), kept(slabs, *vector), matrix],
        [band_panels, back_map, state, load, reduced, y, w],
        anywhere=2,
        scratch=[pltpu.VMEM((2, size, size), F32), pltpu.SemaphoreType.DMA((2,))],
    )
    for at in range(hub - 1, 0, -1):
        got = lax.ppermute(send, "elem", [(at + 1, at)])
        state, send = call(
            functools.partial(backward_kernel, modes, at),
            [kept(*state.shape), shape(*vector)],
            [got, base, back, state],
            aliases={3: 0},
        )
    got = lax.ppermute(send, "elem", [(1, 0)])
    found, own, before, radt = call(
        functools.partial(own_map_kernel, modes, mode_total, hub, place),
        [kept(slabs, *vector), half(slabs, many, 2 * size), kept(*vector), half(slabs, size, 2 * size)],
        [band_panels, radial_basis, state, reduced, y, w, front, prev, ahead, behind, found],
        anywhere=2,
        scratch=[
            pltpu.VMEM((slabs, many, 2 * size), BF16),
            pltpu.VMEM((slabs - 1, many, 2 * size), BF16),
            pltpu.VMEM(band_panels.shape, F32),
            pltpu.VMEM(radial_basis.shape, F32),
            pltpu.SemaphoreType.DMA((2,)),
        ],
        aliases={10: 0},
    )
    final = lax.ppermute(final, "elem", [(hub, last)])
    return call(
        functools.partial(final_kernel, modes, mode_total, hub, place),
        [pltpu.HBM((rows, slabs * (inner + 1) * size), F32)],
        [
            zsrc, inv, state, got, base, final, load, found, own, back, before, prev, w, radt, axial, weight,
        ],
        smem=2,
        scratch=[
            pltpu.VMEM((slabs + 1, *vector), F32),
            pltpu.VMEM((slabs, rows, (inner + 1) * size), F32),
            pltpu.SemaphoreType.DMA((slabs,)),
        ],
    )[0]


def solution(mesh):
    placed = (
        P(None, ("elem", "mode")),
        P("elem", None, None),
        P("elem", None, None),
        P("elem", None),
        P("elem", None),
        P("elem", None, None),
        P("elem", None, None),
        P("elem", None, None),
        P("elem", None, None),
        P(None, "elem", None, None),
        P("mode", "elem", None, None),
    )
    return jax.shard_map(
        body, mesh=mesh, in_specs=placed, out_specs=P("mode", "elem"), check_vma=False
    )
```

```python
import functools
import math

import jax
import jax.numpy as jnp
import numpy as np
from jax import lax
from jax.experimental import pallas as pl
from jax.experimental.pallas import tpu as pltpu
from jax.sharding import PartitionSpec as P

F32 = jnp.float32
BF16 = jnp.bfloat16
VMEM = pl.BlockSpec(memory_space=pltpu.VMEM)
SMEM = pl.BlockSpec(memory_space=pltpu.SMEM)
HBM = pl.BlockSpec(memory_space=pltpu.HBM)
ANY = pl.BlockSpec(memory_space=pl.ANY)
NN = (((1,), (0,)), ((), ()))
NT = (((1,), (1,)), ((), ()))


def call(kernel, outs, args, smem=0, anywhere=0, free=0, outside=0, scratch=(), aliases=None):
    inside = len(args) - smem - anywhere - free
    spaces = [None] * free + [pltpu.HBM] * anywhere + [pltpu.VMEM] * inside + [pltpu.SMEM] * smem
    args = [arg if space is None else pltpu.with_memory_space_constraint(arg, space) for arg, space in zip(args, spaces)]
    return pl.pallas_call(
        kernel,
        out_shape=outs,
        in_specs=[ANY] * free + [HBM] * anywhere + [VMEM] * inside + [SMEM] * smem,
        out_specs=[HBM if getattr(out, "memory_space", None) is pltpu.HBM else VMEM for out in outs[: len(outs) - outside]]
        + [SMEM] * outside,
        scratch_shapes=scratch,
        input_output_aliases=aliases or {},
        compiler_params=pltpu.CompilerParams(vmem_limit_bytes=16 * 2**20),
    )(*args)


def split(x):
    high = x.astype(BF16)
    return high, (x - high.astype(F32)).astype(BF16)


def dot(a, b, dims=NN):
    return lax.dot_general(a, b, dims, preferred_element_type=F32)


def wide(x):
    return jnp.concatenate(split(x), axis=1)


def tall(x):
    return jnp.concatenate(split(x), axis=0)


def product(left, right):
    size = right.shape[1] // 2
    out = dot(wide(left), jnp.concatenate([right, right], axis=0))
    return out[:, :size] + out[:, size:]


def by_mode(x, modes):
    mode_of = lax.broadcasted_iota(jnp.int32, x.shape, 0) // 2
    spread = jnp.concatenate([jnp.where(mode_of == k, x, 0.0) for k in range(modes)], axis=1)
    return tall(spread)


def folded(out, rows):
    size = out.shape[1] // 2
    return out[:rows, :size] + out[:rows, size:] + out[rows:, :size]


def apply(x, weight, modes):
    return folded(dot(by_mode(x, modes), weight), x.shape[0])


def wave(mode_total, shape, modes, axis=0):
    first = lax.axis_index("mode") * modes
    index = first + lax.broadcasted_iota(jnp.int32, shape, axis) // 2
    number = index.astype(F32) / mode_total
    return 4.0 * number * number


def wave_of(k, mode_total, modes):
    number = (jnp.full((1, 1), lax.axis_index("mode") * modes + k, jnp.int32)).astype(F32) / mode_total
    return 4.0 * number * number


class Weights:
    def __init__(self, size, *entries):
        self.size, self.rows, self.counts = size, {}, {}
        self.total = 0
        for name, count, rows in entries:
            self.rows[name], self.counts[name] = (self.total, rows), count
            self.total += count * rows

    def at(self, name, index, mode=None):
        start, rows = self.rows[name]
        if mode is None:
            return pl.ds(start + index * rows, rows)
        return pl.ds(start + index * rows + mode * self.size, self.size)

    def pair(self, ref, name, index):
        return jnp.concatenate([ref[self.at(name, index)], ref[self.at(name, index + 1)]], axis=1)

    def band(self, ref, slab):
        return self.pair(ref, "band", 2 * (slab - 1))

    def face(self, ref, slab, side):
        return self.pair(ref, "face", 4 * slab + 2 * side)


def band_wide(stiff, mass):
    return wide(jnp.concatenate([stiff, mass], axis=1))


def whole(weight):
    size = weight.shape[1] // 2
    value = weight.astype(F32)
    return value[:, :size] + value[:, size:]


def start_copies(pairs, sems):
    copies = [pltpu.make_async_copy(src, dst, sems.at[i]) for i, (src, dst) in enumerate(pairs)]
    for copy in copies:
        copy.start()
    return copies


def transform(rhs_ref, table_ref, out_ref, rhs_buf, table_buf, sems, started=None):
    for copy in started or start_copies([(rhs_ref, rhs_buf), (table_ref, table_buf)], sems):
        copy.wait()
    high, low = split(rhs_buf[...])
    rhs_buf[...] = dot(table_buf[...], jnp.concatenate([high, high, low], axis=0))
    return start_copies([(rhs_buf, out_ref)], sems)[0]


def panels_and_transform(panels_ref, ship_ref, rhs_ref, table_ref, out_ref, ship_buf, rhs_buf, table_buf, sems):
    half = ship_buf.shape[0] // 2
    parts = [pl.ds(0, half), pl.ds(half, ship_buf.shape[0] - half)]
    fetch = start_copies([(panels_ref.at[part, panels_ref.shape[1] - 1], ship_buf.at[part]) for part in parts], sems.at[pl.ds(2, 2)])
    result = transform(rhs_ref, table_ref, out_ref, rhs_buf, table_buf, sems)
    ship = []
    for i, part in enumerate(parts):
        fetch[i].wait()
        ship += start_copies([(ship_buf.at[part], ship_ref.at[part])], sems.at[pl.ds(2 + i, 1)])
    for copy in [result] + ship:
        copy.wait()


def ends_kernel(
    modes, mode_total, panels_ref, band_ref, rhs_ref, table_ref, ship_ref, out_ref,
    panels_buf, band_buf, ship_buf, rhs_buf, table_buf, sems,
):
    slabs, size = panels_ref.shape[1:3]
    elem, last = lax.axis_index("elem"), lax.axis_size("elem") - 1

    @pl.when(elem == 0)
    def _():
        panels_and_transform(panels_ref, ship_ref, rhs_ref, table_ref, out_ref, ship_buf, rhs_buf, table_buf, sems)

    @pl.when(elem == last)
    def _():
        copies = start_copies(
            [(band_ref, band_buf)] + [(panels_ref.at[:, j], panels_buf.at[j]) for j in range(slabs)],
            sems.at[pl.ds(2, slabs + 1)],
        )
        started = start_copies([(rhs_ref, rhs_buf), (table_ref, table_buf)], sems)
        copies[0].wait()
        band_t = [(band_buf[0, j].T, band_buf[1, j].T) for j in range(slabs)]
        lam = [wave_of(k, mode_total, modes) for k in range(modes)]
        forward = []
        for j in range(slabs):
            copies[1 + j].wait()
            steps = [
                product(panels_buf[j, k], wide(band_buf[0, j] + lam[k] * band_buf[1, j])) for k in range(modes)
            ]
            if j == 0:
                forward.append([-step for step in steps])
            else:
                forward.append([-product(steps[k], wide(forward[-1][k])) for k in range(modes)])
        current = forward[-1]
        for j in range(slabs - 2, -1, -1):
            steps = [
                product(panels_buf[j, k], wide(band_t[j + 1][0] + lam[k] * band_t[j + 1][1])) for k in range(modes)
            ]
            current = [forward[j][k] - product(steps[k], wide(current[k])) for k in range(modes)]
        ship = [transform(rhs_ref, table_ref, out_ref, rhs_buf, table_buf, sems, started)]
        half = modes // 2
        for i, part in enumerate((range(half), range(half, modes))):
            for k in part:
                ship_buf[k] = product(band_t[0][0] + lam[k] * band_t[0][1], wide(current[k]))
            rows = pl.ds(part.start, len(part))
            ship += start_copies([(ship_buf.at[rows], ship_ref.at[rows])], sems.at[pl.ds(2 + i, 1)])
        for copy in ship:
            copy.wait()


def between_kernel(hub, panels_ref, rhs_ref, table_ref, old_ref, ship_ref, out_ref, ship_buf, rhs_buf, table_buf, sems):
    elem = lax.axis_index("elem")

    @pl.when((elem > 0) & (elem < hub))
    def _():
        panels_and_transform(panels_ref, ship_ref, rhs_ref, table_ref, out_ref, ship_buf, rhs_buf, table_buf, sems)


def late_kernel(hub, rhs_ref, table_ref, old_ref, out_ref, rhs_buf, table_buf, sems):
    @pl.when(lax.axis_index("elem") == hub)
    def _():
        transform(rhs_ref, table_ref, out_ref, rhs_buf, table_buf, sems).wait()


def maps_kernel(
    modes, mode_total, hub, place, panels_ref, band_ref, radial_ref, stiff_ref, mass_ref, number_ref, reig_ref, axial_ref, aeig_ref,
    coup_ref, front_ref, back_ref, behind_ref, w_ref, reig_out, axial_out, weight_out, aeig_out,
    panels_buf, band_buf, radial_buf, stiff_buf, mass_buf, number_buf, axial_buf, coup_buf, front_buf, back_buf, behind_buf, sems,
):
    slabs, size = panels_ref.shape[1:3]
    inner = aeig_ref.shape[1]
    copies = start_copies(
        [(radial_ref, radial_buf), (stiff_ref, stiff_buf), (mass_ref, mass_buf), (number_ref, number_buf), (band_ref, band_buf)]
        + [(panels_ref.at[:, j], panels_buf.at[j]) for j in range(slabs)]
        + [(axial_ref, axial_buf), (coup_ref, coup_buf), (aeig_ref, aeig_out), (reig_ref, reig_out)],
        sems,
    )
    for copy in copies[:4]:
        copy.wait()
    for j in range(slabs):
        radial = wide(radial_buf[j])
        w_ref[place.at("radial", j)] = radial
        parts = [wide(product(ref[j].T, radial)) for ref in (stiff_buf, mass_buf)]
        for side in range(2):
            spot = lax.broadcasted_iota(jnp.int32, (size, size), 0)
            onehot = jnp.where(number_buf[j, side : side + 1] == spot, 1.0, 0.0).astype(BF16)
            for i in range(2):
                both = jnp.concatenate([p[:, i * size : (i + 1) * size] for p in parts], axis=1)
                w_ref[place.at("face", 4 * j + 2 * side + i)] = dot(onehot, both).astype(BF16)
    copies[4].wait()
    for j in range(1, slabs):
        bands = band_wide(band_buf[0, j], band_buf[1, j])
        for i in range(2):
            w_ref[place.at("band", 2 * (j - 1) + i)] = bands[:, 2 * i * size : 2 * (i + 1) * size]
    for j in range(slabs):
        copies[5 + j].wait()
        for k in range(modes):
            w_ref[place.at("panel", j, k)] = wide(panels_buf[j, k].T)
    for copy in copies[5 + slabs :]:
        copy.wait()
    for j in range(slabs):
        for b in range(inner):
            for a in range(inner):
                axial_out[j, a, b] = axial_buf[j, a, b]
            for side in range(2):
                weight = coup_buf[j, side, 0] * axial_buf[j, 0, b]
                for a in range(1, inner):
                    weight = weight + coup_buf[j, side, a] * axial_buf[j, a, b]
                weight_out[j, side, b] = weight

    @pl.when((lax.axis_index("elem") > 0) & (lax.axis_index("elem") <= hub))
    def _():
        lam = [wave_of(k, mode_total, modes) for k in range(modes)]
        current = None
        for j in range(slabs):
            first, second = band_buf[0, j].T, band_buf[1, j].T
            steps = [product(first + lam[k] * second, w_ref[place.at("panel", j, k)]) for k in range(modes)]
            if current is None:
                current = [-step for step in steps]
            else:
                current = [-product(current[k], wide(steps[k])) for k in range(modes)]
        for k in range(modes):
            front_buf[pl.ds(k * size, size)] = wide(current[k])
        start_copies([(front_buf, front_ref)], sems.at[pl.ds(1, 1)])

        @pl.when(lax.axis_index("elem") <= hub)
        def _():
            current = [-whole(w_ref[place.at("panel", slabs - 1, k)]) for k in range(modes)]
            for j in range(slabs - 2, -1, -1):
                steps = [
                    product(band_buf[0, j + 1] + lam[k] * band_buf[1, j + 1], w_ref[place.at("panel", j, k)]) for k in range(modes)
                ]
                current = [-product(current[k], wide(steps[k])) for k in range(modes)]
            for k in range(modes):
                back_buf[pl.ds(k * size, size)] = wide(product(current[k], wide(band_buf[0, 0] + lam[k] * band_buf[1, 0])))
            for copy in start_copies([(back_buf, back_ref)], sems):
                copy.wait()

        pltpu.make_async_copy(front_buf, front_ref, sems.at[1]).wait()

    @pl.when(lax.axis_index("elem") == lax.axis_size("elem") - 1)
    def _():
        behind_maps(behind_buf, band_buf, [wave_of(k, mode_total, modes) for k in range(modes)], w_ref, place)
        for copy in start_copies([(behind_buf, behind_ref)], sems):
            copy.wait()


def face_push(values, weight, lam):
    rows, size = values.shape
    high, low = split(values)
    blocks = [weight[:, i * size : (i + 1) * size] for i in range(4)]
    out = dot(
        jnp.concatenate([high, low], axis=0), jnp.concatenate(blocks, axis=0), NT
    )
    out = out[:rows, : 2 * size] + out[:rows, 2 * size :] + out[rows:, : 2 * size]
    return out[:, :size] + lam * out[:, size:]


def face_lift(values, weight, lam):
    rows, size = values.shape
    out = folded(dot(tall(values), weight), rows)
    return out[:, :size] + lam * out[:, size:]


def block_of(spec_ref, index, size):
    per = spec_ref.shape[2] // size
    at = index % per * size
    return spec_ref[index // per, :, at : at + size]


def band_step(values, weight, lam):
    return face_push(values, weight, lam)


def inner_kernel(modes, mode_total, place, hub, first_call, band_ref, front_ref, behind_ref, *refs):
    elem = lax.axis_index("elem")
    if first_call:
        spec_ref, w_ref, reig_ref, axial_ref, weight_ref, aeig_ref, zsrc_ref, inv_ref, reduced_ref, y_ref, send_ref = refs
    else:
        spec_ref, w_ref, reig_ref = refs[:3]
        axial_ref, weight_ref, aeig_ref, zsrc_ref, inv_ref, reduced_ref, y_ref, load_ref, front_out, band_buf, behind_buf, sems = refs[7:]
        inside = (elem > 0) & (elem <= hub)
        early = (front_ref, front_out)
        late = [(band_ref.at[:, 0], band_buf), (behind_ref, behind_buf)]

        @pl.when(inside)
        def _():
            start_copies([early], sems.at[pl.ds(1, 1)])

        @pl.when(elem == lax.axis_size("elem") - 1)
        def _():
            start_copies(late, sems)

    @pl.when((elem == 0) == first_call)
    def _():
        load, values = inner_part(
            modes, mode_total, place, spec_ref, w_ref, reig_ref, axial_ref, weight_ref, aeig_ref, zsrc_ref, inv_ref, reduced_ref, y_ref
        )
        if first_call:
            send_ref[...] = values[-1]
            return
        load_ref[1] = load

        @pl.when(inside)
        def _():
            pltpu.make_async_copy(*early, sems.at[1]).wait()

        @pl.when(elem == lax.axis_size("elem") - 1)
        def _():
            lam = wave(mode_total, load.shape, modes)
            current = values[-1]
            for i, pair in enumerate(late):
                pltpu.make_async_copy(*pair, sems.at[i]).wait()
            for j in range(len(values) - 2, -1, -1):
                current = values[j] - apply(current, behind_buf[j], modes)
            load_ref[0] = load + face_lift(current, band_wide(band_buf[0], band_buf[1]), lam)


def inner_part(
    modes, mode_total, place, spec_ref, w_ref, reig_ref, axial_ref, weight_ref, aeig_ref, zsrc_ref, inv_ref, solved_ref, y_ref
):
    slabs, inner, rows, size = zsrc_ref.shape
    lam = wave(mode_total, (rows, size), modes)
    pushed = []
    for j in range(slabs):
        source = jnp.concatenate(
            [block_of(spec_ref, j * (inner + 1) + a, size) for a in range(inner)], axis=0
        )
        first = product(source, w_ref[place.at("radial", j)])
        first = [first[a * rows : (a + 1) * rows] for a in range(inner)]
        sums = [None, None]
        for b in range(inner):
            value = first[0] * axial_ref[j, 0, b]
            for a in range(1, inner):
                value = value + first[a] * axial_ref[j, a, b]
            inverse = 1.0 / (aeig_ref[j, b] + reig_ref[j : j + 1] + lam)
            inv_ref[j, b] = inverse
            value = value * inverse
            zsrc_ref[j, b] = value
            for side in range(2):
                term = value * weight_ref[j, side, b]
                sums[side] = term if sums[side] is None else sums[side] + term
        pushed.append([face_push(sums[side], place.face(w_ref, j, side), lam) for side in range(2)])
    load = pushed[0][0]
    values = []
    for j in range(slabs):
        reduced = block_of(spec_ref, j * (inner + 1) + inner, size) - pushed[j][1]
        if j + 1 < slabs:
            reduced = reduced - pushed[j + 1][0]
        panel = w_ref[place.at("panel", j)]
        solved_ref[j] = reduced
        if j > 0:
            reduced = reduced - band_step(values[-1], place.band(w_ref, j), lam)
        values.append(apply(reduced, panel, modes))
        y_ref[j] = values[j]
    return load, values


def previous_weight(panel_ref, modes):
    parts = [split(panel_ref[k]) for k in range(modes)]
    return jnp.concatenate(
        [jnp.concatenate([p[i] for p in parts], axis=1) for i in range(2)], axis=0
    )


def apply_nt(x, weight, modes):
    return folded(dot(by_mode(x, modes), weight, NT), x.shape[0])


def backward_values(values, after, panel, behind_ref, modes):
    slabs = len(values)
    out = [None] * slabs
    out[-1] = values[-1]
    if after is not None:
        out[-1] = out[-1] - apply(after, panel, modes)
    for j in range(slabs - 2, -1, -1):
        out[j] = values[j] - apply(out[j + 1], behind_ref[j], modes)
    return out


def push_kernel(modes, first_ref, load_ref, prev_ref, push_ref, prev_buf, sems):
    @pl.when(lax.axis_index("elem") == 1)
    def _():
        for copy in start_copies([(first_ref, prev_buf)], sems):
            copy.wait()
        weight = previous_weight(prev_buf, modes)
        prev_ref[...] = weight
        push_ref[...] = apply_nt(load_ref[1], weight, modes)


def forward_kernel(modes, at, got_ref, push_ref, y_ref, front_ref, old_ref, state_ref, send_ref):
    @pl.when(lax.axis_index("elem") == at)
    def _():
        before = got_ref[...] - push_ref[...]
        state_ref[0] = before
        send_ref[...] = y_ref[y_ref.shape[0] - 1] + apply(before, front_ref[...], modes)


def base_kernel(
    modes, mode_total, hub, place, band_ref, map_ref, state_ref, load_ref, reduced_ref, y_ref, w_ref,
    base_ref, found_ref, back_ref, band_buf, sems,
):
    elem = lax.axis_index("elem")
    slabs, rows, size = reduced_ref.shape
    lam = wave(mode_total, (rows, size), modes)

    @pl.when((elem > 0) & (elem < hub))
    def _():
        copies = start_copies([(band_ref.at[:, 0], band_buf), (map_ref, back_ref)], sems)
        copies[0].wait()
        first = band_wide(band_buf[0], band_buf[1])
        bands = [first] + [place.band(w_ref, j) for j in range(1, slabs)]
        panels = [w_ref[place.at("panel", j)] for j in range(slabs)]
        values = []
        for j in range(slabs):
            step = face_push(values[-1] if j > 0 else state_ref[0], bands[j], lam)
            values.append(apply(reduced_ref[j] - step, panels[j], modes))
        found = values[-1]
        found_ref[slabs - 1] = found
        for j in range(slabs - 2, -1, -1):
            found = values[j] - apply(face_lift(found, bands[j + 1], lam), panels[j], modes)
            found_ref[j] = found
        base_ref[...] = load_ref[1] + face_lift(found, first, lam)
        copies[1].wait()


def ahead_maps(ahead_ref, band_buf, waves, w_ref, place):
    slabs, many, _ = ahead_ref.shape
    for j in range(slabs):
        first, second = band_buf[0, j].T, band_buf[1, j].T
        for k, lam in enumerate(waves):
            ahead_ref[j, pl.ds(k * place.size, place.size)] = wide(product(first + lam * second, w_ref[place.at("panel", j, k)]))


def behind_maps(behind_ref, band_buf, waves, w_ref, place):
    for j in range(behind_ref.shape[0]):
        for k, lam in enumerate(waves):
            step = product(band_buf[0, j + 1] + lam * band_buf[1, j + 1], w_ref[place.at("panel", j, k)])
            behind_ref[j, pl.ds(k * place.size, place.size)] = wide(step)


def hub_map_kernel(
    modes, mode_total, hub, place, map_ref, pprev_ref, band_ref, given_ref, load_ref, y_ref, w_ref, front_ref, old_prev_ref, old_push_ref,
    prev_ref, push_ref, ahead_ref, behind_ref, back_ref, base_ref, cross_ref, through_ref, band_buf, map_buf, prev_buf, sems,
):
    slabs, rows, size = y_ref.shape
    lam = wave(mode_total, (rows, size), modes)
    inside = (lax.axis_index("elem") > 1) & (lax.axis_index("elem") <= hub)

    @pl.when(inside)
    def _():
        start_copies([(pprev_ref, prev_buf)], sems.at[pl.ds(2, 1)])

    @pl.when(lax.axis_index("elem") == hub)
    def _():
        copies = start_copies([(band_ref, band_buf), (map_ref, map_buf)], sems)
        given = start_copies([(given_ref, back_ref)], sems.at[pl.ds(3, 1)])[0]
        waves = [wave_of(k, mode_total, modes) for k in range(modes)]

        def part(k):
            return pl.ds(k * size, size)

        copies[0].wait()
        ahead_maps(ahead_ref, band_buf, waves, w_ref, place)
        behind_maps(behind_ref, band_buf, waves, w_ref, place)
        entry = [wide(band_buf[0, 0] + waves[k] * band_buf[1, 0]) for k in range(modes)]
        forward = [[-whole(ahead_ref[0, part(k)]) for k in range(modes)]]
        for j in range(1, slabs - 1):
            forward.append([-product(forward[-1][k], ahead_ref[j, part(k)]) for k in range(modes)])
        cross = [whole(front_ref[part(k)]) for k in range(modes)]
        for j in range(slabs - 2, -1, -1):
            cross = [forward[j][k] - product(cross[k], behind_ref[j, part(k)]) for k in range(modes)]
        for k in range(modes):
            cross_ref[part(k)] = wide(product(cross[k], entry[k]))
        found = backward_values([y_ref[j] for j in range(slabs)], None, None, behind_ref, modes)
        base_ref[...] = load_ref[1] + face_lift(found[0], band_wide(band_buf[0, 0], band_buf[1, 0]), lam)
        copies[1].wait()
        given.wait()
        for k in range(modes):
            through_ref[part(k)] = wide(product(map_buf[k].T, back_ref[part(k)]))

    @pl.when(inside)
    def _():
        pltpu.make_async_copy(pprev_ref, prev_buf, sems.at[2]).wait()
        weight = previous_weight(prev_buf, modes)
        prev_ref[...] = weight
        push_ref[...] = apply_nt(load_ref[1], weight, modes)


def hub_kernel(
    modes, at, place, got_ref, push_ref, far_ref, through_ref, y_ref, front_ref, back_ref, cross_ref, base_ref, w_ref,
    send_ref, values_ref,
):
    slabs = y_ref.shape[0]

    @pl.when(lax.axis_index("elem") == at)
    def _():
        before = got_ref[...] - push_ref[...]
        load = apply(far_ref[1], w_ref[place.at("panel", slabs - 1)], modes)
        value = y_ref[slabs - 1] + apply(before, front_ref[...], modes)
        out = base_ref[...] + apply(before, cross_ref[...], modes) + apply(far_ref[0], back_ref[...], modes)
        final = value - load
        send_ref[...] = out + apply(final, through_ref[...], modes)
        values_ref[0] = before
        values_ref[1] = value
        values_ref[2] = final


def hub_values_kernel(modes, at, place, map_ref, far_ref, values_ref, w_ref, old_ref, state_ref, last_ref):
    @pl.when(lax.axis_index("elem") == at)
    def _():
        final = values_ref[2]
        after = far_ref[0] + apply_nt(final, previous_weight(map_ref, modes), modes)
        state_ref[0] = values_ref[0]
        state_ref[1] = after
        last_ref[0] = final
        last_ref[1] = values_ref[1] - apply(after, w_ref[place.at("panel", place.counts["panel"] - 1)], modes)


def own_map_kernel(
    modes, mode_total, hub, place, band_ref, radial_ref, state_ref, reduced_ref, y_ref, w_ref, front_ref, prev_ref, ahead_ref, behind_ref, old_ref,
    found_ref, own_ref, before_ref, radt_ref, ahead_buf, behind_buf, band_buf, radial_buf, sems,
):
    slabs, rows, size = reduced_ref.shape
    elem, last = lax.axis_index("elem"), lax.axis_size("elem") - 1
    lam = wave(mode_total, (rows, size), modes)
    waves = [wave_of(k, mode_total, modes) for k in range(modes)]
    copies = start_copies([(band_ref, band_buf), (radial_ref, radial_buf)], sems)

    def part(k):
        return pl.ds(k * size, size)

    copies[0].wait()

    @pl.when(elem == hub)
    def _():
        panels = [w_ref[place.at("panel", j)] for j in range(slabs)]
        before, values = state_ref[0], []
        for j in range(slabs):
            if j == slabs - 1:
                values.append(y_ref[j] + apply(before, front_ref[...], modes))
                continue
            solved = apply(reduced_ref[j], panels[j], modes)
            values.append(solved - apply(values[-1] if j > 0 else before, ahead_ref[j], modes))
        found = backward_values(values, state_ref[1], panels[-1], behind_ref, modes)
        for j in range(slabs):
            found_ref[j] = found[j]
        back = face_lift(found[0], band_wide(band_buf[0, 0], band_buf[1, 0]), lam)
        before_ref[...] = before - apply_nt(back, prev_ref[...], modes)

    @pl.when(elem != hub)
    def _():
        behind_maps(behind_buf, band_buf, waves, w_ref, place)

    @pl.when(elem < hub)
    def _():
        current = [-whole(w_ref[place.at("panel", slabs - 1, k)]) for k in range(modes)]
        for k in range(modes):
            own_ref[slabs - 1, part(k)] = -w_ref[place.at("panel", slabs - 1, k)]
        for j in range(slabs - 2, -1, -1):
            current = [-product(current[k], behind_buf[j, part(k)]) for k in range(modes)]
            for k in range(modes):
                own_ref[j, part(k)] = wide(current[k])

    @pl.when(elem == last)
    def _():
        ahead_maps(ahead_buf, band_buf, waves, w_ref, place)
        forward = [[-whole(ahead_buf[0, part(k)]) for k in range(modes)]]
        for j in range(1, slabs):
            forward.append([-product(forward[-1][k], ahead_buf[j, part(k)]) for k in range(modes)])
        current = forward[-1]
        for k in range(modes):
            own_ref[slabs - 1, part(k)] = wide(current[k])
        for j in range(slabs - 2, -1, -1):
            current = [forward[j][k] - product(current[k], behind_buf[j, part(k)]) for k in range(modes)]
            for k in range(modes):
                own_ref[j, part(k)] = wide(current[k])

    @pl.when((elem == 0) | (elem == last))
    def _():
        found = backward_values([y_ref[j] for j in range(slabs)], None, None, behind_buf, modes)
        for j in range(slabs):
            found_ref[j] = found[j]

    copies[1].wait()
    for j in range(slabs):
        radt_ref[j] = wide(radial_buf[j].T)


def backward_kernel(modes, at, got_ref, base_ref, back_ref, old_ref, state_ref, send_ref):
    @pl.when(lax.axis_index("elem") == at)
    def _():
        after = got_ref[...]
        state_ref[1] = after
        send_ref[...] = base_ref[...] + apply(after, back_ref[...], modes)


def final_kernel(
    modes, mode_total, hub, place, zsrc_ref, inv_ref, state_ref, got_ref, base_ref, last_ref, load_ref, found_ref, own_ref, back_ref, before_ref, prev_ref, w_ref, radt_ref, axial_ref, weight_ref,
    out_ref, x_ref, out_buf, sems,
):
    slabs, inner, rows, size = zsrc_ref.shape
    lam = wave(mode_total, (rows, size), modes)
    elem, last = lax.axis_index("elem"), lax.axis_size("elem") - 1

    def values(given):
        for j in range(slabs):
            x_ref[j + 1] = found_ref[j] + apply(given, own_ref[j], modes)

    @pl.when(elem == 0)
    def _():
        x_ref[0] = jnp.zeros((rows, size), F32)
        values(got_ref[...])

    @pl.when((elem > 0) & (elem < hub))
    def _():
        after = state_ref[1]
        values(after)
        back = base_ref[...] - load_ref[1] + apply(after, back_ref[...], modes)
        x_ref[0] = state_ref[0] - apply_nt(back, prev_ref[...], modes)

    @pl.when(elem == hub)
    def _():
        for j in range(slabs):
            x_ref[j + 1] = found_ref[j]
        x_ref[0] = before_ref[...]

    @pl.when(elem == last)
    def _():
        values(last_ref[0])
        x_ref[0] = last_ref[1]

    copies = []
    for j in range(slabs):
        lifted = [face_lift(x_ref[j + side], place.face(w_ref, j, side), lam) for side in range(2)]
        kept = []
        for b in range(inner):
            total = lifted[0] * weight_ref[j, 0, b] + lifted[1] * weight_ref[j, 1, b]
            kept.append(zsrc_ref[j, b] - total * inv_ref[j, b])
        values = []
        for a in range(inner):
            value = kept[0] * axial_ref[j, a, 0]
            for b in range(1, inner):
                value = value + kept[b] * axial_ref[j, a, b]
            values.append(value)
        result = product(jnp.concatenate(values, axis=0), radt_ref[j])
        for a in range(inner):
            out_buf[j, :, a * size : (a + 1) * size] = result[a * rows : (a + 1) * rows]
        out_buf[j, :, inner * size :] = x_ref[j + 1]
        width = (inner + 1) * size
        copies += start_copies([(out_buf.at[j], out_ref.at[:, pl.ds(j * width, width)])], sems.at[pl.ds(j, 1)])
    for copy in copies:
        copy.wait()


def dft_table(planes):
    row, col = np.arange(planes)[:, None], np.arange(planes)[None]
    angle = row // 2 * col % planes * (2.0 * math.pi / planes)
    table = np.where(row % 2 == 0, np.cos(angle), -np.sin(angle)) / math.sqrt(planes)
    table = jnp.asarray(table, F32)
    high, low = split(table)
    return jnp.concatenate([high, low, high], axis=1)


def body(
    rhs_phys, radial_basis, axial_basis, radial_eig, axial_eig, face_stiff, face_mass, axial_coupling, face_numbering,
    band_panels, inverse_panels,
):
    planes, nodes = rhs_phys.shape
    modes, slabs, size, _ = inverse_panels.shape
    inner = axial_basis.shape[1]
    devices = lax.axis_size("mode")
    elems = lax.axis_size("elem")
    mode_total = modes * devices
    rows = 2 * modes
    hub = elems - 2
    last = elems - 1

    def shape(*dims):
        return jax.ShapeDtypeStruct(dims, F32)

    def kept(*dims):
        return pltpu.VMEM(dims, F32)

    def half(*dims):
        return pltpu.VMEM(dims, BF16)

    table = dft_table(planes)
    many = modes * size
    place = Weights(size, ("panel", slabs, many), ("radial", slabs, size), ("face", 4 * slabs, size), ("band", 2 * (slabs - 1), size))
    buffers = [pltpu.VMEM((planes, nodes), F32), pltpu.VMEM(table.shape, BF16), pltpu.SemaphoreType.DMA((slabs + 3,))]
    whole_spectrum = pltpu.HBM((planes, nodes), F32)
    whole_panels = pltpu.HBM((modes, size, size), F32)
    panels_buffer = pltpu.VMEM((modes, size, size), F32)
    ship, spectrum = call(
        functools.partial(ends_kernel, modes, mode_total),
        [whole_panels, whole_spectrum],
        [inverse_panels, band_panels, rhs_phys, table],
        anywhere=4,
        scratch=[pltpu.VMEM((slabs, modes, size, size), F32), pltpu.VMEM(band_panels.shape, F32), panels_buffer] + buffers,
    )
    if hub > 1:
        first = far_map = lax.ppermute(ship, "elem", [(0, 1), (last, hub)])
    else:
        first, far_map = lax.ppermute(ship, "elem", [(0, 1)]), lax.ppermute(ship, "elem", [(last, hub)])
    ship, spectrum = call(
        functools.partial(between_kernel, hub),
        [whole_panels, whole_spectrum],
        [inverse_panels, rhs_phys, table, spectrum],
        anywhere=4,
        scratch=[panels_buffer] + buffers,
        aliases={3: 1},
    )
    pprev = lax.ppermute(ship, "elem", [(i, i + 1) for i in range(1, hub)]) if hub > 1 else first
    spectrum = call(
        functools.partial(late_kernel, hub),
        [whole_spectrum],
        [rhs_phys, table, spectrum],
        anywhere=3,
        scratch=buffers,
        aliases={2: 0},
    )[0]
    spectrum = lax.all_to_all(spectrum.reshape(devices, rows, nodes), "mode", 0, 0, tiled=False)
    if nodes % size:
        spectrum = jnp.swapaxes(spectrum, 0, 1).reshape(1, rows, devices * nodes)
    vector = (rows, size)
    matrix = half(many, 2 * size)
    front, back_map, later, w, reig, axial, weight, aeig = call(
        functools.partial(maps_kernel, modes, mode_total, hub, place),
        [
            pltpu.HBM((many, 2 * size), BF16),
            pltpu.HBM((many, 2 * size), BF16),
            pltpu.HBM((slabs - 1, many, 2 * size), BF16),
            half(place.total, 2 * size),
            kept(*radial_eig.shape),
            pltpu.SMEM(axial_basis.shape, F32),
            pltpu.SMEM((slabs, 2, inner), F32),
            pltpu.SMEM(axial_eig.shape, F32),
        ],
        [
            inverse_panels, band_panels, radial_basis, face_stiff, face_mass, face_numbering,
            radial_eig, axial_basis, axial_eig, axial_coupling,
        ],
        anywhere=10,
        outside=3,
        scratch=[
            pltpu.VMEM((slabs, modes, size, size), F32),
            pltpu.VMEM(band_panels.shape, F32),
            pltpu.VMEM(radial_basis.shape, F32),
            pltpu.VMEM(face_stiff.shape, F32),
            pltpu.VMEM(face_mass.shape, F32),
            pltpu.VMEM(face_numbering.shape, jnp.int32),
            pltpu.SMEM(axial_basis.shape, F32),
            pltpu.SMEM(axial_coupling.shape, F32),
            pltpu.VMEM((many, 2 * size), BF16),
            pltpu.VMEM((many, 2 * size), BF16),
            pltpu.VMEM((slabs - 1, many, 2 * size), BF16),
            pltpu.SemaphoreType.DMA((slabs + 9,)),
        ],
    )
    solves = [kept(slabs, inner, *vector), kept(slabs, inner, *vector), kept(slabs, *vector), kept(slabs, *vector)]
    *solve, send = call(
        functools.partial(inner_kernel, modes, mode_total, place, hub, True),
        solves + [kept(*vector)],
        [band_panels, front, later, spectrum, w, reig, axial, weight, aeig],
        anywhere=3,
        smem=3,
    )
    got = lax.ppermute(send, "elem", [(0, 1)])
    zsrc, inv, reduced, y, load, front = call(
        functools.partial(inner_kernel, modes, mode_total, place, hub, False),
        solves + [kept(2, *vector), matrix],
        [band_panels, front, later, spectrum, w, reig, *solve, axial, weight, aeig],
        anywhere=3,
        smem=3,
        scratch=[
            pltpu.VMEM((2, size, size), F32),
            pltpu.VMEM((slabs - 1, many, 2 * size), BF16),
            pltpu.SemaphoreType.DMA((2,)),
        ],
        aliases={6 + i: i for i in range(4)},
    )
    far = lax.ppermute(load, "elem", [(last, hub)])
    prev, push = call(
        functools.partial(push_kernel, modes),
        [half(2 * size, many), kept(*vector)],
        [first, load],
        free=1,
        scratch=[panels_buffer, pltpu.SemaphoreType.DMA((1,))],
    )
    prev, later_push, ahead, behind, hub_back, hub_base, cross, through = call(
        functools.partial(hub_map_kernel, modes, mode_total, hub, place),
        [
            half(2 * size, many), kept(*vector), half(slabs - 1, many, 2 * size), half(slabs - 1, many, 2 * size), matrix,
            kept(*vector), matrix, matrix,
        ],
        [far_map, pprev, band_panels, back_map, load, y, w, front, prev, push],
        free=2,
        anywhere=2,
        scratch=[pltpu.VMEM(band_panels.shape, F32), panels_buffer, panels_buffer, pltpu.SemaphoreType.DMA((4,))],
        aliases={8: 0, 9: 1},
    )
    state = jnp.zeros((2, *vector), F32)
    for at in range(1, hub):
        state, send = call(
            functools.partial(forward_kernel, modes, at),
            [kept(*state.shape), shape(*vector)],
            [got, push if at == 1 else later_push, y, front, state],
            aliases={4: 0},
        )
        got = lax.ppermute(send, "elem", [(at, at + 1)])
    send, values = call(
        functools.partial(hub_kernel, modes, hub, place),
        [shape(*vector), kept(3, *vector)],
        [got, push if hub == 1 else later_push, far, through, y, front, hub_back, cross, hub_base, w],
    )
    state, final = call(
        functools.partial(hub_values_kernel, modes, hub, place),
        [kept(*state.shape), shape(2, *vector)],
        [far_map, far, values, w, state],
        aliases={4: 0},
    )
    base, found, back = call(
        functools.partial(base_kernel, modes, mode_total, hub, place),
        [kept(*vector), kept(slabs, *vector), matrix],
        [band_panels, back_map, state, load, reduced, y, w],
        anywhere=2,
        scratch=[pltpu.VMEM((2, size, size), F32), pltpu.SemaphoreType.DMA((2,))],
    )
    for at in range(hub - 1, 0, -1):
        got = lax.ppermute(send, "elem", [(at + 1, at)])
        state, send = call(
            functools.partial(backward_kernel, modes, at),
            [kept(*state.shape), shape(*vector)],
            [got, base, back, state],
            aliases={3: 0},
        )
    got = lax.ppermute(send, "elem", [(1, 0)])
    found, own, before, radt = call(
        functools.partial(own_map_kernel, modes, mode_total, hub, place),
        [kept(slabs, *vector), half(slabs, many, 2 * size), kept(*vector), half(slabs, size, 2 * size)],
        [band_panels, radial_basis, state, reduced, y, w, front, prev, ahead, behind, found],
        anywhere=2,
        scratch=[
            pltpu.VMEM((slabs, many, 2 * size), BF16),
            pltpu.VMEM((slabs - 1, many, 2 * size), BF16),
            pltpu.VMEM(band_panels.shape, F32),
            pltpu.VMEM(radial_basis.shape, F32),
            pltpu.SemaphoreType.DMA((2,)),
        ],
        aliases={10: 0},
    )
    final = lax.ppermute(final, "elem", [(hub, last)])
    return call(
        functools.partial(final_kernel, modes, mode_total, hub, place),
        [pltpu.HBM((rows, slabs * (inner + 1) * size), F32)],
        [
            zsrc, inv, state, got, base, final, load, found, own, back, before, prev, w, radt, axial, weight,
        ],
        smem=2,
        scratch=[
            pltpu.VMEM((slabs + 1, *vector), F32),
            pltpu.VMEM((slabs, rows, (inner + 1) * size), F32),
            pltpu.SemaphoreType.DMA((slabs,)),
        ],
    )[0]


def solution(mesh):
    placed = (
        P(None, ("elem", "mode")),
        P("elem", None, None),
        P("elem", None, None),
        P("elem", None),
        P("elem", None),
        P("elem", None, None),
        P("elem", None, None),
        P("elem", None, None),
        P("elem", None, None),
        P(None, "elem", None, None),
        P("mode", "elem", None, None),
    )
    return jax.shard_map(
        body, mesh=mesh, in_specs=placed, out_specs=P("mode", "elem"), check_vma=False
    )
```

```python
import functools
import math

import jax
import jax.numpy as jnp
import numpy as np
from jax import lax
from jax.experimental import pallas as pl
from jax.experimental.pallas import tpu as pltpu
from jax.sharding import PartitionSpec as P

F32 = jnp.float32
BF16 = jnp.bfloat16
VMEM = pl.BlockSpec(memory_space=pltpu.VMEM)
SMEM = pl.BlockSpec(memory_space=pltpu.SMEM)
HBM = pl.BlockSpec(memory_space=pltpu.HBM)
ANY = pl.BlockSpec(memory_space=pl.ANY)
NN = (((1,), (0,)), ((), ()))
NT = (((1,), (1,)), ((), ()))


def call(kernel, outs, args, smem=0, anywhere=0, free=0, outside=0, scratch=(), aliases=None):
    inside = len(args) - smem - anywhere - free
    spaces = [None] * free + [pltpu.HBM] * anywhere + [pltpu.VMEM] * inside + [pltpu.SMEM] * smem
    args = [arg if space is None else pltpu.with_memory_space_constraint(arg, space) for arg, space in zip(args, spaces)]
    return pl.pallas_call(
        kernel,
        out_shape=outs,
        in_specs=[ANY] * free + [HBM] * anywhere + [VMEM] * inside + [SMEM] * smem,
        out_specs=[HBM if getattr(out, "memory_space", None) is pltpu.HBM else VMEM for out in outs[: len(outs) - outside]]
        + [SMEM] * outside,
        scratch_shapes=scratch,
        input_output_aliases=aliases or {},
        compiler_params=pltpu.CompilerParams(vmem_limit_bytes=16 * 2**20),
    )(*args)


def split(x):
    high = x.astype(BF16)
    return high, (x - high.astype(F32)).astype(BF16)


def dot(a, b, dims=NN):
    return lax.dot_general(a, b, dims, preferred_element_type=F32)


def wide(x):
    return jnp.concatenate(split(x), axis=1)


def tall(x):
    return jnp.concatenate(split(x), axis=0)


def product(left, right):
    size = right.shape[1] // 2
    out = dot(wide(left), jnp.concatenate([right, right], axis=0))
    return out[:, :size] + out[:, size:]


def by_mode(x, modes):
    both = tall(x)
    mode_of = lax.broadcasted_iota(jnp.int32, both.shape, 0) % x.shape[0] // 2
    return jnp.concatenate([jnp.where(mode_of == k, both, jnp.zeros_like(both)) for k in range(modes)], axis=1)


def folded(out, rows):
    size = out.shape[1] // 2
    return out[:rows, :size] + out[:rows, size:] + out[rows:, :size]


def apply(x, weight, modes):
    return folded(dot(by_mode(x, modes), weight), x.shape[0])


def wave(mode_total, shape, modes, axis=0):
    first = lax.axis_index("mode") * modes
    index = first + lax.broadcasted_iota(jnp.int32, shape, axis) // 2
    number = index.astype(F32) / mode_total
    return 4.0 * number * number


def wave_of(k, mode_total, modes):
    number = (jnp.full((1, 1), lax.axis_index("mode") * modes + k, jnp.int32)).astype(F32) / mode_total
    return 4.0 * number * number


class Weights:
    def __init__(self, size, *entries):
        self.size, self.rows, self.counts = size, {}, {}
        self.total = 0
        for name, count, rows in entries:
            self.rows[name], self.counts[name] = (self.total, rows), count
            self.total += count * rows

    def at(self, name, index, mode=None):
        start, rows = self.rows[name]
        if mode is None:
            return pl.ds(start + index * rows, rows)
        return pl.ds(start + index * rows + mode * self.size, self.size)

    def pair(self, ref, name, index):
        return jnp.concatenate([ref[self.at(name, index)], ref[self.at(name, index + 1)]], axis=1)

    def band(self, ref, slab):
        return self.pair(ref, "band", 2 * (slab - 1))

    def face(self, ref, slab, side):
        return self.pair(ref, "face", 4 * slab + 2 * side)


def band_wide(stiff, mass):
    return wide(jnp.concatenate([stiff, mass], axis=1))


def whole(weight):
    size = weight.shape[1] // 2
    value = weight.astype(F32)
    return value[:, :size] + value[:, size:]


def start_copies(pairs, sems):
    copies = [pltpu.make_async_copy(src, dst, sems.at[i]) for i, (src, dst) in enumerate(pairs)]
    for copy in copies:
        copy.start()
    return copies


def transform(rhs_ref, table_ref, out_ref, rhs_buf, table_buf, sems, started=None):
    for copy in started or start_copies([(rhs_ref, rhs_buf), (table_ref, table_buf)], sems):
        copy.wait()
    high, low = split(rhs_buf[...])
    rhs_buf[...] = dot(table_buf[...], jnp.concatenate([high, high, low], axis=0))
    return start_copies([(rhs_buf, out_ref)], sems)[0]


def panels_and_transform(panels_ref, ship_ref, rhs_ref, table_ref, out_ref, ship_buf, rhs_buf, table_buf, sems):
    half = ship_buf.shape[0] // 2
    parts = [pl.ds(0, half), pl.ds(half, ship_buf.shape[0] - half)]
    fetch = start_copies([(panels_ref.at[part, panels_ref.shape[1] - 1], ship_buf.at[part]) for part in parts], sems.at[pl.ds(2, 2)])
    result = transform(rhs_ref, table_ref, out_ref, rhs_buf, table_buf, sems)
    ship = []
    for i, part in enumerate(parts):
        fetch[i].wait()
        ship += start_copies([(ship_buf.at[part], ship_ref.at[part])], sems.at[pl.ds(2 + i, 1)])
    for copy in [result] + ship:
        copy.wait()


def ends_kernel(
    modes, mode_total, panels_ref, band_ref, rhs_ref, table_ref, ship_ref, out_ref,
    panels_buf, band_buf, ship_buf, rhs_buf, table_buf, sems,
):
    slabs, size = panels_ref.shape[1:3]
    elem, last = lax.axis_index("elem"), lax.axis_size("elem") - 1

    @pl.when(elem == 0)
    def _():
        panels_and_transform(panels_ref, ship_ref, rhs_ref, table_ref, out_ref, ship_buf, rhs_buf, table_buf, sems)

    @pl.when(elem == last)
    def _():
        copies = start_copies(
            [(band_ref, band_buf)] + [(panels_ref.at[:, j], panels_buf.at[j]) for j in range(slabs)],
            sems.at[pl.ds(2, slabs + 1)],
        )
        started = start_copies([(rhs_ref, rhs_buf), (table_ref, table_buf)], sems)
        copies[0].wait()
        band_t = [(band_buf[0, j].T, band_buf[1, j].T) for j in range(slabs)]
        lam = [wave_of(k, mode_total, modes) for k in range(modes)]
        forward = []
        for j in range(slabs):
            copies[1 + j].wait()
            steps = [
                product(panels_buf[j, k], wide(band_buf[0, j] + lam[k] * band_buf[1, j])) for k in range(modes)
            ]
            if j == 0:
                forward.append([-step for step in steps])
            else:
                forward.append([-product(steps[k], wide(forward[-1][k])) for k in range(modes)])
        current = forward[-1]
        for j in range(slabs - 2, -1, -1):
            steps = [
                product(panels_buf[j, k], wide(band_t[j + 1][0] + lam[k] * band_t[j + 1][1])) for k in range(modes)
            ]
            current = [forward[j][k] - product(steps[k], wide(current[k])) for k in range(modes)]
        ship = [transform(rhs_ref, table_ref, out_ref, rhs_buf, table_buf, sems, started)]
        half = modes // 2
        for i, part in enumerate((range(half), range(half, modes))):
            for k in part:
                ship_buf[k] = product(band_t[0][0] + lam[k] * band_t[0][1], wide(current[k]))
            rows = pl.ds(part.start, len(part))
            ship += start_copies([(ship_buf.at[rows], ship_ref.at[rows])], sems.at[pl.ds(2 + i, 1)])
        for copy in ship:
            copy.wait()


def between_kernel(hub, panels_ref, rhs_ref, table_ref, old_ref, ship_ref, out_ref, ship_buf, rhs_buf, table_buf, sems):
    elem = lax.axis_index("elem")

    @pl.when((elem > 0) & (elem < hub))
    def _():
        panels_and_transform(panels_ref, ship_ref, rhs_ref, table_ref, out_ref, ship_buf, rhs_buf, table_buf, sems)


def late_kernel(hub, rhs_ref, table_ref, old_ref, out_ref, rhs_buf, table_buf, sems):
    @pl.when(lax.axis_index("elem") == hub)
    def _():
        transform(rhs_ref, table_ref, out_ref, rhs_buf, table_buf, sems).wait()


def maps_kernel(
    modes, mode_total, hub, place, panels_ref, band_ref, radial_ref, stiff_ref, mass_ref, number_ref, reig_ref, axial_ref, aeig_ref,
    coup_ref, front_ref, back_ref, behind_ref, w_ref, reig_out, axial_out, weight_out, aeig_out,
    panels_buf, band_buf, radial_buf, stiff_buf, mass_buf, number_buf, axial_buf, coup_buf, front_buf, back_buf, behind_buf, sems,
):
    slabs, size = panels_ref.shape[1:3]
    inner = aeig_ref.shape[1]
    copies = start_copies(
        [(radial_ref, radial_buf), (stiff_ref, stiff_buf), (mass_ref, mass_buf), (number_ref, number_buf), (band_ref, band_buf)]
        + [(panels_ref.at[:, j], panels_buf.at[j]) for j in range(slabs)]
        + [(axial_ref, axial_buf), (coup_ref, coup_buf), (aeig_ref, aeig_out), (reig_ref, reig_out)],
        sems,
    )
    for copy in copies[:4]:
        copy.wait()
    for j in range(slabs):
        radial = wide(radial_buf[j])
        w_ref[place.at("radial", j)] = radial
        parts = [wide(product(ref[j].T, radial)) for ref in (stiff_buf, mass_buf)]
        for side in range(2):
            spot = lax.broadcasted_iota(jnp.int32, (size, size), 0)
            onehot = jnp.where(number_buf[j, side : side + 1] == spot, 1.0, 0.0).astype(BF16)
            for i in range(2):
                both = jnp.concatenate([p[:, i * size : (i + 1) * size] for p in parts], axis=1)
                w_ref[place.at("face", 4 * j + 2 * side + i)] = dot(onehot, both).astype(BF16)
    copies[4].wait()
    for j in range(1, slabs):
        bands = band_wide(band_buf[0, j].T, band_buf[1, j].T)
        for i in range(2):
            w_ref[place.at("band", 2 * (j - 1) + i)] = bands[:, 2 * i * size : 2 * (i + 1) * size]
    for j in range(slabs):
        copies[5 + j].wait()
        for k in range(modes):
            w_ref[place.at("panel", j, k)] = wide(panels_buf[j, k].T)
    for copy in copies[5 + slabs :]:
        copy.wait()
    for j in range(slabs):
        for b in range(inner):
            for a in range(inner):
                axial_out[j, a, b] = axial_buf[j, a, b]
            for side in range(2):
                weight = coup_buf[j, side, 0] * axial_buf[j, 0, b]
                for a in range(1, inner):
                    weight = weight + coup_buf[j, side, a] * axial_buf[j, a, b]
                weight_out[j, side, b] = weight

    @pl.when((lax.axis_index("elem") > 0) & (lax.axis_index("elem") <= hub))
    def _():
        lam = [wave_of(k, mode_total, modes) for k in range(modes)]
        current = None
        for j in range(slabs):
            first, second = band_buf[0, j].T, band_buf[1, j].T
            steps = [product(first + lam[k] * second, w_ref[place.at("panel", j, k)]) for k in range(modes)]
            if current is None:
                current = [-step for step in steps]
            else:
                current = [-product(current[k], wide(steps[k])) for k in range(modes)]
        for k in range(modes):
            front_buf[pl.ds(k * size, size)] = wide(current[k])
        start_copies([(front_buf, front_ref)], sems.at[pl.ds(1, 1)])

        @pl.when(lax.axis_index("elem") <= hub)
        def _():
            current = [-whole(w_ref[place.at("panel", slabs - 1, k)]) for k in range(modes)]
            for j in range(slabs - 2, -1, -1):
                steps = [
                    product(band_buf[0, j + 1] + lam[k] * band_buf[1, j + 1], w_ref[place.at("panel", j, k)]) for k in range(modes)
                ]
                current = [-product(current[k], wide(steps[k])) for k in range(modes)]
            for k in range(modes):
                back_buf[pl.ds(k * size, size)] = wide(product(current[k], wide(band_buf[0, 0] + lam[k] * band_buf[1, 0])))
            for copy in start_copies([(back_buf, back_ref)], sems):
                copy.wait()

        pltpu.make_async_copy(front_buf, front_ref, sems.at[1]).wait()

    @pl.when(lax.axis_index("elem") == lax.axis_size("elem") - 1)
    def _():
        behind_maps(behind_buf, band_buf, [wave_of(k, mode_total, modes) for k in range(modes)], w_ref, place)
        for copy in start_copies([(behind_buf, behind_ref)], sems):
            copy.wait()


def face_push(values, weight, lam):
    rows, size = values.shape
    high, low = split(values)
    blocks = [weight[:, i * size : (i + 1) * size] for i in range(4)]
    out = dot(
        jnp.concatenate([high, low], axis=0), jnp.concatenate(blocks, axis=0), NT
    )
    out = out[:rows, : 2 * size] + out[:rows, 2 * size :] + out[rows:, : 2 * size]
    return out[:, :size] + lam * out[:, size:]


def face_lift(values, weight, lam):
    rows, size = values.shape
    out = folded(dot(tall(values), weight), rows)
    return out[:, :size] + lam * out[:, size:]


def block_of(spec_ref, index, size):
    per = spec_ref.shape[2] // size
    at = index % per * size
    return spec_ref[index // per, :, at : at + size]


def inner_kernel(modes, mode_total, place, hub, first_call, band_ref, front_ref, behind_ref, *refs):
    elem = lax.axis_index("elem")
    if first_call:
        spec_ref, w_ref, reig_ref, axial_ref, weight_ref, aeig_ref, zsrc_ref, inv_ref, reduced_ref, y_ref, send_ref = refs
    else:
        spec_ref, w_ref, reig_ref = refs[:3]
        axial_ref, weight_ref, aeig_ref, zsrc_ref, inv_ref, reduced_ref, y_ref, load_ref, front_out, band_buf, behind_buf, sems = refs[7:]
        inside = (elem > 0) & (elem <= hub)
        early = (front_ref, front_out)
        late = [(band_ref.at[:, 0], band_buf), (behind_ref, behind_buf)]

        @pl.when(inside)
        def _():
            start_copies([early], sems.at[pl.ds(1, 1)])

        @pl.when(elem == lax.axis_size("elem") - 1)
        def _():
            start_copies(late, sems)

    @pl.when((elem == 0) == first_call)
    def _():
        load, values = inner_part(
            modes, mode_total, place, spec_ref, w_ref, reig_ref, axial_ref, weight_ref, aeig_ref, zsrc_ref, inv_ref, reduced_ref, y_ref
        )
        if first_call:
            send_ref[...] = values[-1]
            return
        load_ref[1] = load

        @pl.when(inside)
        def _():
            pltpu.make_async_copy(*early, sems.at[1]).wait()

        @pl.when(elem == lax.axis_size("elem") - 1)
        def _():
            lam = wave(mode_total, load.shape, modes)
            current = values[-1]
            for i, pair in enumerate(late):
                pltpu.make_async_copy(*pair, sems.at[i]).wait()
            for j in range(len(values) - 2, -1, -1):
                current = values[j] - apply(current, behind_buf[j], modes)
            load_ref[0] = load + face_lift(current, band_wide(band_buf[0], band_buf[1]), lam)


def inner_part(
    modes, mode_total, place, spec_ref, w_ref, reig_ref, axial_ref, weight_ref, aeig_ref, zsrc_ref, inv_ref, solved_ref, y_ref
):
    slabs, inner, rows, size = zsrc_ref.shape
    lam = wave(mode_total, (rows, size), modes)
    pushed = []
    for j in range(slabs):
        source = jnp.concatenate(
            [block_of(spec_ref, j * (inner + 1) + a, size) for a in range(inner)], axis=0
        )
        first = product(source, w_ref[place.at("radial", j)])
        first = [first[a * rows : (a + 1) * rows] for a in range(inner)]
        sums = [None, None]
        for b in range(inner):
            value = first[0] * axial_ref[j, 0, b]
            for a in range(1, inner):
                value = value + first[a] * axial_ref[j, a, b]
            inverse = 1.0 / (aeig_ref[j, b] + reig_ref[j : j + 1] + lam)
            inv_ref[j, b] = inverse
            value = value * inverse
            zsrc_ref[j, b] = value
            for side in range(2):
                term = value * weight_ref[j, side, b]
                sums[side] = term if sums[side] is None else sums[side] + term
        pushed.append([face_push(sums[side], place.face(w_ref, j, side), lam) for side in range(2)])
    load = pushed[0][0]
    values = []
    for j in range(slabs):
        reduced = block_of(spec_ref, j * (inner + 1) + inner, size) - pushed[j][1]
        if j + 1 < slabs:
            reduced = reduced - pushed[j + 1][0]
        panel = w_ref[place.at("panel", j)]
        solved_ref[j] = reduced
        if j > 0:
            reduced = reduced - face_lift(values[-1], place.band(w_ref, j), lam)
        values.append(apply(reduced, panel, modes))
        y_ref[j] = values[j]
    return load, values


def previous_weight(panel_ref, modes):
    parts = [split(panel_ref[k]) for k in range(modes)]
    return jnp.concatenate(
        [jnp.concatenate([p[i] for p in parts], axis=1) for i in range(2)], axis=0
    )


def apply_nt(x, weight, modes):
    return folded(dot(by_mode(x, modes), weight, NT), x.shape[0])


def backward_values(values, after, panel, behind_ref, modes):
    slabs = len(values)
    out = [None] * slabs
    out[-1] = values[-1]
    if after is not None:
        out[-1] = out[-1] - apply(after, panel, modes)
    for j in range(slabs - 2, -1, -1):
        out[j] = values[j] - apply(out[j + 1], behind_ref[j], modes)
    return out


def push_kernel(modes, first_ref, load_ref, prev_ref, push_ref, prev_buf, sems):
    @pl.when(lax.axis_index("elem") == 1)
    def _():
        for copy in start_copies([(first_ref, prev_buf)], sems):
            copy.wait()
        weight = previous_weight(prev_buf, modes)
        prev_ref[...] = weight
        push_ref[...] = apply_nt(load_ref[1], weight, modes)


def forward_kernel(modes, at, got_ref, push_ref, y_ref, front_ref, old_ref, state_ref, send_ref):
    @pl.when(lax.axis_index("elem") == at)
    def _():
        before = got_ref[...] - push_ref[...]
        state_ref[0] = before
        send_ref[...] = y_ref[y_ref.shape[0] - 1] + apply(before, front_ref[...], modes)


def base_kernel(
    modes, mode_total, hub, place, band_ref, map_ref, state_ref, load_ref, reduced_ref, y_ref, w_ref,
    base_ref, found_ref, back_ref, band_buf, sems,
):
    elem = lax.axis_index("elem")
    slabs, rows, size = reduced_ref.shape
    lam = wave(mode_total, (rows, size), modes)

    @pl.when((elem > 0) & (elem < hub))
    def _():
        copies = start_copies([(band_ref.at[:, 0], band_buf), (map_ref, back_ref)], sems)
        copies[0].wait()
        first = band_wide(band_buf[0], band_buf[1])
        bands = [first] + [place.band(w_ref, j) for j in range(1, slabs)]
        panels = [w_ref[place.at("panel", j)] for j in range(slabs)]
        values = []
        for j in range(slabs):
            step = face_lift(values[-1], bands[j], lam) if j > 0 else face_push(state_ref[0], first, lam)
            values.append(apply(reduced_ref[j] - step, panels[j], modes))
        found = values[-1]
        found_ref[slabs - 1] = found
        for j in range(slabs - 2, -1, -1):
            found = values[j] - apply(face_push(found, bands[j + 1], lam), panels[j], modes)
            found_ref[j] = found
        base_ref[...] = load_ref[1] + face_lift(found, first, lam)
        copies[1].wait()


def ahead_maps(ahead_ref, band_buf, waves, w_ref, place):
    slabs, many, _ = ahead_ref.shape
    for j in range(slabs):
        first, second = band_buf[0, j].T, band_buf[1, j].T
        for k, lam in enumerate(waves):
            ahead_ref[j, pl.ds(k * place.size, place.size)] = wide(product(first + lam * second, w_ref[place.at("panel", j, k)]))


def behind_maps(behind_ref, band_buf, waves, w_ref, place):
    for j in range(behind_ref.shape[0]):
        for k, lam in enumerate(waves):
            step = product(band_buf[0, j + 1] + lam * band_buf[1, j + 1], w_ref[place.at("panel", j, k)])
            behind_ref[j, pl.ds(k * place.size, place.size)] = wide(step)


def hub_map_kernel(
    modes, mode_total, hub, place, map_ref, pprev_ref, band_ref, given_ref, load_ref, y_ref, w_ref, front_ref, old_prev_ref, old_push_ref,
    prev_ref, push_ref, ahead_ref, behind_ref, back_ref, base_ref, cross_ref, through_ref, band_buf, map_buf, prev_buf, sems,
):
    slabs, rows, size = y_ref.shape
    lam = wave(mode_total, (rows, size), modes)
    inside = (lax.axis_index("elem") > 1) & (lax.axis_index("elem") <= hub)

    @pl.when(inside)
    def _():
        start_copies([(pprev_ref, prev_buf)], sems.at[pl.ds(2, 1)])

    @pl.when(lax.axis_index("elem") == hub)
    def _():
        copies = start_copies([(band_ref, band_buf), (map_ref, map_buf)], sems)
        given = start_copies([(given_ref, back_ref)], sems.at[pl.ds(3, 1)])[0]
        waves = [wave_of(k, mode_total, modes) for k in range(modes)]

        def part(k):
            return pl.ds(k * size, size)

        copies[0].wait()
        ahead_maps(ahead_ref, band_buf, waves, w_ref, place)
        behind_maps(behind_ref, band_buf, waves, w_ref, place)
        entry = [wide(band_buf[0, 0] + waves[k] * band_buf[1, 0]) for k in range(modes)]
        forward = [[-whole(ahead_ref[0, part(k)]) for k in range(modes)]]
        for j in range(1, slabs - 1):
            forward.append([-product(forward[-1][k], ahead_ref[j, part(k)]) for k in range(modes)])
        cross = [whole(front_ref[part(k)]) for k in range(modes)]
        for j in range(slabs - 2, -1, -1):
            cross = [forward[j][k] - product(cross[k], behind_ref[j, part(k)]) for k in range(modes)]
        for k in range(modes):
            cross_ref[part(k)] = wide(product(cross[k], entry[k]))
        found = backward_values([y_ref[j] for j in range(slabs)], None, None, behind_ref, modes)
        base_ref[...] = load_ref[1] + face_lift(found[0], band_wide(band_buf[0, 0], band_buf[1, 0]), lam)
        copies[1].wait()
        given.wait()
        for k in range(modes):
            through_ref[part(k)] = wide(product(map_buf[k].T, back_ref[part(k)]))

    @pl.when(inside)
    def _():
        pltpu.make_async_copy(pprev_ref, prev_buf, sems.at[2]).wait()
        weight = previous_weight(prev_buf, modes)
        prev_ref[...] = weight
        push_ref[...] = apply_nt(load_ref[1], weight, modes)


def hub_kernel(
    modes, at, place, got_ref, push_ref, far_ref, through_ref, y_ref, front_ref, back_ref, cross_ref, base_ref, w_ref,
    send_ref, values_ref,
):
    slabs = y_ref.shape[0]

    @pl.when(lax.axis_index("elem") == at)
    def _():
        before = got_ref[...] - push_ref[...]
        load = apply(far_ref[1], w_ref[place.at("panel", slabs - 1)], modes)
        value = y_ref[slabs - 1] + apply(before, front_ref[...], modes)
        out = base_ref[...] + apply(before, cross_ref[...], modes) + apply(far_ref[0], back_ref[...], modes)
        final = value - load
        send_ref[...] = out + apply(final, through_ref[...], modes)
        values_ref[0] = before
        values_ref[1] = value
        values_ref[2] = final


def hub_values_kernel(modes, at, place, map_ref, far_ref, values_ref, w_ref, old_ref, state_ref, last_ref):
    @pl.when(lax.axis_index("elem") == at)
    def _():
        final = values_ref[2]
        after = far_ref[0] + apply_nt(final, previous_weight(map_ref, modes), modes)
        state_ref[0] = values_ref[0]
        state_ref[1] = after
        last_ref[0] = final
        last_ref[1] = values_ref[1] - apply(after, w_ref[place.at("panel", place.counts["panel"] - 1)], modes)


def own_map_kernel(
    modes, mode_total, hub, place, band_ref, radial_ref, state_ref, reduced_ref, y_ref, w_ref, front_ref, prev_ref, ahead_ref, behind_ref, old_ref,
    found_ref, own_ref, before_ref, radt_ref, ahead_buf, behind_buf, band_buf, radial_buf, sems,
):
    slabs, rows, size = reduced_ref.shape
    elem, last = lax.axis_index("elem"), lax.axis_size("elem") - 1
    lam = wave(mode_total, (rows, size), modes)
    waves = [wave_of(k, mode_total, modes) for k in range(modes)]
    copies = start_copies([(band_ref, band_buf), (radial_ref, radial_buf)], sems)

    def part(k):
        return pl.ds(k * size, size)

    copies[0].wait()

    @pl.when(elem == hub)
    def _():
        panels = [w_ref[place.at("panel", j)] for j in range(slabs)]
        before, values = state_ref[0], []
        for j in range(slabs):
            if j == slabs - 1:
                values.append(y_ref[j] + apply(before, front_ref[...], modes))
                continue
            solved = apply(reduced_ref[j], panels[j], modes)
            values.append(solved - apply(values[-1] if j > 0 else before, ahead_ref[j], modes))
        found = backward_values(values, state_ref[1], panels[-1], behind_ref, modes)
        for j in range(slabs):
            found_ref[j] = found[j]
        back = face_lift(found[0], band_wide(band_buf[0, 0], band_buf[1, 0]), lam)
        before_ref[...] = before - apply_nt(back, prev_ref[...], modes)

    @pl.when(elem != hub)
    def _():
        behind_maps(behind_buf, band_buf, waves, w_ref, place)

    @pl.when(elem < hub)
    def _():
        current = [-whole(w_ref[place.at("panel", slabs - 1, k)]) for k in range(modes)]
        for k in range(modes):
            own_ref[slabs - 1, part(k)] = -w_ref[place.at("panel", slabs - 1, k)]
        for j in range(slabs - 2, -1, -1):
            current = [-product(current[k], behind_buf[j, part(k)]) for k in range(modes)]
            for k in range(modes):
                own_ref[j, part(k)] = wide(current[k])

    @pl.when(elem == last)
    def _():
        ahead_maps(ahead_buf, band_buf, waves, w_ref, place)
        forward = [[-whole(ahead_buf[0, part(k)]) for k in range(modes)]]
        for j in range(1, slabs):
            forward.append([-product(forward[-1][k], ahead_buf[j, part(k)]) for k in range(modes)])
        current = forward[-1]
        for k in range(modes):
            own_ref[slabs - 1, part(k)] = wide(current[k])
        for j in range(slabs - 2, -1, -1):
            current = [forward[j][k] - product(current[k], behind_buf[j, part(k)]) for k in range(modes)]
            for k in range(modes):
                own_ref[j, part(k)] = wide(current[k])

    @pl.when((elem == 0) | (elem == last))
    def _():
        found = backward_values([y_ref[j] for j in range(slabs)], None, None, behind_buf, modes)
        for j in range(slabs):
            found_ref[j] = found[j]

    copies[1].wait()
    for j in range(slabs):
        radt_ref[j] = wide(radial_buf[j].T)


def backward_kernel(modes, at, got_ref, base_ref, back_ref, old_ref, state_ref, send_ref):
    @pl.when(lax.axis_index("elem") == at)
    def _():
        after = got_ref[...]
        state_ref[1] = after
        send_ref[...] = base_ref[...] + apply(after, back_ref[...], modes)


def final_kernel(
    modes, mode_total, hub, place, zsrc_ref, inv_ref, state_ref, got_ref, base_ref, last_ref, load_ref, found_ref, own_ref, back_ref, before_ref, prev_ref, w_ref, radt_ref, axial_ref, weight_ref,
    out_ref, x_ref, out_buf, sems,
):
    slabs, inner, rows, size = zsrc_ref.shape
    lam = wave(mode_total, (rows, size), modes)
    elem, last = lax.axis_index("elem"), lax.axis_size("elem") - 1

    def values(given):
        for j in range(slabs):
            x_ref[j + 1] = found_ref[j] + apply(given, own_ref[j], modes)

    @pl.when(elem == 0)
    def _():
        x_ref[0] = jnp.zeros((rows, size), F32)
        values(got_ref[...])

    @pl.when((elem > 0) & (elem < hub))
    def _():
        after = state_ref[1]
        values(after)
        back = base_ref[...] - load_ref[1] + apply(after, back_ref[...], modes)
        x_ref[0] = state_ref[0] - apply_nt(back, prev_ref[...], modes)

    @pl.when(elem == hub)
    def _():
        for j in range(slabs):
            x_ref[j + 1] = found_ref[j]
        x_ref[0] = before_ref[...]

    @pl.when(elem == last)
    def _():
        values(last_ref[0])
        x_ref[0] = last_ref[1]

    copies = []
    for j in range(slabs):
        lifted = [face_lift(x_ref[j + side], place.face(w_ref, j, side), lam) for side in range(2)]
        kept = []
        for b in range(inner):
            total = lifted[0] * weight_ref[j, 0, b] + lifted[1] * weight_ref[j, 1, b]
            kept.append(zsrc_ref[j, b] - total * inv_ref[j, b])
        values = []
        for a in range(inner):
            value = kept[0] * axial_ref[j, a, 0]
            for b in range(1, inner):
                value = value + kept[b] * axial_ref[j, a, b]
            values.append(value)
        result = product(jnp.concatenate(values, axis=0), radt_ref[j])
        for a in range(inner):
            out_buf[j, :, a * size : (a + 1) * size] = result[a * rows : (a + 1) * rows]
        out_buf[j, :, inner * size :] = x_ref[j + 1]
        width = (inner + 1) * size
        copies += start_copies([(out_buf.at[j], out_ref.at[:, pl.ds(j * width, width)])], sems.at[pl.ds(j, 1)])
    for copy in copies:
        copy.wait()


def dft_table(planes):
    row, col = np.arange(planes)[:, None], np.arange(planes)[None]
    angle = row // 2 * col % planes * (2.0 * math.pi / planes)
    table = np.where(row % 2 == 0, np.cos(angle), -np.sin(angle)) / math.sqrt(planes)
    table = jnp.asarray(table, F32)
    high, low = split(table)
    return jnp.concatenate([high, low, high], axis=1)


def body(
    rhs_phys, radial_basis, axial_basis, radial_eig, axial_eig, face_stiff, face_mass, axial_coupling, face_numbering,
    band_panels, inverse_panels,
):
    planes, nodes = rhs_phys.shape
    modes, slabs, size, _ = inverse_panels.shape
    inner = axial_basis.shape[1]
    devices = lax.axis_size("mode")
    elems = lax.axis_size("elem")
    mode_total = modes * devices
    rows = 2 * modes
    hub = elems - 2
    last = elems - 1

    def shape(*dims):
        return jax.ShapeDtypeStruct(dims, F32)

    def kept(*dims):
        return pltpu.VMEM(dims, F32)

    def half(*dims):
        return pltpu.VMEM(dims, BF16)

    table = dft_table(planes)
    many = modes * size
    place = Weights(size, ("panel", slabs, many), ("radial", slabs, size), ("face", 4 * slabs, size), ("band", 2 * (slabs - 1), size))
    buffers = [pltpu.VMEM((planes, nodes), F32), pltpu.VMEM(table.shape, BF16), pltpu.SemaphoreType.DMA((slabs + 3,))]
    whole_spectrum = pltpu.HBM((planes, nodes), F32)
    whole_panels = pltpu.HBM((modes, size, size), F32)
    panels_buffer = pltpu.VMEM((modes, size, size), F32)
    ship, spectrum = call(
        functools.partial(ends_kernel, modes, mode_total),
        [whole_panels, whole_spectrum],
        [inverse_panels, band_panels, rhs_phys, table],
        anywhere=4,
        scratch=[pltpu.VMEM((slabs, modes, size, size), F32), pltpu.VMEM(band_panels.shape, F32), panels_buffer] + buffers,
    )
    if hub > 1:
        first = far_map = lax.ppermute(ship, "elem", [(0, 1), (last, hub)])
    else:
        first, far_map = lax.ppermute(ship, "elem", [(0, 1)]), lax.ppermute(ship, "elem", [(last, hub)])
    ship, spectrum = call(
        functools.partial(between_kernel, hub),
        [whole_panels, whole_spectrum],
        [inverse_panels, rhs_phys, table, spectrum],
        anywhere=4,
        scratch=[panels_buffer] + buffers,
        aliases={3: 1},
    )
    pprev = lax.ppermute(ship, "elem", [(i, i + 1) for i in range(1, hub)]) if hub > 1 else first
    spectrum = call(
        functools.partial(late_kernel, hub),
        [whole_spectrum],
        [rhs_phys, table, spectrum],
        anywhere=3,
        scratch=buffers,
        aliases={2: 0},
    )[0]
    spectrum = lax.all_to_all(spectrum.reshape(devices, rows, nodes), "mode", 0, 0, tiled=False)
    if nodes % size:
        spectrum = jnp.swapaxes(spectrum, 0, 1).reshape(1, rows, devices * nodes)
    vector = (rows, size)
    matrix = half(many, 2 * size)
    front, back_map, later, w, reig, axial, weight, aeig = call(
        functools.partial(maps_kernel, modes, mode_total, hub, place),
        [
            pltpu.HBM((many, 2 * size), BF16),
            pltpu.HBM((many, 2 * size), BF16),
            pltpu.HBM((slabs - 1, many, 2 * size), BF16),
            half(place.total, 2 * size),
            kept(*radial_eig.shape),
            pltpu.SMEM(axial_basis.shape, F32),
            pltpu.SMEM((slabs, 2, inner), F32),
            pltpu.SMEM(axial_eig.shape, F32),
        ],
        [
            inverse_panels, band_panels, radial_basis, face_stiff, face_mass, face_numbering,
            radial_eig, axial_basis, axial_eig, axial_coupling,
        ],
        anywhere=10,
        outside=3,
        scratch=[
            pltpu.VMEM((slabs, modes, size, size), F32),
            pltpu.VMEM(band_panels.shape, F32),
            pltpu.VMEM(radial_basis.shape, F32),
            pltpu.VMEM(face_stiff.shape, F32),
            pltpu.VMEM(face_mass.shape, F32),
            pltpu.VMEM(face_numbering.shape, jnp.int32),
            pltpu.SMEM(axial_basis.shape, F32),
            pltpu.SMEM(axial_coupling.shape, F32),
            pltpu.VMEM((many, 2 * size), BF16),
            pltpu.VMEM((many, 2 * size), BF16),
            pltpu.VMEM((slabs - 1, many, 2 * size), BF16),
            pltpu.SemaphoreType.DMA((slabs + 9,)),
        ],
    )
    solves = [kept(slabs, inner, *vector), kept(slabs, inner, *vector), kept(slabs, *vector), kept(slabs, *vector)]
    *solve, send = call(
        functools.partial(inner_kernel, modes, mode_total, place, hub, True),
        solves + [kept(*vector)],
        [band_panels, front, later, spectrum, w, reig, axial, weight, aeig],
        anywhere=3,
        smem=3,
    )
    got = lax.ppermute(send, "elem", [(0, 1)])
    zsrc, inv, reduced, y, load, front = call(
        functools.partial(inner_kernel, modes, mode_total, place, hub, False),
        solves + [kept(2, *vector), matrix],
        [band_panels, front, later, spectrum, w, reig, *solve, axial, weight, aeig],
        anywhere=3,
        smem=3,
        scratch=[
            pltpu.VMEM((2, size, size), F32),
            pltpu.VMEM((slabs - 1, many, 2 * size), BF16),
            pltpu.SemaphoreType.DMA((2,)),
        ],
        aliases={6 + i: i for i in range(4)},
    )
    far = lax.ppermute(load, "elem", [(last, hub)])
    prev, push = call(
        functools.partial(push_kernel, modes),
        [half(2 * size, many), kept(*vector)],
        [first, load],
        free=1,
        scratch=[panels_buffer, pltpu.SemaphoreType.DMA((1,))],
    )
    prev, later_push, ahead, behind, hub_back, hub_base, cross, through = call(
        functools.partial(hub_map_kernel, modes, mode_total, hub, place),
        [
            half(2 * size, many), kept(*vector), half(slabs - 1, many, 2 * size), half(slabs - 1, many, 2 * size), matrix,
            kept(*vector), matrix, matrix,
        ],
        [far_map, pprev, band_panels, back_map, load, y, w, front, prev, push],
        free=2,
        anywhere=2,
        scratch=[pltpu.VMEM(band_panels.shape, F32), panels_buffer, panels_buffer, pltpu.SemaphoreType.DMA((4,))],
        aliases={8: 0, 9: 1},
    )
    state = jnp.zeros((2, *vector), F32)
    for at in range(1, hub):
        state, send = call(
            functools.partial(forward_kernel, modes, at),
            [kept(*state.shape), shape(*vector)],
            [got, push if at == 1 else later_push, y, front, state],
            aliases={4: 0},
        )
        got = lax.ppermute(send, "elem", [(at, at + 1)])
    send, values = call(
        functools.partial(hub_kernel, modes, hub, place),
        [shape(*vector), kept(3, *vector)],
        [got, push if hub == 1 else later_push, far, through, y, front, hub_back, cross, hub_base, w],
    )
    state, final = call(
        functools.partial(hub_values_kernel, modes, hub, place),
        [kept(*state.shape), shape(2, *vector)],
        [far_map, far, values, w, state],
        aliases={4: 0},
    )
    base, found, back = call(
        functools.partial(base_kernel, modes, mode_total, hub, place),
        [kept(*vector), kept(slabs, *vector), matrix],
        [band_panels, back_map, state, load, reduced, y, w],
        anywhere=2,
        scratch=[pltpu.VMEM((2, size, size), F32), pltpu.SemaphoreType.DMA((2,))],
    )
    for at in range(hub - 1, 0, -1):
        got = lax.ppermute(send, "elem", [(at + 1, at)])
        state, send = call(
            functools.partial(backward_kernel, modes, at),
            [kept(*state.shape), shape(*vector)],
            [got, base, back, state],
            aliases={3: 0},
        )
    got = lax.ppermute(send, "elem", [(1, 0)])
    found, own, before, radt = call(
        functools.partial(own_map_kernel, modes, mode_total, hub, place),
        [kept(slabs, *vector), half(slabs, many, 2 * size), kept(*vector), half(slabs, size, 2 * size)],
        [band_panels, radial_basis, state, reduced, y, w, front, prev, ahead, behind, found],
        anywhere=2,
        scratch=[
            pltpu.VMEM((slabs, many, 2 * size), BF16),
            pltpu.VMEM((slabs - 1, many, 2 * size), BF16),
            pltpu.VMEM(band_panels.shape, F32),
            pltpu.VMEM(radial_basis.shape, F32),
            pltpu.SemaphoreType.DMA((2,)),
        ],
        aliases={10: 0},
    )
    final = lax.ppermute(final, "elem", [(hub, last)])
    return call(
        functools.partial(final_kernel, modes, mode_total, hub, place),
        [pltpu.HBM((rows, slabs * (inner + 1) * size), F32)],
        [
            zsrc, inv, state, got, base, final, load, found, own, back, before, prev, w, radt, axial, weight,
        ],
        smem=2,
        scratch=[
            pltpu.VMEM((slabs + 1, *vector), F32),
            pltpu.VMEM((slabs, rows, (inner + 1) * size), F32),
            pltpu.SemaphoreType.DMA((slabs,)),
        ],
    )[0]


def solution(mesh):
    placed = (
        P(None, ("elem", "mode")),
        P("elem", None, None),
        P("elem", None, None),
        P("elem", None),
        P("elem", None),
        P("elem", None, None),
        P("elem", None, None),
        P("elem", None, None),
        P("elem", None, None),
        P(None, "elem", None, None),
        P("mode", "elem", None, None),
    )
    return jax.shard_map(
        body, mesh=mesh, in_specs=placed, out_specs=P("mode", "elem"), check_vma=False
    )
```
